512 devices in a mesh: dp: 64 (over z, y_hi, core), ctx: 8 (over x, y_lo).
Axes of the slice: x: 4, y: 4 (y_hi: 2, y_lo: 2; y = y_hi * 2 + y_lo), z: 16, core: 2. Of those that a mesh axis runs over, the one named last changes fastest.
Arguments:
- query_loader: bfloat16 [64, 2048, 1024], P('dp', 'ctx'), may hold values from -10 to 10, as said below
- key_loader: bfloat16 [64, 2048, 1024], P('dp', 'ctx'), may hold values from -10 to 10
- value_loader: bfloat16 [64, 2048, 1024], P('dp', 'ctx'), may hold values from -6 to 6
- conv_loader: bfloat16 [64, 2048, 1536], P('dp', 'ctx'), may hold values from -6 to 6
- slot_tile: int32 [8, 128], P('ctx'), may hold values from 0 to 127, each once within a row
- lengths: int32 [64, 4], P('dp'), may hold values from 1 to 32, 64 in all within a row
- conv_taps: float32 [31, 1536], replicated, may hold values from -1 to 1
- norm_scale: float32 [1536], replicated, may hold values from 0.5 to 2
- norm_shift: float32 [1536], replicated, may hold values from -2 to 2
Outputs:
- attention_out: bfloat16 [64, 2048, 1024], P('dp', 'ctx')
- conv_out: bfloat16 [64, 2048, 1536], P('dp', 'ctx')
The draws below stay inside these ranges and needn't reach their ends.
Inputs may be any that keep to these rules, and one draw needn't show every extreme that they name: `query_loader`: in some draws, queries and keys share a direction per head.
All inputs are finite; a program needn't handle non-finite values.
Results may differ from the reference program's by a relative error of at most 0.006.
Values may be sent and summed in bfloat16 or wider, within the bound.
A program may use at most 128 MiB of HBM per device.

```python
import math
import jax
import jax.numpy as jnp
import numpy as np
from jax import lax

HEADS = 16
HEAD_DIM = 64
CHANNELS = 1536
KERNEL = 31
TILE = 128
TILES_DEV = 2
SEG_UNIT = 32
GROUP_FRAMES = 2048
RECS = 4
MOST = 32
N_DP = 64
N_CTX = 8


def drawn_draw(key):
    frame_count = N_CTX * TILES_DEV * TILE
    noise_draw = jnp.clip(jax.random.normal(key, (N_DP, frame_count, HEADS, HEAD_DIM), jnp.float32), -4.0, 4.0)
    combined = noise_draw
    return combined.reshape(N_DP, frame_count, HEADS * HEAD_DIM).astype(jnp.bfloat16)


def draw_query_loader(key, part):
    key = jax.random.fold_in(key, 11)
    noise_key = jax.random.fold_in(key, 0)
    return drawn_draw(noise_key)


def draw_key_loader(key, part):
    key = jax.random.fold_in(key, 12)
    noise_key = jax.random.fold_in(key, 0)
    return drawn_draw(noise_key)


def levels(key, dims, cuts, least, largest):
    def one(position, blocks):
        steps = jax.random.uniform(jax.random.fold_in(jax.random.fold_in(key, 6), position), (blocks,), jnp.float32, least / len(cuts), largest / len(cuts))
        return jnp.repeat(jnp.exp(steps), dims[position] // blocks).reshape((-1,) + (1,) * (len(dims) - position - 1))

    level = one(*cuts[0])
    for cut in cuts[1:]:
        level = level * one(*cut)
    return level


def profile(count, total, reach, slope):
    portions = [(1 << 20) // math.isqrt(standing ** slope) + 1 for standing in range(2, count + 1)]
    spare, given = total - reach - (count - 1), [1] * (count - 1)
    while spare > 0:
        free = [i for i in range(count - 1) if given[i] < reach]
        whole, left = sum([portions[i] for i in free]), spare
        for i in free:
            more = min(reach - given[i], max(1, left * portions[i] // whole), spare)
            given[i] = given[i] + more
            spare = spare - more
    return np.array([reach] + given)


def uneven_parts(key, amount, total, reach, lean):
    if amount == 2:
        one = jax.random.randint(key, (), max(1, total - reach), min(reach, total - 1) + 1)
        return jnp.stack([one, total - one])
    sizes = jnp.asarray(profile(amount, total, reach, lean), jnp.int32)
    pairs = (amount - 1) // 2
    source_of, taker = sizes[1:1 + 2 * pairs:2], sizes[2:2 + 2 * pairs:2]
    margin = jnp.minimum(source_of - 1, reach - taker)
    moved = jax.random.randint(jax.random.fold_in(key, 1), (pairs,), 0, 1 << 20) % (margin + 1)
    sizes = sizes.at[1:1 + 2 * pairs:2].set(source_of - moved).at[2:2 + 2 * pairs:2].set(taker + moved)
    return sizes[jax.random.permutation(jax.random.fold_in(key, 2), amount)]


def bell_draw(key, extent, deviation, most, shards=(), kind=jnp.bfloat16):
    result = deviation * jax.random.normal(key, extent, jnp.float32)
    if shards:
        result = result * levels(key, extent, shards, -0.22, 0.18)
    return jnp.clip(result, -most, most).astype(kind)


def setup_inputs(seed: int = 0) -> dict:
    arg_keys = jax.random.split(jax.random.key(seed), 10)
    query_loader = draw_query_loader(jax.random.fold_in(arg_keys[9], 71), 0)
    key_loader = draw_key_loader(jax.random.fold_in(arg_keys[9], 71), 0)
    value_loader = bell_draw(arg_keys[2], (N_DP, GROUP_FRAMES, HEADS * HEAD_DIM), 1.0, 6.0, ((0, 64), (1, 8)))
    conv_loader = bell_draw(arg_keys[3], (N_DP, GROUP_FRAMES, CHANNELS), 1.0, 6.0, ((0, 64), (1, 8)))
    slot_tile = jax.vmap(lambda own: jax.random.permutation(own, N_DP * TILES_DEV))(jax.random.split(arg_keys[4], N_CTX)).reshape((N_CTX, N_DP * TILES_DEV)).astype(jnp.int32)
    lengths = jax.vmap(lambda own: uneven_parts(own, RECS, 4 * N_CTX * TILES_DEV, MOST, 1))(jax.random.split(arg_keys[5], N_DP)).reshape((N_DP, RECS)).astype(jnp.int32)
    conv_taps = bell_draw(arg_keys[6], (KERNEL, CHANNELS), KERNEL ** -0.5, 1.0, (), jnp.float32)
    norm_scale = jnp.clip(jnp.exp(jax.random.uniform(arg_keys[7], (CHANNELS,), jnp.float32, math.log(0.5), math.log(2.0))), 0.5, 2.0)
    norm_shift = bell_draw(arg_keys[8], (CHANNELS,), 0.5, 2.0, (), jnp.float32)
    return {"query_loader": query_loader, "key_loader": key_loader, "value_loader": value_loader, "conv_loader": conv_loader, "slot_tile": slot_tile, "lengths": lengths, "conv_taps": conv_taps, "norm_scale": norm_scale, "norm_shift": norm_shift}


def segment_of(positions, seg_ends):
    unit_index = positions // SEG_UNIT
    return jnp.sum((seg_ends[None, :] <= unit_index[:, None]).astype(jnp.int32), axis=1)


def repack(loader, slot_tile):
    feature_width = loader.shape[2]
    tiles = loader.reshape(N_DP, N_CTX, TILES_DEV, TILE, feature_width)
    tiles = jnp.transpose(tiles, (1, 0, 2, 3, 4)).reshape(N_CTX, N_DP * TILES_DEV, TILE, feature_width)
    picked = jax.vmap(lambda column_tiles, tile_order: column_tiles[tile_order])(tiles, slot_tile)
    picked = picked.reshape(N_CTX, N_DP, TILES_DEV, TILE, feature_width)
    picked = jnp.transpose(picked, (1, 0, 2, 3, 4))
    return picked.reshape(N_DP, N_CTX * TILES_DEV * TILE, feature_width)


def attend_group(queries, keys_all, values_all, segments):
    heads_q = queries.reshape(-1, HEADS, HEAD_DIM).astype(jnp.float32)
    heads_k = keys_all.reshape(-1, HEADS, HEAD_DIM).astype(jnp.float32)
    heads_v = values_all.reshape(-1, HEADS, HEAD_DIM).astype(jnp.float32)
    scores = jnp.einsum("qhd,khd->hqk", heads_q, heads_k) * 0.125
    allowed = (segments[:, None] == segments[None, :])[None]
    masked = jnp.where(allowed, scores, -1e30)
    row_max = jnp.max(masked, axis=2, keepdims=True)
    weights = jnp.where(allowed, jnp.exp(masked - row_max), 0.0)
    norm_total = jnp.sum(weights, axis=2)
    rounded = lax.optimization_barrier(weights.astype(jnp.bfloat16)).astype(jnp.float32)
    mixture = jnp.einsum("hqk,khd->qhd", rounded, heads_v) / jnp.transpose(norm_total)[:, :, None]
    return mixture.reshape(-1, HEADS * HEAD_DIM).astype(jnp.bfloat16)


def convolve_group(signal, segments, conv_taps, norm_scale, norm_shift):
    length = signal.shape[0]
    half_width = (KERNEL - 1) // 2
    padded = jnp.pad(signal.astype(jnp.float32), ((half_width, half_width), (0, 0)))
    padded_seg = jnp.pad(segments, (half_width, half_width), constant_values=-1)
    conv_sum = jnp.zeros(signal.shape, jnp.float32)
    for offset_tap in range(KERNEL):
        same_seg = (padded_seg[offset_tap:offset_tap + length] == segments)[:, None]
        conv_sum = conv_sum + jnp.where(same_seg, conv_taps[offset_tap] * padded[offset_tap:offset_tap + length], 0.0)
    return jax.nn.silu(norm_scale * conv_sum + norm_shift).astype(jnp.bfloat16)


def reference(query_loader, key_loader, value_loader, conv_loader, slot_tile, lengths, conv_taps, norm_scale, norm_shift):
    queries = repack(query_loader, slot_tile)
    keys_all = repack(key_loader, slot_tile)
    values_all = repack(value_loader, slot_tile)
    conv_input = repack(conv_loader, slot_tile)
    seg_ends = jnp.cumsum(lengths, axis=1).astype(jnp.int32)
    positions = jnp.arange(N_CTX * TILES_DEV * TILE, dtype=jnp.int32)
    segments = jax.vmap(lambda ends_row: segment_of(positions, ends_row))(seg_ends)
    attention_out = lax.map(lambda members: attend_group(members[0], members[1], members[2], members[3]), (queries, keys_all, values_all, segments))
    conv_out = lax.map(lambda members: convolve_group(members[0], members[1], conv_taps, norm_scale, norm_shift), (conv_input, segments))
    return attention_out, conv_out
```

```python
import functools

import jax
import jax.numpy as jnp
from jax import lax
from jax.experimental import pallas as pl
from jax.experimental.pallas import tpu as pltpu
from jax.sharding import PartitionSpec as P

MESH = pl.DeviceIdType.MESH
HEADS = 16
HEAD_DIM = 64
KERNEL = 31
TILE = 128
TILES_DEV = 2
SEG_UNIT = 32
ROWS = 16
LANES = 128
N_DP = 64
N_CTX = 8
QKV = 3 * ROWS
CONV_ROWS = 24
QBLOCK = 256
KBLOCK = 256
FRAMES = 2048
UNITS = QBLOCK // SEG_UNIT


def share_of(dp, ctx):
    return (dp // 8) * 8 + lax.rem(dp + ctx, 8)


def entry(count, device):
    barrier = pltpu.get_barrier_semaphore()

    def one(k, carry):
        pl.semaphore_signal(barrier, inc=1, device_id=device(k), device_id_type=MESH)
        return carry

    lax.fori_loop(0, count, one, 0)
    pl.semaphore_wait(barrier, count)


def all_arrived(ref, sem):
    pltpu.make_async_copy(ref, ref, sem).wait()


def spread_kernel(x_ref, out_ref, send_sem, recv_sem):
    dp, ctx = lax.axis_index("dp"), lax.axis_index("ctx")
    entry(N_DP - 1, lambda k: (lax.rem(dp + 1 + k, N_DP), ctx))

    def copy(k):
        peer = lax.rem(dp + k, N_DP)
        return pltpu.make_async_remote_copy(
            src_ref=x_ref.at[share_of(peer, ctx)],
            dst_ref=out_ref.at[dp],
            send_sem=send_sem,
            recv_sem=recv_sem,
            device_id=(peer, ctx),
            device_id_type=MESH,
        )

    own = pltpu.make_async_copy(x_ref.at[share_of(dp, ctx)], out_ref.at[dp], recv_sem)

    def start(k, carry):
        copy(k).start()
        return carry

    def sent(k, carry):
        copy(k).wait_send()
        return carry

    lax.fori_loop(1, N_DP, start, 0)
    own.start()
    lax.fori_loop(1, N_DP, sent, 0)
    all_arrived(out_ref, recv_sem)


def spread(x):
    return pl.pallas_call(
        spread_kernel,
        out_shape=jax.ShapeDtypeStruct(x.shape, x.dtype),
        in_specs=[pl.BlockSpec(memory_space=pl.ANY)],
        out_specs=pl.BlockSpec(memory_space=pl.ANY),
        scratch_shapes=[pltpu.SemaphoreType.DMA, pltpu.SemaphoreType.DMA],
        compiler_params=pltpu.CompilerParams(collective_id=0, has_side_effects=True),
        name="spread",
    )(x)


def heads_kernel(x_ref, out_ref, send_sem, recv_sem):
    dp, ctx = lax.axis_index("dp"), lax.axis_index("ctx")
    share = share_of(dp, ctx)
    group, column = share // 8, lax.rem(share, 8)

    def sender(k):
        other = k // 8
        return (lax.rem(k, 8) * 8 + lax.rem(ctx - other + 8, 8), other)

    barrier = pltpu.get_barrier_semaphore()

    def greet(k, carry):
        peer = sender(k)

        @pl.when(jnp.logical_or(peer[0] != dp, peer[1] != ctx))
        def _():
            pl.semaphore_signal(barrier, inc=1, device_id=peer, device_id_type=MESH)

        return carry

    lax.fori_loop(0, N_DP, greet, 0)
    is_own = column == ctx

    @pl.when(is_own)
    def _():
        pl.semaphore_wait(barrier, N_DP - 1)

    @pl.when(jnp.logical_not(is_own))
    def _():
        pl.semaphore_wait(barrier, N_DP)

    def copy(k):
        peer = lax.rem(dp + k, N_DP)
        return pltpu.make_async_remote_copy(
            src_ref=x_ref.at[peer],
            dst_ref=out_ref.at[pl.ds(ctx * TILES_DEV, TILES_DEV), group],
            send_sem=send_sem,
            recv_sem=recv_sem,
            device_id=(peer, column),
            device_id_type=MESH,
        )

    def start(k, carry):
        copy(k).start()
        return carry

    def sent(k, carry):
        copy(k).wait_send()
        return carry

    lax.fori_loop(1, N_DP, start, 0)

    @pl.when(is_own)
    def _():
        pltpu.make_async_copy(
            x_ref.at[dp], out_ref.at[pl.ds(ctx * TILES_DEV, TILES_DEV), group], recv_sem
        ).start()

    @pl.when(jnp.logical_not(is_own))
    def _():
        copy(0).start()
        copy(0).wait_send()

    lax.fori_loop(1, N_DP, sent, 0)
    all_arrived(out_ref, recv_sem)


def to_heads(x):
    return pl.pallas_call(
        heads_kernel,
        out_shape=jax.ShapeDtypeStruct((N_CTX * TILES_DEV, TILE // ROWS, 3, ROWS, LANES), x.dtype),
        in_specs=[pl.BlockSpec(memory_space=pl.ANY)],
        out_specs=pl.BlockSpec(memory_space=pl.ANY),
        scratch_shapes=[pltpu.SemaphoreType.DMA, pltpu.SemaphoreType.DMA],
        compiler_params=pltpu.CompilerParams(collective_id=1, has_side_effects=True),
        name="to_heads",
    )(x)


def deliver_kernel(x_ref, mix_ref, out_ref, heads_ref, send_sem, recv_sem, mix_send, mix_recv):
    dp, ctx = lax.axis_index("dp"), lax.axis_index("ctx")
    share = share_of(dp, ctx)
    barrier = pltpu.get_barrier_semaphore()

    def greet_dp(k, carry):
        pl.semaphore_signal(
            barrier, inc=1, device_id=(lax.rem(dp + k, N_DP), ctx), device_id_type=MESH
        )
        return carry

    def greet_ctx(k, carry):
        pl.semaphore_signal(
            barrier, inc=1, device_id=(dp, lax.rem(ctx + k, N_CTX)), device_id_type=MESH
        )
        return carry

    lax.fori_loop(1, N_DP, greet_dp, 0)
    lax.fori_loop(1, N_CTX, greet_ctx, 0)
    pl.semaphore_wait(barrier, N_DP - 1 + N_CTX - 1)

    def mix_copy(k):
        peer = lax.rem(ctx + k, N_CTX)
        return pltpu.make_async_remote_copy(
            src_ref=mix_ref.at[peer],
            dst_ref=heads_ref.at[:, pl.ds(pl.multiple_of(ctx * LANES, LANES), LANES)],
            send_sem=mix_send,
            recv_sem=mix_recv,
            device_id=(dp, peer),
            device_id_type=MESH,
        )

    def copy(k):
        peer = lax.rem(dp + k, N_DP)
        return pltpu.make_async_remote_copy(
            src_ref=x_ref.at[peer],
            dst_ref=out_ref.at[share],
            send_sem=send_sem,
            recv_sem=recv_sem,
            device_id=(peer, ctx),
            device_id_type=MESH,
        )

    def start(k, carry):
        copy(k).start()
        return carry

    def sent(k, carry):
        copy(k).wait_send()
        return carry

    def mix_start(k, carry):
        mix_copy(k).start()
        return carry

    def mix_sent(k, carry):
        mix_copy(k).wait_send()
        return carry

    lax.fori_loop(1, N_DP, start, 0)
    lax.fori_loop(1, N_CTX, mix_start, 0)
    pltpu.make_async_copy(x_ref.at[dp], out_ref.at[share], recv_sem).start()
    pltpu.make_async_copy(
        mix_ref.at[ctx],
        heads_ref.at[:, pl.ds(pl.multiple_of(ctx * LANES, LANES), LANES)],
        mix_recv,
    ).start()
    lax.fori_loop(1, N_DP, sent, 0)
    lax.fori_loop(1, N_CTX, mix_sent, 0)
    all_arrived(out_ref, recv_sem)
    all_arrived(heads_ref, mix_recv)


def deliver(x, mix):
    rows = FRAMES // N_CTX
    return pl.pallas_call(
        deliver_kernel,
        out_shape=(
            jax.ShapeDtypeStruct(x.shape, x.dtype),
            jax.ShapeDtypeStruct((rows, N_CTX * LANES), x.dtype),
        ),
        in_specs=[pl.BlockSpec(memory_space=pl.ANY)] * 2,
        out_specs=[pl.BlockSpec(memory_space=pl.ANY)] * 2,
        scratch_shapes=[pltpu.SemaphoreType.DMA] * 4,
        compiler_params=pltpu.CompilerParams(collective_id=2, has_side_effects=True),
        name="deliver",
    )(x, mix)


def attend_kernel(len_ref, x_ref, out_ref):
    block = pl.program_id(0)
    ends = [len_ref[0, 0]]
    for i in range(1, 4):
        ends.append(ends[-1] + len_ref[0, i])
    first = block * UNITS
    last = first + UNITS - 1
    low = jnp.int32(0)
    high = jnp.int32(FRAMES // SEG_UNIT)
    for end in ends:
        low = jnp.where(end <= first, jnp.maximum(low, end), low)
        high = jnp.where(end > last, jnp.minimum(high, end), high)
    per_key = KBLOCK // SEG_UNIT
    low_block = low // per_key
    high_block = (high + per_key - 1) // per_key

    def segment(unit):
        seg = jnp.zeros(unit.shape, jnp.int32)
        for end in ends[:3]:
            seg = seg + (unit >= end).astype(jnp.int32)
        return seg

    per_tile = QBLOCK // TILE
    queries = x_ref[pl.ds(block * per_tile, per_tile), :, 0].reshape(QBLOCK, LANES) * 0.125
    lane = lax.broadcasted_iota(jnp.int32, (QBLOCK, LANES), 1)
    zero = jnp.zeros_like(queries)
    both = jnp.concatenate(
        [jnp.where(lane < HEAD_DIM, queries, zero), jnp.where(lane < HEAD_DIM, zero, queries)], axis=0
    )
    row = lax.broadcasted_iota(jnp.int32, (2 * QBLOCK, 1), 0)
    row_seg = segment(first + lax.rem(row, QBLOCK) // SEG_UNIT)
    key_tiles = KBLOCK // TILE

    def step(index, carry):
        top, total, mixed = carry
        keys = x_ref[pl.ds(index * key_tiles, key_tiles), :, 1].reshape(KBLOCK, LANES)
        values = x_ref[pl.ds(index * key_tiles, key_tiles), :, 2].reshape(KBLOCK, LANES)
        scores = lax.dot_general(
            both, keys, (((1,), (1,)), ((), ())), preferred_element_type=jnp.float32
        )
        col = lax.broadcasted_iota(jnp.int32, (1, KBLOCK), 1)
        col_seg = segment(index * per_key + col // SEG_UNIT)
        scores = jnp.where(row_seg == col_seg, scores, -2e30)
        new_top = jnp.maximum(top, jnp.max(scores, axis=1, keepdims=True))
        weights = jnp.exp(scores - new_top)
        scale = jnp.exp(top - new_top)
        total = total * scale + jnp.sum(weights, axis=1, keepdims=True)
        mixed = mixed * scale + jnp.dot(
            weights.astype(jnp.bfloat16), values, preferred_element_type=jnp.float32
        )
        return new_top, total, mixed

    top, total, mixed = lax.fori_loop(
        low_block,
        high_block,
        step,
        (
            jnp.full((2 * QBLOCK, 1), -1e30, jnp.float32),
            jnp.zeros((2 * QBLOCK, 1), jnp.float32),
            jnp.zeros((2 * QBLOCK, LANES), jnp.float32),
        ),
    )
    mixed = mixed / total
    out_ref[0] = jnp.where(lane < HEAD_DIM, mixed[:QBLOCK], mixed[QBLOCK:]).astype(jnp.bfloat16)


def attend(lengths, x):
    blocks = FRAMES // QBLOCK
    return pl.pallas_call(
        attend_kernel,
        grid_spec=pltpu.PrefetchScalarGridSpec(
            num_scalar_prefetch=1,
            grid=(blocks,),
            in_specs=[pl.BlockSpec(x.shape, lambda i, lens: (0, 0, 0, 0, 0))],
            out_specs=pl.BlockSpec((1, QBLOCK, LANES), lambda i, lens: (i, 0, 0)),
        ),
        out_shape=jax.ShapeDtypeStruct((blocks, QBLOCK, LANES), jnp.bfloat16),
        compiler_params=pltpu.CompilerParams(vmem_limit_bytes=48 * 2**20),
        cost_estimate=pl.CostEstimate(
            flops=8 * FRAMES * FRAMES * LANES, bytes_accessed=2**21, transcendentals=2 * FRAMES * FRAMES
        ),
        name="attend",
    )(lengths, x)


def with_halo(cells, width):
    ends = N_CTX - 1
    head = cells[:width]
    tail = cells[cells.shape[0] - width :]
    return jnp.concatenate(
        [
            lax.ppermute(tail, "ctx", [(i, (i + 1) % N_CTX) for i in range(ends)]),
            cells,
            lax.ppermute(head, "ctx", [((i + 1) % N_CTX, i) for i in range(ends)]),
        ],
        axis=0,
    )


def segment_of(positions, seg_ends):
    unit_index = positions // SEG_UNIT
    return jnp.sum((seg_ends[None, :] <= unit_index[:, None]).astype(jnp.int32), axis=1)


def convolve(signal, lengths, conv_taps, norm_scale, norm_shift):
    row_count = signal.shape[0]
    seg_ends = jnp.cumsum(lengths[0])
    column = lax.axis_index("ctx")
    half_width = (KERNEL - 1) // 2
    query_seg = segment_of(
        column * row_count + jnp.arange(row_count, dtype=jnp.int32), seg_ends
    )
    padded = with_halo(signal, half_width).astype(jnp.float32)
    padded_seg = segment_of(
        column * row_count - half_width + jnp.arange(row_count + 2 * half_width, dtype=jnp.int32),
        seg_ends,
    )
    conv_sum = jnp.zeros(signal.shape, jnp.float32)
    for tap in range(KERNEL):
        same_seg = (padded_seg[tap : tap + row_count] == query_seg)[:, None]
        conv_sum = conv_sum + jnp.where(
            same_seg, conv_taps[tap] * padded[tap : tap + row_count], 0.0
        )
    return jax.nn.silu(norm_scale * conv_sum + norm_shift).astype(jnp.bfloat16)


def on_device(
    query_loader,
    key_loader,
    value_loader,
    conv_loader,
    slot_tile,
    lengths,
    conv_taps,
    norm_scale,
    norm_shift,
):
    qkv = jnp.stack([query_loader[0], key_loader[0], value_loader[0]])
    qkv = qkv.reshape(3, TILES_DEV, TILE // ROWS, ROWS, N_CTX, LANES)
    qkv = jnp.transpose(qkv, (2, 4, 1, 0, 3, 5)).reshape(N_DP, TILES_DEV * QKV, LANES)
    conv = conv_loader[0].reshape(TILES_DEV, N_DP, CONV_ROWS, LANES)
    conv = jnp.transpose(conv, (1, 0, 2, 3)).reshape(N_DP, TILES_DEV * CONV_ROWS, LANES)
    got = spread(jnp.concatenate([qkv, conv], axis=1))
    order = slot_tile[0]
    got_qkv = got[:, : TILES_DEV * QKV].reshape(N_DP * TILES_DEV, 3, ROWS, LANES)
    send_qkv = got_qkv[order].reshape(N_DP, TILES_DEV, 3, ROWS, LANES)
    got_conv = got[:, TILES_DEV * QKV :].reshape(N_DP * TILES_DEV, CONV_ROWS, LANES)
    send_conv = got_conv[order].reshape(N_DP, TILES_DEV * CONV_ROWS, LANES)
    heads = to_heads(send_qkv)
    mix = attend(lengths, heads)
    signal, attention_out = deliver(send_conv, mix)
    signal = signal.reshape(N_DP, TILES_DEV, TILE // N_DP, CONV_ROWS // 2 * LANES)
    signal = jnp.transpose(signal, (1, 0, 2, 3)).reshape(TILES_DEV * TILE, CONV_ROWS // 2 * LANES)
    conv_out = convolve(signal, lengths, conv_taps, norm_scale, norm_shift)
    return (attention_out[None], conv_out[None])


def solution(mesh):
    return jax.shard_map(
        on_device,
        mesh=mesh,
        in_specs=(
            P("dp", "ctx", None),
            P("dp", "ctx", None),
            P("dp", "ctx", None),
            P("dp", "ctx", None),
            P("ctx", None),
            P("dp", None),
            P(),
            P(),
            P(),
        ),
        out_specs=(P("dp", "ctx", None), P("dp", "ctx", None)),
        check_vma=False,
    )
```

```python
import jax
import jax.numpy as jnp
from jax import lax
from jax.experimental import pallas as pl
from jax.experimental.pallas import tpu as pltpu
from jax.sharding import PartitionSpec as P

MESH = pl.DeviceIdType.MESH
HEADS = 16
HEAD_DIM = 64
CHANNELS = 1536
KERNEL = 31
TILE = 128
TILES_DEV = 2
SEG_UNIT = 32
FRAMES = 2048
COLUMN = 256
LANES = 128
N_DP = 64
N_CTX = 8
QBLOCK = 256
KBLOCK = 256
UNITS = QBLOCK // SEG_UNIT

N_Z = 16
PLANE_DP = 4
PLANE = PLANE_DP * N_CTX
HELD = PLANE * TILES_DEV
SHIFTS = N_Z - 1
NEAR, NEAR_SLOTS, FAR_SLOTS = 6, 5, 4
RELAYS, RELAY_SLOTS = 10, 2
MAIN = NEAR * NEAR_SLOTS + (SHIFTS - NEAR) * FAR_SLOTS
EXTRA = RELAYS * RELAY_SLOTS
TABLE = 256
AT_MAIN, AT_EXTRA, AT_FINAL, AT_BAD = 0, 72, 96, 160
RANKS = 16
PAIRS = N_Z * N_Z
LIST = 2304
FIELDS = 0x55555555


def shift_of(j):
    half = j // 2
    return jnp.where(j % 2 == 0, half + 1, N_Z - 1 - half)


def order_of(shift):
    return jnp.where(shift <= N_Z // 2, 2 * (shift - 1), 2 * (N_Z - shift) - 1)


def main_slots(shift):
    return jnp.where(order_of(shift) < NEAR, NEAR_SLOTS, FAR_SLOTS)


def main_offset(shift):
    j = order_of(shift)
    return jnp.where(j < NEAR, NEAR_SLOTS * j, NEAR * NEAR_SLOTS + FAR_SLOTS * (j - NEAR))


def relay_offset(shift):
    return RELAY_SLOTS * order_of(shift)


def place():
    dp, ctx = lax.axis_index("dp"), lax.axis_index("ctx")
    return dp // PLANE_DP, dp % PLANE_DP, ctx


def plane_peer(z, row, ctx, k):
    index = (row * N_CTX + ctx + k) % PLANE
    return index // N_CTX, index % N_CTX, (z * PLANE_DP + index // N_CTX, index % N_CTX)


def z_peer(z, row, ctx, j):
    return ((z + shift_of(j)) % N_Z * PLANE_DP + row, ctx)


def repeat(first, last, body):
    def one(k, carry):
        body(k)
        return carry

    lax.fori_loop(first, last, one, 0)


def remote(src, dst, send, recv, device):
    return pltpu.make_async_remote_copy(
        src_ref=src, dst_ref=dst, send_sem=send, recv_sem=recv, device_id=device, device_id_type=MESH
    )


def await_all(ref, sem):
    pltpu.make_async_copy(ref, ref, sem).wait()


def signal(device):
    pl.semaphore_signal(pltpu.get_barrier_semaphore(), inc=1, device_id=device, device_id_type=MESH)


class Spread:
    def __init__(self, piece, held, send, recv):
        z, row, ctx = place()
        mine = pl.ds((ctx * PLANE_DP + row) * TILES_DEV, TILES_DEV)

        def copy(k):
            to_row, to_ctx, device = plane_peer(z, row, ctx, k)
            return remote(piece(to_row, to_ctx), held.at[mine], send, recv, device)

        self.copy, self.held, self.recv = copy, held, recv
        self.own = pltpu.make_async_copy(piece(row, ctx), held.at[mine], recv)

    def start(self):
        repeat(1, PLANE, lambda k: self.copy(k).start())
        self.own.start()

    def arrived(self):
        await_all(self.held, self.recv)

    def sent(self):
        repeat(1, PLANE, lambda k: self.copy(k).wait_send())


class Along:
    def __init__(self, groups, staged, got, send, recv):
        z, row, ctx = place()
        self.staged, self.got, self.send, self.recv = staged, got, send, recv

        def copy(j, offset, slots):
            part = pl.ds(offset, slots)
            return remote(staged.at[part], got.at[part], send, recv, z_peer(z, row, ctx, j))

        self.copy, self.groups = copy, groups

    def start(self):
        for first, last, base, slots in self.groups:
            repeat(
                first,
                last,
                lambda j: self.copy(j, base + (j - first) * slots, slots).start(),
            )

    def arrived(self):
        await_all(self.got, self.recv)

    def sent(self):
        await_all(self.staged, self.send)


MAIN_GROUPS = ((0, NEAR, 0, NEAR_SLOTS), (NEAR, SHIFTS, NEAR * NEAR_SLOTS, FAR_SLOTS))
EXTRA_GROUPS = ((0, RELAYS, 0, RELAY_SLOTS),)


def stage_main(table, held, staged):
    def one(i):
        staged[i] = held[table[AT_MAIN + i]]

    repeat(0, MAIN, one)


def stage_extra(table, held, got, staged):
    def one(i):
        code = table[AT_EXTRA + i]
        staged[i] = jnp.where(
            code < HELD, held[jnp.minimum(code, HELD - 1)], got[jnp.clip(code - HELD, 0, MAIN - 1)]
        )

    repeat(0, EXTRA, one)


def stage_final(table, held, got, more, staged):
    def one(i):
        code = table[AT_FINAL + i]
        first = held[jnp.minimum(code, HELD - 1)]
        second = got[jnp.clip(code - HELD, 0, MAIN - 1)]
        third = more[jnp.clip(code - HELD - MAIN, 0, EXTRA - 1)]
        staged[i] = jnp.where(code < HELD, first, jnp.where(code < HELD + MAIN, second, third))

    repeat(0, HELD, one)


def head_piece(ref):
    return lambda row, ctx: ref.at[:, row, :, pl.ds(pl.multiple_of(ctx * LANES, LANES), LANES)]


WIDE = CHANNELS // PLANE_DP


def conv_piece(ref):
    return lambda row, ctx: ref.at[:, ctx, :, pl.ds(pl.multiple_of(row * WIDE, LANES), WIDE)]


def first_kernel(q_ref, list_ref, held_ref, lists_ref, send, recv, list_send, list_recv):
    z, row, ctx = place()
    repeat(1, PLANE, lambda k: signal(plane_peer(z, row, ctx, k)[2]))
    pl.semaphore_wait(pltpu.get_barrier_semaphore(), PLANE - 1)

    def tell(k):
        device = (z * PLANE_DP + row, (ctx + k) % N_CTX)
        return remote(list_ref, lists_ref.at[ctx], list_send, list_recv, device)

    repeat(1, N_CTX, lambda k: tell(k).start())
    pltpu.make_async_copy(list_ref, lists_ref.at[ctx], list_recv).start()
    spread = Spread(head_piece(q_ref), held_ref, send, recv)
    spread.start()
    repeat(1, N_CTX, lambda k: tell(k).wait_send())
    await_all(lists_ref, list_recv)
    spread.arrived()
    spread.sent()


def first(q, own_list):
    return pl.pallas_call(
        first_kernel,
        out_shape=(
            jax.ShapeDtypeStruct((HELD, SEG_UNIT, LANES), q.dtype),
            jax.ShapeDtypeStruct((N_CTX,) + own_list.shape, own_list.dtype),
        ),
        in_specs=[pl.BlockSpec(memory_space=pl.ANY)] * 2,
        out_specs=[pl.BlockSpec(memory_space=pl.ANY)] * 2,
        scratch_shapes=[pltpu.SemaphoreType.DMA] * 4,
        compiler_params=pltpu.CompilerParams(collective_id=0, has_side_effects=True),
        name="spread_queries",
    )(q, own_list)


def filled(fields):
    return (fields | (fields >> 1)) & FIELDS


def field_index(bit):
    def step(mask, worth):
        return jnp.where((bit & mask) != 0, worth, 0)

    high = jnp.where(bit >= (1 << 16), 8, 0)
    return high + step(0x7F00FF00, 4) + step(0x70F0F0F0, 2) + step(0x4CCCCCCC & FIELDS, 1)


def route_kernel(
    lists_ref,
    table,
    count_v,
    tile_v,
    slot_v,
    count,
    tile,
    slot,
    direct,
    relay_free,
    next_rank,
    next_main,
    next_extra,
    from_z,
    to_z,
    through,
    sems,
):
    me = lax.axis_index("dp") // PLANE_DP
    tiles = lists_ref[...]
    source = tiles >> 3
    rows = lax.broadcasted_iota(jnp.int32, (HELD, LANES), 0)
    lanes = lax.broadcasted_iota(jnp.int32, (HELD, LANES), 1)
    local = (rows & ~7) + (tiles & 7)
    position = ((rows & 7) >> 1) * 16 + (rows >> 3) * 2 + (rows & 1)

    def add_rank(i, rank):
        other = lists_ref[pl.ds(i, 1), :] >> 3
        return rank + jnp.where((other == source) & (rows > i), 1, 0)

    rank = lax.fori_loop(0, HELD, add_rank, jnp.zeros((HELD, LANES), jnp.int32))
    here = lanes == me
    column_source = jnp.sum(jnp.where(here, source, 0), axis=1, keepdims=True)
    column_rank = jnp.sum(jnp.where(here, rank, 0), axis=1, keepdims=True)
    mine = source == me
    for i in range(N_Z):
        count_v[pl.ds(i, 1), :] = jnp.sum(
            jnp.where(source == i, 1, 0), axis=0, keepdims=True, dtype=jnp.int32
        )
    for i in range(RANKS):
        tile_v[pl.ds(i, 1), :] = jnp.sum(
            jnp.where(mine & (rank == i), local, 0), axis=0, keepdims=True, dtype=jnp.int32
        )
        slot_v[pl.ds(i, 1), :] = jnp.sum(
            jnp.where((column_source == lanes) & (column_rank == i), position, 0),
            axis=0,
            keepdims=True,
            dtype=jnp.int32,
        )
    copies = [
        pltpu.make_async_copy(a, b, sems.at[i])
        for i, (a, b) in enumerate(((count_v, count), (tile_v, tile), (slot_v, slot)))
    ]
    for copy in copies:
        copy.start()

    def clear(i):
        table[i] = 0

    repeat(0, TABLE, clear)

    def relay_fields(y):
        def add(m, fields):
            shift = (y - m) & 15
            open_ = (shift != 0) & (order_of(shift) < RELAYS)
            return fields | jnp.where(open_, jnp.int32(RELAY_SLOTS) << (2 * m), 0)

        relay_free[y] = lax.fori_loop(0, N_Z, add, jnp.int32(0))

    repeat(0, N_Z, relay_fields)
    for copy in copies:
        copy.wait()

    def place_row(z, carry):
        own = jnp.int32(1) << (2 * z)

        def open_pair(y, carry):
            free, bad = carry
            held = count[z, y]
            bad = bad | jnp.where(held > RANKS, 1, 0)
            shift = (y - z) & 15
            most = jnp.where(shift == 0, RANKS, main_slots(shift))
            straight = jnp.minimum(held, most)
            direct[z * N_Z + y] = straight
            left = jnp.where(shift == 0, 3, jnp.minimum(most - straight, 3))
            return free | (left << (2 * y)), bad

        free, bad = lax.fori_loop(0, N_Z, open_pair, (jnp.int32(0), carry[1]))

        def add(n, y, bit):
            from_z[n] = z
            to_z[n] = y
            through[n] = bit

        def take(free, bit):
            return free - jnp.where(bit == own, 0, bit)

        def place_pair(i, carry):
            y = (i + z) & 15
            shift = (y - z) & 15
            most = jnp.where(shift == 0, RANKS, main_slots(shift))
            excess = jnp.minimum(count[z, y], RANKS) - most

            def place_one(_, carry):
                free, n, bad = carry
                open_ = filled(free) & filled(relay_free[y])

                def simple():
                    late = open_ & (jnp.int32(-1) << (2 * ((y + 8) & 15)))
                    chosen = jnp.where(late != 0, late, open_)
                    bit = chosen & -chosen
                    relay_free[y] = relay_free[y] - bit
                    add(n, y, bit)
                    return take(free, bit), n + 1, bad

                def swap():
                    def look(m, carry):
                        free, n, done = carry
                        bit = jnp.int32(1) << (2 * m)
                        other = filled(free) & filled(relay_free[m])
                        fits = (
                            (done == 0)
                            & (m != z)
                            & (m != y)
                            & ((filled(relay_free[y]) & bit) != 0)
                            & (direct[z * N_Z + m] > 0)
                            & (other != 0)
                        )

                        def do():
                            instead = other & -other
                            direct[z * N_Z + m] = direct[z * N_Z + m] - 1
                            relay_free[m] = relay_free[m] - instead
                            relay_free[y] = relay_free[y] - bit
                            add(n, m, instead)
                            add(n + 1, y, bit)
                            return take(free, instead), n + 2, jnp.int32(1)

                        return lax.cond(fits, do, lambda: (free, n, done))

                    free_, n_, done = lax.fori_loop(0, N_Z, look, (free, n, jnp.int32(0)))
                    return free_, n_, bad | (1 - done)

                return lax.cond(open_ != 0, simple, swap)

            return lax.fori_loop(0, excess, place_one, carry)

        free, n, bad = lax.fori_loop(0, N_Z, place_pair, (free, carry[0], bad))
        return n, bad

    n, bad = lax.fori_loop(0, N_Z, place_row, (jnp.int32(0), jnp.int32(0)))
    table[AT_BAD] = bad

    def begin(i):
        next_rank[i] = direct[i]
        next_main[i] = direct[i]
        next_extra[i] = 0

    repeat(0, PAIRS, begin)

    def straight(other):
        shift_out = (other - me) & 15
        shift_in = (me - other) & 15

        def out(r):
            @pl.when(shift_out != 0)
            def _():
                table[AT_MAIN + main_offset(shift_out) + r] = tile[r, other]

        def arrive(r):
            table[AT_FINAL + slot[r, other]] = jnp.where(
                shift_in == 0, tile[r, other], HELD + main_offset(shift_in) + r
            )

        repeat(0, direct[me * N_Z + other], out)
        repeat(0, direct[other * N_Z + me], arrive)

    repeat(0, N_Z, straight)

    def finish(i):
        z, y, bit = from_z[i], to_z[i], through[i]
        m = field_index(bit)
        rank = next_rank[z * N_Z + y]
        next_rank[z * N_Z + y] = rank + 1
        stays = m == z
        main = next_main[z * N_Z + m]
        next_main[z * N_Z + m] = main + 1
        extra = next_extra[m * N_Z + y]
        next_extra[m * N_Z + y] = extra + 1
        main_at = main_offset((m - z) & 15) + main
        extra_at = relay_offset((y - m) & 15) + extra

        @pl.when((z == me) & jnp.logical_not(stays))
        def _():
            table[AT_MAIN + main_at] = tile[rank, y]

        @pl.when(m == me)
        def _():
            table[AT_EXTRA + extra_at] = jnp.where(stays, tile[rank, y], HELD + main_at)

        @pl.when(y == me)
        def _():
            table[AT_FINAL + slot[rank, z]] = HELD + MAIN + extra_at

    repeat(0, n, finish)


def route(lists):
    smem = pltpu.SMEM
    pair = smem((PAIRS,), jnp.int32)
    square = smem((N_Z, LANES), jnp.int32)
    square_v = pltpu.VMEM((N_Z, LANES), jnp.int32)
    return pl.pallas_call(
        route_kernel,
        out_shape=jax.ShapeDtypeStruct((TABLE,), jnp.int32),
        in_specs=[pl.BlockSpec(memory_space=pltpu.VMEM)],
        out_specs=pl.BlockSpec(memory_space=smem),
        scratch_shapes=[square_v] * 3
        + [square] * 3
        + [pair, smem((N_Z,), jnp.int32), pair, pair, pair]
        + [smem((LIST,), jnp.int32)] * 3
        + [pltpu.SemaphoreType.DMA((3,))],
        name="route",
    )(lists)


def heads_kernel(
    table, held_q, k_ref, v_ref, conv_ref, q_out, k_out, v_out, held_conv, *scratch
):
    z, row, ctx = place()
    repeat(1, PLANE, lambda k: signal(plane_peer(z, row, ctx, k)[2]))
    repeat(0, SHIFTS, lambda j: signal(z_peer(z, row, ctx, j)))
    pl.semaphore_wait(pltpu.get_barrier_semaphore(), PLANE - 1 + SHIFTS)
    held_k, held_v, *scratch = scratch
    main_staged, main_got, extra_staged, extra_got, staged = (scratch[3 * i : 3 * i + 3] for i in range(5))
    sems = scratch[15]
    held = (held_q, held_k, held_v)
    outs = (q_out, k_out, v_out)
    spread = [
        None,
        Spread(head_piece(k_ref), held_k, sems.at[0], sems.at[1]),
        Spread(head_piece(v_ref), held_v, sems.at[2], sems.at[3]),
    ]
    spread_conv = Spread(conv_piece(conv_ref), held_conv, sems.at[4], sems.at[5])
    main = [
        Along(MAIN_GROUPS, main_staged[i], main_got[i], sems.at[6 + 2 * i], sems.at[7 + 2 * i])
        for i in range(3)
    ]
    extra = [
        Along(EXTRA_GROUPS, extra_staged[i], extra_got[i], sems.at[12 + 2 * i], sems.at[13 + 2 * i])
        for i in range(3)
    ]

    def final_copy(i, k):
        to = (row + k) % PLANE_DP
        return remote(
            staged[i].at[pl.ds(to * 16, 16)],
            outs[i].at[:, row],
            sems.at[18 + 2 * i],
            sems.at[19 + 2 * i],
            (z * PLANE_DP + to, ctx),
        )

    def start_main(i):
        if i:
            spread[i].arrived()
        stage_main(table, held[i], main_staged[i])
        main[i].start()

    def start_extra(i):
        main[i].arrived()
        stage_extra(table, held[i], main_got[i], extra_staged[i])
        extra[i].start()

    def start_final(i):
        extra[i].arrived()
        stage_final(table, held[i], main_got[i], extra_got[i], staged[i])
        repeat(1, PLANE_DP, lambda k: final_copy(i, k).start())
        pltpu.make_async_copy(
            staged[i].at[pl.ds(row * 16, 16)], outs[i].at[:, row], sems.at[19 + 2 * i]
        ).start()

    spread[1].start()
    start_main(0)
    spread[2].start()
    start_main(1)
    spread_conv.start()
    start_extra(0)
    start_main(2)
    start_extra(1)
    start_final(0)
    start_extra(2)
    start_final(1)
    start_final(2)
    spread_conv.arrived()
    spread_conv.sent()
    for i in range(3):
        if i:
            spread[i].sent()
        main[i].sent()
        extra[i].sent()
        repeat(1, PLANE_DP, lambda k: final_copy(i, k).wait_send())
        await_all(outs[i], sems.at[19 + 2 * i])


def to_heads(table, held_q, k, v, conv):
    unit = (SEG_UNIT, LANES)
    kind = held_q.dtype

    def buffers(count):
        return [pltpu.VMEM((count,) + unit, kind)] * 3

    heads = jax.ShapeDtypeStruct((N_CTX * TILES_DEV, PLANE_DP) + unit, kind)
    return pl.pallas_call(
        heads_kernel,
        out_shape=(heads, heads, heads, jax.ShapeDtypeStruct((HELD, 16, WIDE), kind)),
        in_specs=[pl.BlockSpec(memory_space=pltpu.SMEM), pl.BlockSpec(memory_space=pltpu.VMEM)]
        + [pl.BlockSpec(memory_space=pl.ANY)] * 3,
        out_specs=[pl.BlockSpec(memory_space=pl.ANY)] * 4,
        scratch_shapes=buffers(HELD)[:2]
        + buffers(MAIN)
        + buffers(MAIN)
        + buffers(EXTRA)
        + buffers(EXTRA)
        + buffers(HELD)
        + [pltpu.SemaphoreType.DMA((24,))],
        compiler_params=pltpu.CompilerParams(
            collective_id=1, has_side_effects=True, vmem_limit_bytes=32 * 2**20
        ),
        name="to_heads",
    )(table, held_q, k, v, conv)


def conv_kernel(
    table,
    held,
    mix_ref,
    rows_out,
    halo_out,
    heads_out,
    main_staged,
    main_got,
    extra_staged,
    extra_got,
    staged,
    sems,
    halo_sems,
):
    z, row, ctx = place()
    repeat(1, PLANE, lambda k: signal(plane_peer(z, row, ctx, k)[2]))
    repeat(0, SHIFTS, lambda j: signal(z_peer(z, row, ctx, j)))
    pl.semaphore_wait(pltpu.get_barrier_semaphore(), PLANE - 1 + SHIFTS)
    main = Along(MAIN_GROUPS, main_staged, main_got, sems.at[0], sems.at[1])
    extra = Along(EXTRA_GROUPS, extra_staged, extra_got, sems.at[2], sems.at[3])
    stage_main(table, held, main_staged)
    main.start()

    mixed = heads_out.at[:, pl.ds(pl.multiple_of(ctx * LANES, LANES), LANES)]

    def mix_copy(k):
        to = (ctx + k) % N_CTX
        return remote(mix_ref.at[to], mixed, sems.at[4], sems.at[5], (z * PLANE_DP + row, to))

    repeat(1, N_CTX, lambda k: mix_copy(k).start())
    pltpu.make_async_copy(mix_ref.at[ctx], mixed, sems.at[5]).start()

    main.arrived()
    stage_extra(table, held, main_got, extra_staged)
    extra.start()
    extra.arrived()
    stage_final(table, held, main_got, extra_got, staged)
    channels = pl.ds(pl.multiple_of(row * WIDE, LANES), WIDE)

    def part(to_row, to_ctx):
        return staged.at[pl.ds(to_row * 16 + to_ctx * TILES_DEV, TILES_DEV)]

    def copy(k):
        to_row, to_ctx, device = plane_peer(z, row, ctx, k)
        return remote(
            part(to_row, to_ctx), rows_out.at[:, ctx, :, channels], sems.at[6], sems.at[7], device
        )

    repeat(1, PLANE, lambda k: copy(k).start())
    pltpu.make_async_copy(part(row, ctx), rows_out.at[:, ctx, :, channels], sems.at[7]).start()

    def halo(side, act):
        step, tile = (1, 1) if side == 0 else (-1, 0)

        def one(k):
            to_row = k // (N_CTX - 1)
            column = k % (N_CTX - 1) + (0 if side == 0 else 1)
            target = column + step
            src = staged.at[to_row * 16 + column * TILES_DEV + tile]
            dst = halo_out.at[side, :, channels]
            is_own = (to_row == row) & (target == ctx)

            @pl.when(is_own)
            def _():
                if act == "start":
                    pltpu.make_async_copy(src, dst, halo_sems.at[side]).start()

            @pl.when(jnp.logical_not(is_own))
            def _():
                far = remote(
                    src, dst, sems.at[8], halo_sems.at[side], (z * PLANE_DP + to_row, target)
                )
                if act == "start":
                    far.start()
                else:
                    far.wait_send()

        @pl.when(ctx == (N_CTX - 1 if side == 0 else 0))
        def _():
            repeat(0, PLANE_DP * (N_CTX - 1), one)

    for act in ("start", "sent"):
        for side in (0, 1):
            halo(side, act)
    repeat(1, PLANE, lambda k: copy(k).wait_send())
    main.sent()
    extra.sent()
    repeat(1, N_CTX, lambda k: mix_copy(k).wait_send())
    await_all(heads_out, sems.at[5])
    await_all(rows_out, sems.at[7])

    @pl.when(ctx > 0)
    def _():
        await_all(halo_out.at[0], halo_sems.at[0])

    @pl.when(ctx < N_CTX - 1)
    def _():
        await_all(halo_out.at[1], halo_sems.at[1])


def to_conv(table, held, mix):
    unit = (16, WIDE)
    kind = held.dtype

    def buffer(count):
        return pltpu.VMEM((count,) + unit, kind)

    return pl.pallas_call(
        conv_kernel,
        out_shape=(
            jax.ShapeDtypeStruct((TILES_DEV, N_CTX, 16, CHANNELS), kind),
            jax.ShapeDtypeStruct((2, 16, CHANNELS), kind),
            jax.ShapeDtypeStruct((COLUMN, N_CTX * LANES), kind),
        ),
        in_specs=[
            pl.BlockSpec(memory_space=pltpu.SMEM),
            pl.BlockSpec(memory_space=pltpu.VMEM),
            pl.BlockSpec(memory_space=pl.ANY),
        ],
        out_specs=[pl.BlockSpec(memory_space=pl.ANY)] * 3,
        scratch_shapes=[buffer(MAIN), buffer(MAIN), buffer(EXTRA), buffer(EXTRA), buffer(HELD)]
        + [pltpu.SemaphoreType.DMA((9,)), pltpu.SemaphoreType.DMA((2,))],
        compiler_params=pltpu.CompilerParams(
            collective_id=2, has_side_effects=True, vmem_limit_bytes=32 * 2**20
        ),
        name="to_conv",
    )(table, held, mix)


def attend_kernel(len_ref, q_ref, k_ref, v_ref, out_ref):
    block = pl.program_id(0)
    ends = [len_ref[0, 0]]
    for i in range(1, 4):
        ends.append(ends[-1] + len_ref[0, i])
    first = block * UNITS
    last = first + UNITS - 1
    low = jnp.int32(0)
    high = jnp.int32(FRAMES // SEG_UNIT)
    for end in ends:
        low = jnp.where(end <= first, jnp.maximum(low, end), low)
        high = jnp.where(end > last, jnp.minimum(high, end), high)
    per_key = KBLOCK // SEG_UNIT
    low_block = low // per_key
    high_block = (high + per_key - 1) // per_key

    def segment(unit):
        seg = jnp.zeros(unit.shape, jnp.int32)
        for end in ends[:3]:
            seg = seg + (unit >= end).astype(jnp.int32)
        return seg

    queries = q_ref[...] * 0.125
    lane = lax.broadcasted_iota(jnp.int32, (QBLOCK, LANES), 1)
    zero = jnp.zeros_like(queries)
    both = jnp.concatenate(
        [jnp.where(lane < HEAD_DIM, queries, zero), jnp.where(lane < HEAD_DIM, zero, queries)], axis=0
    )
    row = lax.broadcasted_iota(jnp.int32, (2 * QBLOCK, 1), 0)
    row_seg = segment(first + lax.rem(row, QBLOCK) // SEG_UNIT)
    def step(index, carry):
        top, total, mixed = carry
        part = pl.ds(pl.multiple_of(index * KBLOCK, KBLOCK), KBLOCK)
        keys = k_ref[part, :]
        values = v_ref[part, :]
        scores = lax.dot_general(
            both, keys, (((1,), (1,)), ((), ())), preferred_element_type=jnp.float32
        )
        col = lax.broadcasted_iota(jnp.int32, (1, KBLOCK), 1)
        col_seg = segment(index * per_key + col // SEG_UNIT)
        scores = jnp.where(row_seg == col_seg, scores, -2e30)
        new_top = jnp.maximum(top, jnp.max(scores, axis=1, keepdims=True))
        weights = jnp.exp(scores - new_top)
        scale = jnp.exp(top - new_top)
        total = total * scale + jnp.sum(weights, axis=1, keepdims=True)
        mixed = mixed * scale + jnp.dot(
            weights.astype(jnp.bfloat16), values, preferred_element_type=jnp.float32
        )
        return new_top, total, mixed

    top, total, mixed = lax.fori_loop(
        low_block,
        high_block,
        step,
        (
            jnp.full((2 * QBLOCK, 1), -1e30, jnp.float32),
            jnp.zeros((2 * QBLOCK, 1), jnp.float32),
            jnp.zeros((2 * QBLOCK, LANES), jnp.float32),
        ),
    )
    mixed = mixed / total
    out_ref[0] = jnp.where(lane < HEAD_DIM, mixed[:QBLOCK], mixed[QBLOCK:]).astype(jnp.bfloat16)


def attend(lengths, q, k, v):
    blocks = FRAMES // QBLOCK
    return pl.pallas_call(
        attend_kernel,
        grid_spec=pltpu.PrefetchScalarGridSpec(
            num_scalar_prefetch=1,
            grid=(blocks,),
            in_specs=[
                pl.BlockSpec((QBLOCK, LANES), lambda i, lens: (i, 0)),
                pl.BlockSpec((FRAMES, LANES), lambda i, lens: (0, 0)),
                pl.BlockSpec((FRAMES, LANES), lambda i, lens: (0, 0)),
            ],
            out_specs=pl.BlockSpec((1, QBLOCK, LANES), lambda i, lens: (i, 0, 0)),
        ),
        out_shape=jax.ShapeDtypeStruct((blocks, QBLOCK, LANES), jnp.bfloat16),
        compiler_params=pltpu.CompilerParams(vmem_limit_bytes=48 * 2**20),
        cost_estimate=pl.CostEstimate(
            flops=8 * FRAMES * FRAMES * LANES, bytes_accessed=2**21, transcendentals=2 * FRAMES * FRAMES
        ),
        name="attend",
    )(lengths, q, k, v)


def with_halo(cells, sides, width):
    for axis, dim in sides:
        count = lax.axis_size(axis)
        ends = count - 1
        head = lax.slice_in_dim(cells, 0, width, axis=dim)
        tail = lax.slice_in_dim(cells, cells.shape[dim] - width, cells.shape[dim], axis=dim)
        cells = jnp.concatenate(
            [
                lax.ppermute(tail, axis, [(i, (i + 1) % count) for i in range(ends)]),
                cells,
                lax.ppermute(head, axis, [((i + 1) % count, i) for i in range(ends)]),
            ],
            axis=dim,
        )
    return cells


def segment_of(positions, seg_ends):
    unit_index = positions // SEG_UNIT
    return jnp.sum((seg_ends[None, :] <= unit_index[:, None]).astype(jnp.int32), axis=1)


def split_shares(loader, dp_count):
    return loader[0].reshape(TILES_DEV, dp_count, TILE // dp_count, loader.shape[2])


def arrange_tiles(spread, tile_order, dp_count):
    shares = spread.reshape(dp_count * TILES_DEV, TILE // dp_count, spread.shape[3])
    return shares[tile_order]


def softmax_update(carry, queries, query_seg, keys_piece, values_piece, key_seg):
    running_max, norm_total, accumulated = carry
    scores = (
        jnp.einsum("qhd,khd->hqk", queries, keys_piece, preferred_element_type=jnp.float32) * 0.125
    )
    allowed = (query_seg[:, None] == key_seg[None, :])[None]
    masked = jnp.where(allowed, scores, -1e30)
    new_max = jnp.maximum(running_max, jnp.max(masked, axis=2))
    weights = jnp.where(allowed, jnp.exp(masked - new_max[:, :, None]), 0.0)
    norm_total = jnp.sum(weights, axis=2)
    update = jnp.einsum(
        "hqk,khd->qhd",
        weights.astype(jnp.bfloat16),
        values_piece,
        preferred_element_type=jnp.float32,
    )
    accumulated = update
    return (new_max, norm_total, accumulated)


def general_path(
    query_loader,
    key_loader,
    value_loader,
    conv_loader,
    slot_tile,
    lengths,
    conv_taps,
    norm_scale,
    norm_shift,
):
    dp_count = lax.axis_size("dp")
    row_count = query_loader.shape[1]
    feature_width = HEADS * HEAD_DIM
    spread_query, spread_key, spread_value, spread_conv = (
        lax.all_to_all(
            split_shares(query_loader, dp_count), "dp", split_axis=1, concat_axis=0, tiled=True
        ),
        lax.all_to_all(
            split_shares(key_loader, dp_count), "dp", split_axis=1, concat_axis=0, tiled=True
        ),
        lax.all_to_all(
            split_shares(value_loader, dp_count), "dp", split_axis=1, concat_axis=0, tiled=True
        ),
        lax.all_to_all(
            split_shares(conv_loader, dp_count), "dp", split_axis=1, concat_axis=0, tiled=True
        ),
    )
    tile_order = jnp.transpose(slot_tile[0].reshape(dp_count, TILES_DEV))
    send_query = arrange_tiles(spread_query, tile_order, dp_count)
    send_key = arrange_tiles(spread_key, tile_order, dp_count)
    send_value = arrange_tiles(spread_value, tile_order, dp_count)
    send_conv = arrange_tiles(spread_conv, tile_order, dp_count)
    got_query, got_key, got_value, got_conv = (
        lax.all_to_all(send_query, "dp", split_axis=1, concat_axis=1, tiled=True),
        lax.all_to_all(send_key, "dp", split_axis=1, concat_axis=1, tiled=True),
        lax.all_to_all(send_value, "dp", split_axis=1, concat_axis=1, tiled=True),
        lax.all_to_all(send_conv, "dp", split_axis=1, concat_axis=1, tiled=True),
    )
    queries = got_query.reshape(row_count, HEADS, HEAD_DIM)
    keys_local = got_key.reshape(row_count, HEADS, HEAD_DIM)
    values_local = got_value.reshape(row_count, HEADS, HEAD_DIM)
    seg_ends = jnp.cumsum(lengths[0])
    column = lax.axis_index("ctx")
    local_positions = column * row_count + jnp.arange(row_count, dtype=jnp.int32)
    query_seg = segment_of(local_positions, seg_ends)
    initial = (
        jnp.full((HEADS, row_count), -1e30, jnp.float32),
        jnp.zeros((HEADS, row_count), jnp.float32),
        jnp.zeros((row_count, HEADS, HEAD_DIM), jnp.float32),
    )
    keys_piece = lax.all_gather(keys_local, "ctx", axis=0, tiled=True)
    values_piece = lax.all_gather(values_local, "ctx", axis=0, tiled=True)
    piece_rows = keys_piece.shape[0]
    key_seg = segment_of(jnp.arange(piece_rows, dtype=jnp.int32), seg_ends)
    running_max, norm_total, accumulated = softmax_update(
        initial, queries, query_seg, keys_piece, values_piece, key_seg
    )
    mixture = (accumulated / jnp.transpose(norm_total)[:, :, None]).astype(jnp.bfloat16)
    attention_out = mixture.reshape(1, row_count, feature_width)
    signal = got_conv.reshape(row_count, got_conv.shape[3])
    half_width = (KERNEL - 1) // 2
    padded = with_halo(signal, (("ctx", 0),), half_width).astype(jnp.float32)
    padded_seg = segment_of(
        column * row_count - half_width + jnp.arange(row_count + 2 * half_width, dtype=jnp.int32),
        seg_ends,
    )
    conv_sum = jnp.zeros(signal.shape, jnp.float32)
    for offset_tap in range(KERNEL):
        same_seg = (padded_seg[offset_tap : offset_tap + row_count] == query_seg)[:, None]
        conv_sum = conv_sum + jnp.where(
            same_seg, conv_taps[offset_tap] * padded[offset_tap : offset_tap + row_count], 0.0
        )
    conv_out = jax.nn.silu(norm_scale * conv_sum + norm_shift).astype(jnp.bfloat16)
    return (attention_out, conv_out.reshape(1, row_count, signal.shape[1]))


def convolve(signal, halo, lengths, conv_taps, norm_scale, norm_shift):
    seg_ends = jnp.cumsum(lengths[0])
    column = lax.axis_index("ctx")
    half_width = (KERNEL - 1) // 2
    query_seg = segment_of(column * COLUMN + jnp.arange(COLUMN, dtype=jnp.int32), seg_ends)
    before = jnp.where(column > 0, halo[0], 0)
    after = jnp.where(column < N_CTX - 1, halo[1], 0)
    padded = jnp.concatenate([before[1:], signal, after[:half_width]], axis=0).astype(jnp.float32)
    padded_seg = segment_of(
        column * COLUMN - half_width + jnp.arange(COLUMN + 2 * half_width, dtype=jnp.int32), seg_ends
    )
    conv_sum = jnp.zeros(signal.shape, jnp.float32)
    for tap in range(KERNEL):
        same_seg = (padded_seg[tap : tap + COLUMN] == query_seg)[:, None]
        conv_sum = conv_sum + jnp.where(same_seg, conv_taps[tap] * padded[tap : tap + COLUMN], 0.0)
    return jax.nn.silu(norm_scale * conv_sum + norm_shift).astype(jnp.bfloat16)


def on_device(*inputs):
    query, key, value, conv, slot_tile, lengths, conv_taps, norm_scale, norm_shift = inputs
    places = jnp.transpose(slot_tile[0].reshape(N_Z, 8))
    places = jnp.pad(places, ((0, 0), (0, LANES - N_Z)), constant_values=1 << 16)
    shape = (TILES_DEV, PLANE_DP, SEG_UNIT, HEADS * HEAD_DIM)
    held_q, lists = first(query.reshape(shape), places)
    table = route(lists.reshape(HELD, LANES))
    q, k, v, held_conv = to_heads(
        table,
        held_q,
        key.reshape(shape),
        value.reshape(shape),
        conv.reshape(TILES_DEV, N_CTX, 16, CHANNELS),
    )
    heads = (FRAMES, LANES)
    mix = attend(lengths, q.reshape(heads), k.reshape(heads), v.reshape(heads))
    rows, halo, attention_out = to_conv(table, held_conv, mix)
    conv_out = convolve(
        rows.reshape(COLUMN, CHANNELS), halo, lengths, conv_taps, norm_scale, norm_shift
    )
    return lax.cond(
        table[AT_BAD] == 0,
        lambda: (attention_out[None], conv_out[None]),
        lambda: general_path(*inputs),
    )


def solution(mesh):
    return jax.shard_map(
        on_device,
        mesh=mesh,
        in_specs=(
            P("dp", "ctx", None),
            P("dp", "ctx", None),
            P("dp", "ctx", None),
            P("dp", "ctx", None),
            P("ctx", None),
            P("dp", None),
            P(),
            P(),
            P(),
        ),
        out_specs=(P("dp", "ctx", None), P("dp", "ctx", None)),
        check_vma=False,
    )
```

```python
import jax
import jax.numpy as jnp
from jax import lax
from jax.experimental import pallas as pl
from jax.experimental.pallas import tpu as pltpu
from jax.sharding import PartitionSpec as P

MESH = pl.DeviceIdType.MESH
HEADS = 16
HEAD_DIM = 64
CHANNELS = 1536
KERNEL = 31
TILE = 128
TILES_DEV = 2
SEG_UNIT = 32
FRAMES = 2048
COLUMN = 256
LANES = 128
N_DP = 64
N_CTX = 8
ROWS = 16
QKV = 3 * ROWS
CONV_ROWS = 24
QBLOCK = 256
KBLOCK = 256
UNITS = QBLOCK // SEG_UNIT

N_Z = 16
PLANE_DP = 4
PLANE = PLANE_DP * N_CTX
HELD = PLANE * TILES_DEV
SHIFTS = N_Z - 1
NEAR, NEAR_SLOTS, FAR_SLOTS = 6, 5, 4
RELAYS, RELAY_SLOTS = 10, 2
MAIN = NEAR * NEAR_SLOTS + (SHIFTS - NEAR) * FAR_SLOTS
EXTRA = RELAYS * RELAY_SLOTS
TABLE = 256
AT_MAIN, AT_EXTRA, AT_FINAL, AT_BAD = 0, 72, 96, 160
RANKS = 16
PAIRS = N_Z * N_Z
LIST = 2304
FIELDS = 0x55555555


def shift_of(j):
    half = j // 2
    return jnp.where(j % 2 == 0, half + 1, N_Z - 1 - half)


def order_of(shift):
    return jnp.where(shift <= N_Z // 2, 2 * (shift - 1), 2 * (N_Z - shift) - 1)


def main_slots(shift):
    return jnp.where(order_of(shift) < NEAR, NEAR_SLOTS, FAR_SLOTS)


def main_offset(shift):
    j = order_of(shift)
    return jnp.where(j < NEAR, NEAR_SLOTS * j, NEAR * NEAR_SLOTS + FAR_SLOTS * (j - NEAR))


def relay_offset(shift):
    return RELAY_SLOTS * order_of(shift)


def place():
    dp, ctx = lax.axis_index("dp"), lax.axis_index("ctx")
    return dp // PLANE_DP, dp % PLANE_DP, ctx


def plane_peer(z, row, ctx, k):
    index = (row * N_CTX + ctx + k) % PLANE
    return index // N_CTX, index % N_CTX, (z * PLANE_DP + index // N_CTX, index % N_CTX)


def z_peer(z, row, ctx, j):
    return ((z + shift_of(j)) % N_Z * PLANE_DP + row, ctx)


def repeat(first, last, body):
    def one(k, carry):
        body(k)
        return carry

    lax.fori_loop(first, last, one, 0)


def remote(src, dst, send, recv, device):
    return pltpu.make_async_remote_copy(
        src_ref=src, dst_ref=dst, send_sem=send, recv_sem=recv, device_id=device, device_id_type=MESH
    )


def await_all(ref, sem):
    pltpu.make_async_copy(ref, ref, sem).wait()


def signal(device):
    pl.semaphore_signal(pltpu.get_barrier_semaphore(), inc=1, device_id=device, device_id_type=MESH)


class Spread:
    def __init__(self, piece, held, send, recv):
        z, row, ctx = place()
        mine = pl.ds((ctx * PLANE_DP + row) * TILES_DEV, TILES_DEV)

        def copy(k):
            to_row, to_ctx, device = plane_peer(z, row, ctx, k)
            return remote(piece(to_row, to_ctx), held.at[mine], send, recv, device)

        self.copy, self.held, self.recv = copy, held, recv
        self.own = pltpu.make_async_copy(piece(row, ctx), held.at[mine], recv)

    def start(self):
        repeat(1, PLANE, lambda k: self.copy(k).start())
        self.own.start()

    def arrived(self):
        await_all(self.held, self.recv)

    def sent(self):
        repeat(1, PLANE, lambda k: self.copy(k).wait_send())


class Along:
    def __init__(self, groups, staged, got, send, recv):
        z, row, ctx = place()
        self.staged, self.got, self.send, self.recv = staged, got, send, recv

        def copy(j, offset, slots):
            part = pl.ds(offset, slots)
            return remote(staged.at[part], got.at[part], send, recv, z_peer(z, row, ctx, j))

        self.copy, self.groups = copy, groups

    def start(self):
        for first, last, base, slots in self.groups:
            repeat(
                first,
                last,
                lambda j: self.copy(j, base + (j - first) * slots, slots).start(),
            )

    def arrived(self):
        await_all(self.got, self.recv)

    def sent(self):
        await_all(self.staged, self.send)


MAIN_GROUPS = ((0, NEAR, 0, NEAR_SLOTS), (NEAR, SHIFTS, NEAR * NEAR_SLOTS, FAR_SLOTS))
EXTRA_GROUPS = ((0, RELAYS, 0, RELAY_SLOTS),)


def stage_main(table, held, staged):
    def one(i):
        staged[i] = held[table[AT_MAIN + i]]

    repeat(0, MAIN, one)


def stage_extra(table, held, got, staged):
    def one(i):
        code = table[AT_EXTRA + i]
        staged[i] = jnp.where(
            code < HELD, held[jnp.minimum(code, HELD - 1)], got[jnp.clip(code - HELD, 0, MAIN - 1)]
        )

    repeat(0, EXTRA, one)


def stage_final(table, held, got, more, staged):
    def one(i):
        code = table[AT_FINAL + i]
        first = held[jnp.minimum(code, HELD - 1)]
        second = got[jnp.clip(code - HELD, 0, MAIN - 1)]
        third = more[jnp.clip(code - HELD - MAIN, 0, EXTRA - 1)]
        staged[i] = jnp.where(code < HELD, first, jnp.where(code < HELD + MAIN, second, third))

    repeat(0, HELD, one)


def head_piece(ref):
    return lambda row, ctx: ref.at[:, row, :, pl.ds(pl.multiple_of(ctx * LANES, LANES), LANES)]


WIDE = CHANNELS // PLANE_DP


def conv_piece(ref):
    return lambda row, ctx: ref.at[:, ctx, :, pl.ds(pl.multiple_of(row * WIDE, LANES), WIDE)]


def first_kernel(q_ref, list_ref, held_ref, lists_ref, send, recv, list_send, list_recv):
    z, row, ctx = place()
    repeat(1, PLANE, lambda k: signal(plane_peer(z, row, ctx, k)[2]))
    pl.semaphore_wait(pltpu.get_barrier_semaphore(), PLANE - 1)

    def tell(k):
        device = (z * PLANE_DP + row, (ctx + k) % N_CTX)
        return remote(list_ref, lists_ref.at[ctx], list_send, list_recv, device)

    repeat(1, N_CTX, lambda k: tell(k).start())
    pltpu.make_async_copy(list_ref, lists_ref.at[ctx], list_recv).start()
    spread = Spread(head_piece(q_ref), held_ref, send, recv)
    spread.start()
    repeat(1, N_CTX, lambda k: tell(k).wait_send())
    await_all(lists_ref, list_recv)
    spread.arrived()
    spread.sent()


def first(q, own_list):
    return pl.pallas_call(
        first_kernel,
        out_shape=(
            jax.ShapeDtypeStruct((HELD, SEG_UNIT, LANES), q.dtype),
            jax.ShapeDtypeStruct((N_CTX,) + own_list.shape, own_list.dtype),
        ),
        in_specs=[pl.BlockSpec(memory_space=pl.ANY)] * 2,
        out_specs=[pl.BlockSpec(memory_space=pl.ANY)] * 2,
        scratch_shapes=[pltpu.SemaphoreType.DMA] * 4,
        compiler_params=pltpu.CompilerParams(collective_id=0, has_side_effects=True),
        name="spread_queries",
    )(q, own_list)


def filled(fields):
    return (fields | (fields >> 1)) & FIELDS


def field_index(bit):
    def step(mask, worth):
        return jnp.where((bit & mask) != 0, worth, 0)

    high = jnp.where(bit >= (1 << 16), 8, 0)
    return high + step(0x7F00FF00, 4) + step(0x70F0F0F0, 2) + step(0x4CCCCCCC & FIELDS, 1)


def field_value(fields, bit):
    return jnp.where((fields & bit) != 0, 1, 0) + jnp.where((fields & (bit << 1)) != 0, 2, 0)


def relay_fields(y):
    fields = 0
    for m in range(N_Z):
        shift = (y - m) % N_Z
        order = 2 * (shift - 1) if shift <= N_Z // 2 else 2 * (N_Z - shift) - 1
        if shift and order < RELAYS:
            fields |= RELAY_SLOTS << (2 * m)
    return fields - (1 << 32) if fields >= 1 << 31 else fields


LOW, HIGH, OVER = N_Z, N_Z + 1, N_Z + 2


def route_kernel(
    lists_ref,
    table,
    count_v,
    excess_v,
    tile_v,
    slot_v,
    count,
    excess,
    tile,
    slot,
    direct,
    relay_free,
    sems,
):
    me = lax.axis_index("dp") // PLANE_DP
    tiles = lists_ref[...]
    source = tiles >> 3
    rows = lax.broadcasted_iota(jnp.int32, (HELD, LANES), 0)
    lanes = lax.broadcasted_iota(jnp.int32, (HELD, LANES), 1)
    local = (rows & ~7) + (tiles & 7)
    position = ((rows & 7) >> 1) * 16 + (rows >> 3) * 2 + (rows & 1)

    def total(values):
        return jnp.sum(values, axis=0, keepdims=True, dtype=jnp.int32)

    for i in range(N_Z):
        count_v[pl.ds(i, 1), :] = total(jnp.where(source == i, 1, 0))
    held = count_v[...]
    z = lax.broadcasted_iota(jnp.int32, held.shape, 0)
    y = lax.broadcasted_iota(jnp.int32, held.shape, 1)
    shift = (y - z) & 15
    stays = shift == 0
    most = jnp.where(stays, RANKS, main_slots(shift))
    real = y < N_Z
    left = jnp.where(stays, 3, jnp.clip(most - held, 0, 3)) << (2 * (y & 7))
    low = jnp.sum(jnp.where(y < 8, left, 0), axis=1, keepdims=True)
    high = jnp.sum(jnp.where((y >= 8) & real, left, 0), axis=1, keepdims=True)
    over = jnp.max(jnp.where(real & (held > RANKS), 1, 0), axis=1, keepdims=True)
    extra = jnp.where(real, jnp.maximum(jnp.minimum(held, RANKS) - most, 0), 0)
    extra = jnp.where(y == LOW, low, jnp.where(y == HIGH, high, jnp.where(y == OVER, over, extra)))
    excess_v[...] = extra
    copies = [
        pltpu.make_async_copy(a, b, sems.at[i])
        for i, (a, b) in enumerate(
            ((count_v, count), (excess_v, excess), (tile_v, tile), (slot_v, slot))
        )
    ]
    copies[0].start()
    copies[1].start()

    def add_rank(i, rank):
        other = lists_ref[pl.ds(i, 1), :] >> 3
        return rank + jnp.where((other == source) & (rows > i), 1, 0)

    rank = lax.fori_loop(0, HELD, add_rank, jnp.zeros((HELD, LANES), jnp.int32), unroll=8)
    here = lanes == me
    column_source = jnp.sum(jnp.where(here, source, 0), axis=1, keepdims=True)
    column_rank = jnp.sum(jnp.where(here, rank, 0), axis=1, keepdims=True)
    mine = jnp.where(source == me, rank, -1)
    taken = jnp.where(column_source == lanes, column_rank, -1)
    for i in range(RANKS):
        tile_v[pl.ds(i, 1), :] = total(jnp.where(mine == i, local, 0))
        slot_v[pl.ds(i, 1), :] = total(jnp.where(taken == i, position, 0))
    copies[2].start()
    copies[3].start()
    for i in range(AT_BAD):
        table[i] = 0
    for i in range(N_Z):
        relay_free[i] = jnp.int32(relay_fields(i))
    for copy in copies:
        copy.wait()

    def open_row(z):
        def open_pair(y):
            shift = (y - z) & 15
            most = jnp.where(shift == 0, RANKS, main_slots(shift))
            direct[z * N_Z + y] = jnp.minimum(count[z, y], most)

        for y in range(N_Z):
            open_pair(y)

    repeat(0, N_Z, open_row)
    my_bit = jnp.int32(1) << (2 * me)

    def record(z, y, bit, rank, free, relay, main):
        @pl.when((z == me) | (bit == my_bit) | (y == me))
        def _():
            m = field_index(bit)
            own = jnp.where(main >= 0, main, count[z, m] + field_value(free, bit) - 1)
            main_at = main_offset((m - z) & 15) + own
            extra_at = relay_offset((y - m) & 15) + field_value(relay, bit) - 1

            @pl.when((z == me) & (m != z))
            def _():
                table[AT_MAIN + main_at] = tile[rank, y]

            @pl.when(m == me)
            def _():
                table[AT_EXTRA + extra_at] = jnp.where(m == z, tile[rank, y], HELD + main_at)

            @pl.when(y == me)
            def _():
                table[AT_FINAL + slot[rank, z]] = HELD + MAIN + extra_at

    def place_row(z, bad):
        own = jnp.int32(1) << (2 * z)

        def take(free, bit):
            return free - jnp.where(bit == own, 0, bit)

        def place_pair(i, carry):
            y = (i + z) & 15
            most = main_slots(i)

            def place_one(e, carry):
                free, bad = carry
                relay = relay_free[y]
                open_ = filled(free) & filled(relay)

                def simple():
                    late = open_ & (jnp.int32(-1) << (2 * ((y + 8) & 15)))
                    chosen = jnp.where(late != 0, late, open_)
                    bit = chosen & -chosen
                    record(z, y, bit, most + e, free, relay, jnp.int32(-1))
                    relay_free[y] = relay - bit
                    return take(free, bit), bad

                def swap():
                    def look(m, carry):
                        free, done = carry
                        bit = jnp.int32(1) << (2 * m)
                        relay_m = relay_free[m]
                        other = filled(free) & filled(relay_m)
                        straight = direct[z * N_Z + m]
                        fits = (
                            (done == 0)
                            & (m != z)
                            & (m != y)
                            & ((filled(relay) & bit) != 0)
                            & (straight > 0)
                            & (other != 0)
                        )

                        def do():
                            instead = other & -other
                            direct[z * N_Z + m] = straight - 1
                            record(z, m, instead, straight - 1, free, relay_m, jnp.int32(-1))
                            record(z, y, bit, most + e, free, relay, straight - 1)
                            relay_free[m] = relay_m - instead
                            relay_free[y] = relay - bit
                            return take(free, instead), jnp.int32(1)

                        return lax.cond(fits, do, lambda: (free, done))

                    free_, done = lax.fori_loop(0, N_Z, look, (free, jnp.int32(0)))
                    return free_, bad | (1 - done)

                return lax.cond(open_ != 0, simple, swap)

            return lax.fori_loop(0, excess[z, y], place_one, carry)

        free = excess[z, LOW] | (excess[z, HIGH] << 16)
        free, bad = lax.fori_loop(1, N_Z, place_pair, (free, bad | excess[z, OVER]))
        return bad

    table[AT_BAD] = lax.fori_loop(0, N_Z, place_row, jnp.int32(0))

    def straight(other):
        shift_out = (other - me) & 15
        shift_in = (me - other) & 15

        @pl.when(shift_out != 0)
        def _():
            first_out = AT_MAIN + main_offset(shift_out)
            first_in = HELD + main_offset(shift_in)

            def out(r):
                table[first_out + r] = tile[r, other]

            def arrive(r):
                table[AT_FINAL + slot[r, other]] = first_in + r

            repeat(0, direct[me * N_Z + other], out)
            repeat(0, direct[other * N_Z + me], arrive)

        @pl.when(shift_out == 0)
        def _():
            def keep(r):
                table[AT_FINAL + slot[r, me]] = tile[r, me]

            repeat(0, direct[me * N_Z + me], keep)

    repeat(0, N_Z, straight)


def route(lists):
    smem = pltpu.SMEM
    square = smem((N_Z, LANES), jnp.int32)
    square_v = pltpu.VMEM((N_Z, LANES), jnp.int32)
    return pl.pallas_call(
        route_kernel,
        out_shape=jax.ShapeDtypeStruct((TABLE,), jnp.int32),
        in_specs=[pl.BlockSpec(memory_space=pltpu.VMEM)],
        out_specs=pl.BlockSpec(memory_space=smem),
        scratch_shapes=[square_v] * 4
        + [square] * 4
        + [smem((PAIRS,), jnp.int32), smem((N_Z,), jnp.int32), pltpu.SemaphoreType.DMA((4,))],
        name="route",
    )(lists)


def exchange_kernel(
    table, held_q, conv_ref, k_ref, v_ref, q_out, k_out, v_out, rows_out, halo_out, *scratch
):
    z, row, ctx = place()
    repeat(1, PLANE, lambda k: signal(plane_peer(z, row, ctx, k)[2]))
    repeat(0, SHIFTS, lambda j: signal(z_peer(z, row, ctx, j)))
    pl.semaphore_wait(pltpu.get_barrier_semaphore(), PLANE - 1 + SHIFTS)
    held = (held_q,) + scratch[:3]
    main_staged, main_got, extra_staged, extra_got, staged = (
        scratch[3 + 4 * i : 7 + 4 * i] for i in range(5)
    )
    sems, halo_sems = scratch[23:]
    outs = (q_out, rows_out, k_out, v_out)
    pieces = (None, conv_piece(conv_ref), head_piece(k_ref), head_piece(v_ref))
    spread = [None] + [
        Spread(pieces[i], held[i], sems.at[0, i], sems.at[1, i]) for i in range(1, 4)
    ]
    main = [
        Along(MAIN_GROUPS, main_staged[i], main_got[i], sems.at[2, i], sems.at[3, i])
        for i in range(4)
    ]
    extra = [
        Along(EXTRA_GROUPS, extra_staged[i], extra_got[i], sems.at[4, i], sems.at[5, i])
        for i in range(4)
    ]

    def start_main(i):
        if i:
            spread[i].arrived()
        stage_main(table, held[i], main_staged[i])
        main[i].start()

    def start_extra(i):
        main[i].arrived()
        stage_extra(table, held[i], main_got[i], extra_staged[i])
        extra[i].start()

    def head_copy(i, k):
        to = (row + k) % PLANE_DP
        return remote(
            staged[i].at[pl.ds(to * 16, 16)],
            outs[i].at[:, row],
            sems.at[6, i],
            sems.at[7, i],
            (z * PLANE_DP + to, ctx),
        )

    channels = pl.ds(pl.multiple_of(row * WIDE, LANES), WIDE)

    def part(to_row, to_ctx):
        return staged[1].at[pl.ds(to_row * 16 + to_ctx * TILES_DEV, TILES_DEV)]

    def conv_copy(k):
        to_row, to_ctx, device = plane_peer(z, row, ctx, k)
        return remote(
            part(to_row, to_ctx), rows_out.at[:, ctx, :, channels], sems.at[6, 1], sems.at[7, 1], device
        )

    def halo(side, act):
        step, tile = (1, 1) if side == 0 else (-1, 0)

        def one(k):
            to_row = k // (N_CTX - 1)
            column = k % (N_CTX - 1) + (0 if side == 0 else 1)
            target = column + step
            src = staged[1].at[to_row * 16 + column * TILES_DEV + tile]
            dst = halo_out.at[side, :, channels]
            is_own = (to_row == row) & (target == ctx)

            @pl.when(is_own)
            def _():
                if act == "start":
                    pltpu.make_async_copy(src, dst, halo_sems.at[side]).start()

            @pl.when(jnp.logical_not(is_own))
            def _():
                far = remote(
                    src, dst, halo_sems.at[2], halo_sems.at[side], (z * PLANE_DP + to_row, target)
                )
                if act == "start":
                    far.start()
                else:
                    far.wait_send()

        @pl.when(ctx == (N_CTX - 1 if side == 0 else 0))
        def _():
            repeat(0, PLANE_DP * (N_CTX - 1), one)

    def start_final(i):
        extra[i].arrived()
        stage_final(table, held[i], main_got[i], extra_got[i], staged[i])
        if i == 1:
            repeat(1, PLANE, lambda k: conv_copy(k).start())
            pltpu.make_async_copy(
                part(row, ctx), rows_out.at[:, ctx, :, channels], sems.at[7, 1]
            ).start()
            halo(0, "start")
            halo(1, "start")
        else:
            repeat(1, PLANE_DP, lambda k: head_copy(i, k).start())
            pltpu.make_async_copy(
                staged[i].at[pl.ds(row * 16, 16)], outs[i].at[:, row], sems.at[7, i]
            ).start()

    spread[1].start()
    start_main(0)
    spread[2].start()
    start_main(1)
    spread[3].start()
    start_extra(0)
    start_main(2)
    start_extra(1)
    start_final(0)
    start_main(3)
    start_extra(2)
    start_final(1)
    start_extra(3)
    start_final(2)
    start_final(3)
    halo(0, "sent")
    halo(1, "sent")
    repeat(1, PLANE, lambda k: conv_copy(k).wait_send())
    for i in range(4):
        if i:
            spread[i].sent()
        main[i].sent()
        extra[i].sent()
        if i != 1:
            repeat(1, PLANE_DP, lambda k: head_copy(i, k).wait_send())
        await_all(outs[i], sems.at[7, i])

    @pl.when(ctx > 0)
    def _():
        await_all(halo_out.at[0], halo_sems.at[0])

    @pl.when(ctx < N_CTX - 1)
    def _():
        await_all(halo_out.at[1], halo_sems.at[1])


def exchange(table, held_q, conv, k, v):
    unit = (SEG_UNIT, LANES)
    conv_unit = (16, WIDE)
    kind = held_q.dtype

    def buffers(count):
        return [pltpu.VMEM((count,) + (conv_unit if i == 1 else unit), kind) for i in range(4)]

    heads = jax.ShapeDtypeStruct((N_CTX * TILES_DEV, PLANE_DP) + unit, kind)
    return pl.pallas_call(
        exchange_kernel,
        out_shape=(
            heads,
            heads,
            heads,
            jax.ShapeDtypeStruct((TILES_DEV, N_CTX, 16, CHANNELS), kind),
            jax.ShapeDtypeStruct((2, 16, CHANNELS), kind),
        ),
        in_specs=[pl.BlockSpec(memory_space=pltpu.SMEM), pl.BlockSpec(memory_space=pltpu.VMEM)]
        + [pl.BlockSpec(memory_space=pl.ANY)] * 3,
        out_specs=[pl.BlockSpec(memory_space=pl.ANY)] * 5,
        scratch_shapes=buffers(HELD)[1:]
        + buffers(MAIN)
        + buffers(MAIN)
        + buffers(EXTRA)
        + buffers(EXTRA)
        + buffers(HELD)
        + [pltpu.SemaphoreType.DMA((8, 4)), pltpu.SemaphoreType.DMA((3,))],
        compiler_params=pltpu.CompilerParams(
            collective_id=1, has_side_effects=True, vmem_limit_bytes=40 * 2**20
        ),
        name="exchange",
    )(table, held_q, conv, k, v)


def mix_kernel(mix_ref, heads_out, send, recv):
    z, row, ctx = place()
    dp = z * PLANE_DP + row
    repeat(1, N_CTX, lambda k: signal((dp, (ctx + k) % N_CTX)))
    pl.semaphore_wait(pltpu.get_barrier_semaphore(), N_CTX - 1)
    mixed = heads_out.at[:, pl.ds(pl.multiple_of(ctx * LANES, LANES), LANES)]

    def copy(k):
        to = (ctx + k) % N_CTX
        return remote(mix_ref.at[to], mixed, send, recv, (dp, to))

    repeat(1, N_CTX, lambda k: copy(k).start())
    pltpu.make_async_copy(mix_ref.at[ctx], mixed, recv).start()
    repeat(1, N_CTX, lambda k: copy(k).wait_send())
    await_all(heads_out, recv)


def to_frames(mix):
    return pl.pallas_call(
        mix_kernel,
        out_shape=jax.ShapeDtypeStruct((COLUMN, N_CTX * LANES), mix.dtype),
        in_specs=[pl.BlockSpec(memory_space=pl.ANY)],
        out_specs=pl.BlockSpec(memory_space=pl.ANY),
        scratch_shapes=[pltpu.SemaphoreType.DMA, pltpu.SemaphoreType.DMA],
        compiler_params=pltpu.CompilerParams(collective_id=2, has_side_effects=True),
        name="to_frames",
    )(mix)


def attend_kernel(len_ref, q_ref, k_ref, v_ref, out_ref):
    block = pl.program_id(0)
    ends = [len_ref[0, 0]]
    for i in range(1, 4):
        ends.append(ends[-1] + len_ref[0, i])
    first = block * UNITS
    last = first + UNITS - 1
    low = jnp.int32(0)
    high = jnp.int32(FRAMES // SEG_UNIT)
    for end in ends:
        low = jnp.where(end <= first, jnp.maximum(low, end), low)
        high = jnp.where(end > last, jnp.minimum(high, end), high)
    per_key = KBLOCK // SEG_UNIT
    low_block = low // per_key
    high_block = (high + per_key - 1) // per_key

    def segment(unit):
        seg = jnp.zeros(unit.shape, jnp.int32)
        for end in ends[:3]:
            seg = seg + (unit >= end).astype(jnp.int32)
        return seg

    queries = q_ref[...] * 0.125
    lane = lax.broadcasted_iota(jnp.int32, (QBLOCK, LANES), 1)
    zero = jnp.zeros_like(queries)
    both = jnp.concatenate(
        [jnp.where(lane < HEAD_DIM, queries, zero), jnp.where(lane < HEAD_DIM, zero, queries)], axis=0
    )
    row = lax.broadcasted_iota(jnp.int32, (2 * QBLOCK, 1), 0)
    row_seg = segment(first + lax.rem(row, QBLOCK) // SEG_UNIT)
    def step(index, carry):
        top, total, mixed = carry
        part = pl.ds(pl.multiple_of(index * KBLOCK, KBLOCK), KBLOCK)
        keys = k_ref[part, :]
        values = v_ref[part, :]
        scores = lax.dot_general(
            both, keys, (((1,), (1,)), ((), ())), preferred_element_type=jnp.float32
        )
        col = lax.broadcasted_iota(jnp.int32, (1, KBLOCK), 1)
        col_seg = segment(index * per_key + col // SEG_UNIT)
        scores = jnp.where(row_seg == col_seg, scores, -2e30)
        new_top = jnp.maximum(top, jnp.max(scores, axis=1, keepdims=True))
        weights = jnp.exp(scores - new_top)
        scale = jnp.exp(top - new_top)
        total = total * scale + jnp.sum(weights, axis=1, keepdims=True)
        mixed = mixed * scale + jnp.dot(
            weights.astype(jnp.bfloat16), values, preferred_element_type=jnp.float32
        )
        return new_top, total, mixed

    top, total, mixed = lax.fori_loop(
        low_block,
        high_block,
        step,
        (
            jnp.full((2 * QBLOCK, 1), -1e30, jnp.float32),
            jnp.zeros((2 * QBLOCK, 1), jnp.float32),
            jnp.zeros((2 * QBLOCK, LANES), jnp.float32),
        ),
    )
    mixed = mixed / total
    out_ref[0] = jnp.where(lane < HEAD_DIM, mixed[:QBLOCK], mixed[QBLOCK:]).astype(jnp.bfloat16)


def attend(lengths, q, k, v):
    blocks = FRAMES // QBLOCK
    return pl.pallas_call(
        attend_kernel,
        grid_spec=pltpu.PrefetchScalarGridSpec(
            num_scalar_prefetch=1,
            grid=(blocks,),
            in_specs=[
                pl.BlockSpec((QBLOCK, LANES), lambda i, lens: (i, 0)),
                pl.BlockSpec((FRAMES, LANES), lambda i, lens: (0, 0)),
                pl.BlockSpec((FRAMES, LANES), lambda i, lens: (0, 0)),
            ],
            out_specs=pl.BlockSpec((1, QBLOCK, LANES), lambda i, lens: (i, 0, 0)),
        ),
        out_shape=jax.ShapeDtypeStruct((blocks, QBLOCK, LANES), jnp.bfloat16),
        compiler_params=pltpu.CompilerParams(vmem_limit_bytes=48 * 2**20),
        cost_estimate=pl.CostEstimate(
            flops=8 * FRAMES * FRAMES * LANES, bytes_accessed=2**21, transcendentals=2 * FRAMES * FRAMES
        ),
        name="attend",
    )(lengths, q, k, v)


def segment_of(positions, seg_ends):
    unit_index = positions // SEG_UNIT
    return jnp.sum((seg_ends[None, :] <= unit_index[:, None]).astype(jnp.int32), axis=1)


def convolve(signal, halo, lengths, conv_taps, norm_scale, norm_shift):
    seg_ends = jnp.cumsum(lengths[0])
    column = lax.axis_index("ctx")
    half_width = (KERNEL - 1) // 2
    query_seg = segment_of(column * COLUMN + jnp.arange(COLUMN, dtype=jnp.int32), seg_ends)
    before = jnp.where(column > 0, halo[0], 0)
    after = jnp.where(column < N_CTX - 1, halo[1], 0)
    padded = jnp.concatenate([before[1:], signal, after[:half_width]], axis=0).astype(jnp.float32)
    padded_seg = segment_of(
        column * COLUMN - half_width + jnp.arange(COLUMN + 2 * half_width, dtype=jnp.int32), seg_ends
    )
    conv_sum = jnp.zeros(signal.shape, jnp.float32)
    for tap in range(KERNEL):
        same_seg = (padded_seg[tap : tap + COLUMN] == query_seg)[:, None]
        conv_sum = conv_sum + jnp.where(same_seg, conv_taps[tap] * padded[tap : tap + COLUMN], 0.0)
    return jax.nn.silu(norm_scale * conv_sum + norm_shift).astype(jnp.bfloat16)


def share_of(dp, ctx):
    return (dp // 8) * 8 + lax.rem(dp + ctx, 8)


def entry(count, device):
    barrier = pltpu.get_barrier_semaphore()

    def one(k, carry):
        pl.semaphore_signal(barrier, inc=1, device_id=device(k), device_id_type=MESH)
        return carry

    lax.fori_loop(0, count, one, 0)
    pl.semaphore_wait(barrier, count)


def all_arrived(ref, sem):
    pltpu.make_async_copy(ref, ref, sem).wait()


def general_spread_kernel(x_ref, out_ref, send_sem, recv_sem):
    dp, ctx = lax.axis_index("dp"), lax.axis_index("ctx")
    entry(N_DP - 1, lambda k: (lax.rem(dp + 1 + k, N_DP), ctx))

    def copy(k):
        peer = lax.rem(dp + k, N_DP)
        return pltpu.make_async_remote_copy(
            src_ref=x_ref.at[share_of(peer, ctx)],
            dst_ref=out_ref.at[dp],
            send_sem=send_sem,
            recv_sem=recv_sem,
            device_id=(peer, ctx),
            device_id_type=MESH,
        )

    own = pltpu.make_async_copy(x_ref.at[share_of(dp, ctx)], out_ref.at[dp], recv_sem)

    def start(k, carry):
        copy(k).start()
        return carry

    def sent(k, carry):
        copy(k).wait_send()
        return carry

    lax.fori_loop(1, N_DP, start, 0)
    own.start()
    lax.fori_loop(1, N_DP, sent, 0)
    all_arrived(out_ref, recv_sem)


def general_spread(x):
    return pl.pallas_call(
        general_spread_kernel,
        out_shape=jax.ShapeDtypeStruct(x.shape, x.dtype),
        in_specs=[pl.BlockSpec(memory_space=pl.ANY)],
        out_specs=pl.BlockSpec(memory_space=pl.ANY),
        scratch_shapes=[pltpu.SemaphoreType.DMA, pltpu.SemaphoreType.DMA],
        compiler_params=pltpu.CompilerParams(collective_id=3, has_side_effects=True),
        name="general_spread",
    )(x)


def general_heads_kernel(x_ref, out_ref, send_sem, recv_sem):
    dp, ctx = lax.axis_index("dp"), lax.axis_index("ctx")
    share = share_of(dp, ctx)
    group, column = share // 8, lax.rem(share, 8)

    def sender(k):
        other = k // 8
        return (lax.rem(k, 8) * 8 + lax.rem(ctx - other + 8, 8), other)

    barrier = pltpu.get_barrier_semaphore()

    def greet(k, carry):
        peer = sender(k)

        @pl.when(jnp.logical_or(peer[0] != dp, peer[1] != ctx))
        def _():
            pl.semaphore_signal(barrier, inc=1, device_id=peer, device_id_type=MESH)

        return carry

    lax.fori_loop(0, N_DP, greet, 0)
    is_own = column == ctx

    @pl.when(is_own)
    def _():
        pl.semaphore_wait(barrier, N_DP - 1)

    @pl.when(jnp.logical_not(is_own))
    def _():
        pl.semaphore_wait(barrier, N_DP)

    def copy(k):
        peer = lax.rem(dp + k, N_DP)
        return pltpu.make_async_remote_copy(
            src_ref=x_ref.at[peer],
            dst_ref=out_ref.at[pl.ds(ctx * TILES_DEV, TILES_DEV), group],
            send_sem=send_sem,
            recv_sem=recv_sem,
            device_id=(peer, column),
            device_id_type=MESH,
        )

    def start(k, carry):
        copy(k).start()
        return carry

    def sent(k, carry):
        copy(k).wait_send()
        return carry

    lax.fori_loop(1, N_DP, start, 0)

    @pl.when(is_own)
    def _():
        pltpu.make_async_copy(
            x_ref.at[dp], out_ref.at[pl.ds(ctx * TILES_DEV, TILES_DEV), group], recv_sem
        ).start()

    @pl.when(jnp.logical_not(is_own))
    def _():
        copy(0).start()
        copy(0).wait_send()

    lax.fori_loop(1, N_DP, sent, 0)
    all_arrived(out_ref, recv_sem)


def general_heads(x):
    return pl.pallas_call(
        general_heads_kernel,
        out_shape=jax.ShapeDtypeStruct((N_CTX * TILES_DEV, TILE // ROWS, 3, ROWS, LANES), x.dtype),
        in_specs=[pl.BlockSpec(memory_space=pl.ANY)],
        out_specs=pl.BlockSpec(memory_space=pl.ANY),
        scratch_shapes=[pltpu.SemaphoreType.DMA, pltpu.SemaphoreType.DMA],
        compiler_params=pltpu.CompilerParams(collective_id=4, has_side_effects=True),
        name="general_heads",
    )(x)


def general_deliver_kernel(x_ref, mix_ref, out_ref, heads_ref, send_sem, recv_sem, mix_send, mix_recv):
    dp, ctx = lax.axis_index("dp"), lax.axis_index("ctx")
    share = share_of(dp, ctx)
    barrier = pltpu.get_barrier_semaphore()

    def greet_dp(k, carry):
        pl.semaphore_signal(
            barrier, inc=1, device_id=(lax.rem(dp + k, N_DP), ctx), device_id_type=MESH
        )
        return carry

    def greet_ctx(k, carry):
        pl.semaphore_signal(
            barrier, inc=1, device_id=(dp, lax.rem(ctx + k, N_CTX)), device_id_type=MESH
        )
        return carry

    lax.fori_loop(1, N_DP, greet_dp, 0)
    lax.fori_loop(1, N_CTX, greet_ctx, 0)
    pl.semaphore_wait(barrier, N_DP - 1 + N_CTX - 1)

    def mix_copy(k):
        peer = lax.rem(ctx + k, N_CTX)
        return pltpu.make_async_remote_copy(
            src_ref=mix_ref.at[peer],
            dst_ref=heads_ref.at[:, pl.ds(pl.multiple_of(ctx * LANES, LANES), LANES)],
            send_sem=mix_send,
            recv_sem=mix_recv,
            device_id=(dp, peer),
            device_id_type=MESH,
        )

    def copy(k):
        peer = lax.rem(dp + k, N_DP)
        return pltpu.make_async_remote_copy(
            src_ref=x_ref.at[peer],
            dst_ref=out_ref.at[share],
            send_sem=send_sem,
            recv_sem=recv_sem,
            device_id=(peer, ctx),
            device_id_type=MESH,
        )

    def start(k, carry):
        copy(k).start()
        return carry

    def sent(k, carry):
        copy(k).wait_send()
        return carry

    def mix_start(k, carry):
        mix_copy(k).start()
        return carry

    def mix_sent(k, carry):
        mix_copy(k).wait_send()
        return carry

    lax.fori_loop(1, N_DP, start, 0)
    lax.fori_loop(1, N_CTX, mix_start, 0)
    pltpu.make_async_copy(x_ref.at[dp], out_ref.at[share], recv_sem).start()
    pltpu.make_async_copy(
        mix_ref.at[ctx],
        heads_ref.at[:, pl.ds(pl.multiple_of(ctx * LANES, LANES), LANES)],
        mix_recv,
    ).start()
    lax.fori_loop(1, N_DP, sent, 0)
    lax.fori_loop(1, N_CTX, mix_sent, 0)
    all_arrived(out_ref, recv_sem)
    all_arrived(heads_ref, mix_recv)


def general_deliver(x, mix):
    rows = FRAMES // N_CTX
    return pl.pallas_call(
        general_deliver_kernel,
        out_shape=(
            jax.ShapeDtypeStruct(x.shape, x.dtype),
            jax.ShapeDtypeStruct((rows, N_CTX * LANES), x.dtype),
        ),
        in_specs=[pl.BlockSpec(memory_space=pl.ANY)] * 2,
        out_specs=[pl.BlockSpec(memory_space=pl.ANY)] * 2,
        scratch_shapes=[pltpu.SemaphoreType.DMA] * 4,
        compiler_params=pltpu.CompilerParams(collective_id=5, has_side_effects=True),
        name="general_deliver",
    )(x, mix)


def general_path(
    query_loader,
    key_loader,
    value_loader,
    conv_loader,
    slot_tile,
    lengths,
    conv_taps,
    norm_scale,
    norm_shift,
):
    qkv = jnp.stack([query_loader[0], key_loader[0], value_loader[0]])
    qkv = qkv.reshape(3, TILES_DEV, TILE // ROWS, ROWS, N_CTX, LANES)
    qkv = jnp.transpose(qkv, (2, 4, 1, 0, 3, 5)).reshape(N_DP, TILES_DEV * QKV, LANES)
    conv = conv_loader[0].reshape(TILES_DEV, N_DP, CONV_ROWS, LANES)
    conv = jnp.transpose(conv, (1, 0, 2, 3)).reshape(N_DP, TILES_DEV * CONV_ROWS, LANES)
    got = general_spread(jnp.concatenate([qkv, conv], axis=1))
    order = slot_tile[0]
    got_qkv = got[:, : TILES_DEV * QKV].reshape(N_DP * TILES_DEV, 3, ROWS, LANES)
    send_qkv = got_qkv[order].reshape(N_DP, TILES_DEV, 3, ROWS, LANES)
    got_conv = got[:, TILES_DEV * QKV :].reshape(N_DP * TILES_DEV, CONV_ROWS, LANES)
    send_conv = got_conv[order].reshape(N_DP, TILES_DEV * CONV_ROWS, LANES)
    heads = general_heads(send_qkv)
    flat = (FRAMES, LANES)
    mix = attend(lengths, *(heads[:, :, i].reshape(flat) for i in range(3)))
    signal, attention_out = general_deliver(send_conv, mix)
    signal = signal.reshape(N_DP, TILES_DEV, TILE // N_DP, CONV_ROWS // 2 * LANES)
    signal = jnp.transpose(signal, (1, 0, 2, 3)).reshape(TILES_DEV * TILE, CONV_ROWS // 2 * LANES)
    ends = N_CTX - 1
    halo = jnp.stack(
        [
            lax.ppermute(signal[COLUMN - 16 :], "ctx", [(i, i + 1) for i in range(ends)]),
            lax.ppermute(signal[:16], "ctx", [(i + 1, i) for i in range(ends)]),
        ]
    )
    conv_out = convolve(signal, halo, lengths, conv_taps, norm_scale, norm_shift)
    return attention_out[None], conv_out[None]


def on_device(*inputs):
    query, key, value, conv, slot_tile, lengths, conv_taps, norm_scale, norm_shift = inputs
    places = jnp.transpose(slot_tile[0].reshape(N_Z, 8))
    places = jnp.pad(places, ((0, 0), (0, LANES - N_Z)), constant_values=1 << 16)
    shape = (TILES_DEV, PLANE_DP, SEG_UNIT, HEADS * HEAD_DIM)
    held_q, lists = first(query.reshape(shape), places)
    table = route(lists.reshape(HELD, LANES))
    q, k, v, rows, halo = exchange(
        table,
        held_q,
        conv.reshape(TILES_DEV, N_CTX, 16, CHANNELS),
        key.reshape(shape),
        value.reshape(shape),
    )
    heads = (FRAMES, LANES)
    mix = attend(lengths, q.reshape(heads), k.reshape(heads), v.reshape(heads))
    attention_out = to_frames(mix)
    conv_out = convolve(
        rows.reshape(COLUMN, CHANNELS), halo, lengths, conv_taps, norm_scale, norm_shift
    )
    return lax.cond(
        table[AT_BAD] == 0,
        lambda: (attention_out[None], conv_out[None]),
        lambda: general_path(*inputs),
    )


def solution(mesh):
    return jax.shard_map(
        on_device,
        mesh=mesh,
        in_specs=(
            P("dp", "ctx", None),
            P("dp", "ctx", None),
            P("dp", "ctx", None),
            P("dp", "ctx", None),
            P("ctx", None),
            P("dp", None),
            P(),
            P(),
            P(),
        ),
        out_specs=(P("dp", "ctx", None), P("dp", "ctx", None)),
        check_vma=False,
    )
```

```python
import jax
import jax.numpy as jnp
from jax import lax
from jax.experimental import pallas as pl
from jax.experimental.pallas import tpu as pltpu
from jax.sharding import PartitionSpec as P

MESH = pl.DeviceIdType.MESH
HEADS = 16
HEAD_DIM = 64
CHANNELS = 1536
KERNEL = 31
TILE = 128
TILES_DEV = 2
SEG_UNIT = 32
FRAMES = 2048
COLUMN = 256
LANES = 128
N_DP = 64
N_CTX = 8
ROWS = 16
QKV = 3 * ROWS
CONV_ROWS = 24
QBLOCK = 256
KBLOCK = 256
UNITS = QBLOCK // SEG_UNIT

N_Z = 16
PLANE_DP = 4
PLANE = PLANE_DP * N_CTX
HELD = PLANE * TILES_DEV
SHIFTS = N_Z - 1
NEAR, NEAR_SLOTS, FAR_SLOTS = 6, 5, 4
RELAYS, RELAY_SLOTS = 10, 2
MAIN = NEAR * NEAR_SLOTS + (SHIFTS - NEAR) * FAR_SLOTS
EXTRA = RELAYS * RELAY_SLOTS
TABLE = 256
AT_MAIN, AT_EXTRA, AT_FINAL, AT_BAD = 0, 72, 96, 160
RANKS = 16
PAIRS = N_Z * N_Z
LIST = 2304
FIELDS = 0x55555555


def shift_of(j):
    half = j // 2
    return jnp.where(j % 2 == 0, half + 1, N_Z - 1 - half)


def order_of(shift):
    return jnp.where(shift <= N_Z // 2, 2 * (shift - 1), 2 * (N_Z - shift) - 1)


def main_slots(shift):
    return jnp.where(order_of(shift) < NEAR, NEAR_SLOTS, FAR_SLOTS)


def main_offset(shift):
    j = order_of(shift)
    return jnp.where(j < NEAR, NEAR_SLOTS * j, NEAR * NEAR_SLOTS + FAR_SLOTS * (j - NEAR))


def relay_offset(shift):
    return RELAY_SLOTS * order_of(shift)


def place():
    dp, ctx = lax.axis_index("dp"), lax.axis_index("ctx")
    return dp // PLANE_DP, dp % PLANE_DP, ctx


def plane_peer(z, row, ctx, k):
    index = (row * N_CTX + ctx + k) % PLANE
    return index // N_CTX, index % N_CTX, (z * PLANE_DP + index // N_CTX, index % N_CTX)


def z_peer(z, row, ctx, j):
    return ((z + shift_of(j)) % N_Z * PLANE_DP + row, ctx)


def repeat(first, last, body):
    def one(k, carry):
        body(k)
        return carry

    lax.fori_loop(first, last, one, 0)


def remote(src, dst, send, recv, device):
    return pltpu.make_async_remote_copy(
        src_ref=src, dst_ref=dst, send_sem=send, recv_sem=recv, device_id=device, device_id_type=MESH
    )


def await_all(ref, sem):
    pltpu.make_async_copy(ref, ref, sem).wait()


def signal(device):
    pl.semaphore_signal(pltpu.get_barrier_semaphore(), inc=1, device_id=device, device_id_type=MESH)


class Spread:
    def __init__(self, piece, held, send, recv):
        z, row, ctx = place()
        mine = pl.ds((ctx * PLANE_DP + row) * TILES_DEV, TILES_DEV)

        def copy(k):
            to_row, to_ctx, device = plane_peer(z, row, ctx, k)
            return remote(piece(to_row, to_ctx), held.at[mine], send, recv, device)

        self.copy, self.held, self.recv = copy, held, recv
        self.own = pltpu.make_async_copy(piece(row, ctx), held.at[mine], recv)

    def start(self):
        repeat(1, PLANE, lambda k: self.copy(k).start())
        self.own.start()

    def arrived(self):
        await_all(self.held, self.recv)

    def sent(self):
        repeat(1, PLANE, lambda k: self.copy(k).wait_send())


class Along:
    def __init__(self, groups, staged, got, send, recv):
        z, row, ctx = place()
        self.staged, self.got, self.send, self.recv = staged, got, send, recv

        def copy(j, offset, slots):
            part = pl.ds(offset, slots)
            return remote(staged.at[part], got.at[part], send, recv, z_peer(z, row, ctx, j))

        self.copy, self.groups = copy, groups

    def start(self):
        for first, last, base, slots in self.groups:
            repeat(
                first,
                last,
                lambda j: self.copy(j, base + (j - first) * slots, slots).start(),
            )

    def arrived(self):
        await_all(self.got, self.recv)

    def sent(self):
        await_all(self.staged, self.send)


MAIN_GROUPS = ((0, NEAR, 0, NEAR_SLOTS), (NEAR, SHIFTS, NEAR * NEAR_SLOTS, FAR_SLOTS))
EXTRA_GROUPS = ((0, RELAYS, 0, RELAY_SLOTS),)


def stage_main(table, held, staged):
    def one(i):
        staged[i] = held[table[AT_MAIN + i]]

    repeat(0, MAIN, one)


def stage_extra(table, held, got, staged):
    def one(i):
        code = table[AT_EXTRA + i]
        staged[i] = jnp.where(
            code < HELD, held[jnp.minimum(code, HELD - 1)], got[jnp.clip(code - HELD, 0, MAIN - 1)]
        )

    repeat(0, EXTRA, one)


def stage_final(table, held, got, more, staged):
    def one(i):
        code = table[AT_FINAL + i]
        first = held[jnp.minimum(code, HELD - 1)]
        second = got[jnp.clip(code - HELD, 0, MAIN - 1)]
        third = more[jnp.clip(code - HELD - MAIN, 0, EXTRA - 1)]
        staged[i] = jnp.where(code < HELD, first, jnp.where(code < HELD + MAIN, second, third))

    repeat(0, HELD, one)


def head_piece(ref):
    return lambda row, ctx: ref.at[:, row, :, pl.ds(pl.multiple_of(ctx * LANES, LANES), LANES)]


WIDE = CHANNELS // PLANE_DP


def conv_piece(ref):
    return lambda row, ctx: ref.at[:, ctx, :, pl.ds(pl.multiple_of(row * WIDE, LANES), WIDE)]


def first_kernel(q_ref, list_ref, held_ref, lists_ref, send, recv, list_send, list_recv):
    z, row, ctx = place()
    repeat(1, PLANE, lambda k: signal(plane_peer(z, row, ctx, k)[2]))
    pl.semaphore_wait(pltpu.get_barrier_semaphore(), PLANE - 1)

    def tell(k):
        device = (z * PLANE_DP + row, (ctx + k) % N_CTX)
        return remote(list_ref, lists_ref.at[ctx], list_send, list_recv, device)

    repeat(1, N_CTX, lambda k: tell(k).start())
    pltpu.make_async_copy(list_ref, lists_ref.at[ctx], list_recv).start()
    spread = Spread(head_piece(q_ref), held_ref, send, recv)
    spread.start()
    repeat(1, N_CTX, lambda k: tell(k).wait_send())
    await_all(lists_ref, list_recv)
    spread.arrived()
    spread.sent()


def first(q, own_list):
    return pl.pallas_call(
        first_kernel,
        out_shape=(
            jax.ShapeDtypeStruct((HELD, SEG_UNIT, LANES), q.dtype),
            jax.ShapeDtypeStruct((N_CTX,) + own_list.shape, own_list.dtype),
        ),
        in_specs=[pl.BlockSpec(memory_space=pl.ANY)] * 2,
        out_specs=[pl.BlockSpec(memory_space=pl.ANY)] * 2,
        scratch_shapes=[pltpu.SemaphoreType.DMA] * 4,
        compiler_params=pltpu.CompilerParams(collective_id=0, has_side_effects=True),
        name="spread_queries",
    )(q, own_list)


def filled(fields):
    return (fields | (fields >> 1)) & FIELDS


def field_index(bit):
    def step(mask, worth):
        return jnp.where((bit & mask) != 0, worth, 0)

    high = jnp.where(bit >= (1 << 16), 8, 0)
    return high + step(0x7F00FF00, 4) + step(0x70F0F0F0, 2) + step(0x4CCCCCCC & FIELDS, 1)


def field_value(fields, bit):
    return jnp.where((fields & bit) != 0, 1, 0) + jnp.where((fields & (bit << 1)) != 0, 2, 0)


def relay_fields(y):
    fields = 0
    for m in range(N_Z):
        shift = (y - m) % N_Z
        order = 2 * (shift - 1) if shift <= N_Z // 2 else 2 * (N_Z - shift) - 1
        if shift and order < RELAYS:
            fields |= RELAY_SLOTS << (2 * m)
    return fields - (1 << 32) if fields >= 1 << 31 else fields


LOW, HIGH, OVER = N_Z, N_Z + 1, N_Z + 2


def route_kernel(
    lists_ref,
    table,
    count_v,
    excess_v,
    tile_v,
    slot_v,
    count,
    excess,
    tile,
    slot,
    direct,
    relay_free,
    sems,
):
    me = lax.axis_index("dp") // PLANE_DP
    tiles = lists_ref[...]
    source = tiles >> 3
    rows = lax.broadcasted_iota(jnp.int32, (HELD, LANES), 0)
    lanes = lax.broadcasted_iota(jnp.int32, (HELD, LANES), 1)
    local = (rows & ~7) + (tiles & 7)
    position = ((rows & 7) >> 1) * 16 + (rows >> 3) * 2 + (rows & 1)

    def total(values):
        return jnp.sum(values, axis=0, keepdims=True, dtype=jnp.int32)

    for i in range(N_Z):
        count_v[pl.ds(i, 1), :] = total(jnp.where(source == i, 1, 0))
    held = count_v[...]
    z = lax.broadcasted_iota(jnp.int32, held.shape, 0)
    y = lax.broadcasted_iota(jnp.int32, held.shape, 1)
    shift = (y - z) & 15
    stays = shift == 0
    most = jnp.where(stays, RANKS, main_slots(shift))
    real = y < N_Z
    left = jnp.where(stays, 3, jnp.clip(most - held, 0, 3)) << (2 * (y & 7))
    low = jnp.sum(jnp.where(y < 8, left, 0), axis=1, keepdims=True)
    high = jnp.sum(jnp.where((y >= 8) & real, left, 0), axis=1, keepdims=True)
    over = jnp.max(jnp.where(real & (held > RANKS), 1, 0), axis=1, keepdims=True)
    extra = jnp.where(real, jnp.maximum(jnp.minimum(held, RANKS) - most, 0), 0)
    extra = jnp.where(y == LOW, low, jnp.where(y == HIGH, high, jnp.where(y == OVER, over, extra)))
    excess_v[...] = extra
    copies = [
        pltpu.make_async_copy(a, b, sems.at[i])
        for i, (a, b) in enumerate(
            ((count_v, count), (excess_v, excess), (tile_v, tile), (slot_v, slot))
        )
    ]
    copies[0].start()
    copies[1].start()

    def add_rank(i, rank):
        other = lists_ref[pl.ds(i, 1), :] >> 3
        return rank + jnp.where((other == source) & (rows > i), 1, 0)

    rank = lax.fori_loop(0, HELD, add_rank, jnp.zeros((HELD, LANES), jnp.int32), unroll=8)
    here = lanes == me
    column_source = jnp.sum(jnp.where(here, source, 0), axis=1, keepdims=True)
    column_rank = jnp.sum(jnp.where(here, rank, 0), axis=1, keepdims=True)
    mine = jnp.where(source == me, rank, -1)
    taken = jnp.where(column_source == lanes, column_rank, -1)
    for i in range(RANKS):
        tile_v[pl.ds(i, 1), :] = total(jnp.where(mine == i, local, 0))
        slot_v[pl.ds(i, 1), :] = total(jnp.where(taken == i, position, 0))
    copies[2].start()
    copies[3].start()
    for i in range(AT_BAD):
        table[i] = 0
    for i in range(N_Z):
        relay_free[i] = jnp.int32(relay_fields(i))
    for copy in copies:
        copy.wait()

    def open_row(z):
        def open_pair(y):
            shift = (y - z) & 15
            most = jnp.where(shift == 0, RANKS, main_slots(shift))
            direct[z * N_Z + y] = jnp.minimum(count[z, y], most)

        for y in range(N_Z):
            open_pair(y)

    repeat(0, N_Z, open_row)
    my_bit = jnp.int32(1) << (2 * me)

    def record(z, y, bit, rank, free, relay, main):
        @pl.when((z == me) | (bit == my_bit) | (y == me))
        def _():
            m = field_index(bit)
            own = jnp.where(main >= 0, main, count[z, m] + field_value(free, bit) - 1)
            main_at = main_offset((m - z) & 15) + own
            extra_at = relay_offset((y - m) & 15) + field_value(relay, bit) - 1

            @pl.when((z == me) & (m != z))
            def _():
                table[AT_MAIN + main_at] = tile[rank, y]

            @pl.when(m == me)
            def _():
                table[AT_EXTRA + extra_at] = jnp.where(m == z, tile[rank, y], HELD + main_at)

            @pl.when(y == me)
            def _():
                table[AT_FINAL + slot[rank, z]] = HELD + MAIN + extra_at

    def place_row(z, bad):
        own = jnp.int32(1) << (2 * z)

        def take(free, bit):
            return free - jnp.where(bit == own, 0, bit)

        def place_pair(i, carry):
            y = (i + z) & 15
            most = main_slots(i)

            def place_one(e, carry):
                free, bad = carry
                relay = relay_free[y]
                open_ = filled(free) & filled(relay)

                def simple():
                    late = open_ & (jnp.int32(-1) << (2 * ((y + 8) & 15)))
                    chosen = jnp.where(late != 0, late, open_)
                    bit = chosen & -chosen
                    record(z, y, bit, most + e, free, relay, jnp.int32(-1))
                    relay_free[y] = relay - bit
                    return take(free, bit), bad

                def swap():
                    def look(m, carry):
                        free, done = carry
                        bit = jnp.int32(1) << (2 * m)
                        relay_m = relay_free[m]
                        other = filled(free) & filled(relay_m)
                        straight = direct[z * N_Z + m]
                        fits = (
                            (done == 0)
                            & (m != z)
                            & (m != y)
                            & ((filled(relay) & bit) != 0)
                            & (straight > 0)
                            & (other != 0)
                        )

                        def do():
                            instead = other & -other
                            direct[z * N_Z + m] = straight - 1
                            record(z, m, instead, straight - 1, free, relay_m, jnp.int32(-1))
                            record(z, y, bit, most + e, free, relay, straight - 1)
                            relay_free[m] = relay_m - instead
                            relay_free[y] = relay - bit
                            return take(free, instead), jnp.int32(1)

                        return lax.cond(fits, do, lambda: (free, done))

                    free_, done = lax.fori_loop(0, N_Z, look, (free, jnp.int32(0)))
                    return free_, bad | (1 - done)

                return lax.cond(open_ != 0, simple, swap)

            return lax.fori_loop(0, excess[z, y], place_one, carry)

        free = excess[z, LOW] | (excess[z, HIGH] << 16)
        free, bad = lax.fori_loop(1, N_Z, place_pair, (free, bad | excess[z, OVER]))
        return bad

    table[AT_BAD] = lax.fori_loop(0, N_Z, place_row, jnp.int32(0))

    def straight(other):
        shift_out = (other - me) & 15
        shift_in = (me - other) & 15

        @pl.when(shift_out != 0)
        def _():
            first_out = AT_MAIN + main_offset(shift_out)
            first_in = HELD + main_offset(shift_in)

            def out(r):
                table[first_out + r] = tile[r, other]

            def arrive(r):
                table[AT_FINAL + slot[r, other]] = first_in + r

            repeat(0, direct[me * N_Z + other], out)
            repeat(0, direct[other * N_Z + me], arrive)

        @pl.when(shift_out == 0)
        def _():
            def keep(r):
                table[AT_FINAL + slot[r, me]] = tile[r, me]

            repeat(0, direct[me * N_Z + me], keep)

    repeat(0, N_Z, straight)


def route(lists):
    smem = pltpu.SMEM
    square = smem((N_Z, LANES), jnp.int32)
    square_v = pltpu.VMEM((N_Z, LANES), jnp.int32)
    return pl.pallas_call(
        route_kernel,
        out_shape=jax.ShapeDtypeStruct((TABLE,), jnp.int32),
        in_specs=[pl.BlockSpec(memory_space=pltpu.VMEM)],
        out_specs=pl.BlockSpec(memory_space=smem),
        scratch_shapes=[square_v] * 4
        + [square] * 4
        + [smem((PAIRS,), jnp.int32), smem((N_Z,), jnp.int32), pltpu.SemaphoreType.DMA((4,))],
        name="route",
    )(lists)


def exchange_kernel(
    table, held_q, conv_ref, k_ref, v_ref, q_out, k_out, v_out, rows_out, halo_out, *scratch
):
    z, row, ctx = place()
    repeat(1, PLANE, lambda k: signal(plane_peer(z, row, ctx, k)[2]))
    repeat(0, SHIFTS, lambda j: signal(z_peer(z, row, ctx, j)))
    pl.semaphore_wait(pltpu.get_barrier_semaphore(), PLANE - 1 + SHIFTS)
    held = (held_q,) + scratch[:3]
    main_staged, main_got, extra_staged, extra_got, staged = (
        scratch[3 + 4 * i : 7 + 4 * i] for i in range(5)
    )
    sems, halo_sems = scratch[23:]
    outs = (q_out, rows_out, k_out, v_out)
    pieces = (None, conv_piece(conv_ref), head_piece(k_ref), head_piece(v_ref))
    spread = [None] + [
        Spread(pieces[i], held[i], sems.at[0, i], sems.at[1, i]) for i in range(1, 4)
    ]
    main = [
        Along(MAIN_GROUPS, main_staged[i], main_got[i], sems.at[2, i], sems.at[3, i])
        for i in range(4)
    ]
    extra = [
        Along(EXTRA_GROUPS, extra_staged[i], extra_got[i], sems.at[4, i], sems.at[5, i])
        for i in range(4)
    ]

    def start_main(i):
        if i:
            spread[i].arrived()
        stage_main(table, held[i], main_staged[i])
        main[i].start()

    def start_extra(i):
        main[i].arrived()
        stage_extra(table, held[i], main_got[i], extra_staged[i])
        extra[i].start()

    def head_copy(i, k):
        to = (row + k) % PLANE_DP
        return remote(
            staged[i].at[pl.ds(to * 16, 16)],
            outs[i].at[:, row],
            sems.at[6, i],
            sems.at[7, i],
            (z * PLANE_DP + to, ctx),
        )

    channels = pl.ds(pl.multiple_of(row * WIDE, LANES), WIDE)

    def part(to_row, to_ctx):
        return staged[1].at[pl.ds(to_row * 16 + to_ctx * TILES_DEV, TILES_DEV)]

    def conv_copy(k):
        to_row, to_ctx, device = plane_peer(z, row, ctx, k)
        return remote(
            part(to_row, to_ctx), rows_out.at[:, ctx, :, channels], sems.at[6, 1], sems.at[7, 1], device
        )

    def halo(side, act):
        step, tile = (1, 1) if side == 0 else (-1, 0)

        def one(k):
            to_row = k // (N_CTX - 1)
            column = k % (N_CTX - 1) + (0 if side == 0 else 1)
            target = column + step
            src = staged[1].at[to_row * 16 + column * TILES_DEV + tile]
            dst = halo_out.at[side, :, channels]
            is_own = (to_row == row) & (target == ctx)

            @pl.when(is_own)
            def _():
                if act == "start":
                    pltpu.make_async_copy(src, dst, halo_sems.at[side]).start()

            @pl.when(jnp.logical_not(is_own))
            def _():
                far = remote(
                    src, dst, halo_sems.at[2], halo_sems.at[side], (z * PLANE_DP + to_row, target)
                )
                if act == "start":
                    far.start()
                else:
                    far.wait_send()

        @pl.when(ctx == (N_CTX - 1 if side == 0 else 0))
        def _():
            repeat(0, PLANE_DP * (N_CTX - 1), one)

    def start_final(i):
        extra[i].arrived()
        stage_final(table, held[i], main_got[i], extra_got[i], staged[i])
        if i == 1:
            repeat(1, PLANE, lambda k: conv_copy(k).start())
            pltpu.make_async_copy(
                part(row, ctx), rows_out.at[:, ctx, :, channels], sems.at[7, 1]
            ).start()
            halo(0, "start")
            halo(1, "start")
        else:
            repeat(1, PLANE_DP, lambda k: head_copy(i, k).start())
            pltpu.make_async_copy(
                staged[i].at[pl.ds(row * 16, 16)], outs[i].at[:, row], sems.at[7, i]
            ).start()

    spread[1].start()
    start_main(0)
    spread[2].start()
    start_main(1)
    spread[3].start()
    start_extra(0)
    start_main(2)
    start_extra(1)
    start_final(0)
    start_main(3)
    start_extra(2)
    start_final(1)
    start_extra(3)
    start_final(2)
    start_final(3)
    halo(0, "sent")
    halo(1, "sent")
    repeat(1, PLANE, lambda k: conv_copy(k).wait_send())
    for i in range(4):
        if i:
            spread[i].sent()
        main[i].sent()
        extra[i].sent()
        if i != 1:
            repeat(1, PLANE_DP, lambda k: head_copy(i, k).wait_send())
        await_all(outs[i], sems.at[7, i])

    @pl.when(ctx > 0)
    def _():
        await_all(halo_out.at[0], halo_sems.at[0])

    @pl.when(ctx < N_CTX - 1)
    def _():
        await_all(halo_out.at[1], halo_sems.at[1])


def exchange(table, held_q, conv, k, v):
    unit = (SEG_UNIT, LANES)
    conv_unit = (16, WIDE)
    kind = held_q.dtype

    def buffers(count):
        return [pltpu.VMEM((count,) + (conv_unit if i == 1 else unit), kind) for i in range(4)]

    heads = jax.ShapeDtypeStruct((N_CTX * TILES_DEV, PLANE_DP) + unit, kind)
    return pl.pallas_call(
        exchange_kernel,
        out_shape=(
            heads,
            heads,
            heads,
            jax.ShapeDtypeStruct((TILES_DEV, N_CTX, 16, CHANNELS), kind),
            jax.ShapeDtypeStruct((2, 16, CHANNELS), kind),
        ),
        in_specs=[pl.BlockSpec(memory_space=pltpu.SMEM), pl.BlockSpec(memory_space=pltpu.VMEM)]
        + [pl.BlockSpec(memory_space=pl.ANY)] * 3,
        out_specs=[pl.BlockSpec(memory_space=pl.ANY)] * 5,
        scratch_shapes=buffers(HELD)[1:]
        + buffers(MAIN)
        + buffers(MAIN)
        + buffers(EXTRA)
        + buffers(EXTRA)
        + buffers(HELD)
        + [pltpu.SemaphoreType.DMA((8, 4)), pltpu.SemaphoreType.DMA((3,))],
        compiler_params=pltpu.CompilerParams(
            collective_id=1, has_side_effects=True, vmem_limit_bytes=40 * 2**20
        ),
        name="exchange",
    )(table, held_q, conv, k, v)


EDGE = 16


def last_kernel(
    len_ref,
    mix_ref,
    rows_ref,
    halo_ref,
    taps_ref,
    scale_ref,
    shift_ref,
    heads_out,
    conv_out,
    padded,
    send,
    recv,
):
    z, row, ctx = place()
    dp = z * PLANE_DP + row
    repeat(1, N_CTX, lambda k: signal((dp, (ctx + k) % N_CTX)))
    pl.semaphore_wait(pltpu.get_barrier_semaphore(), N_CTX - 1)
    mixed = heads_out.at[:, pl.ds(pl.multiple_of(ctx * LANES, LANES), LANES)]

    def copy(k):
        to = (ctx + k) % N_CTX
        return remote(mix_ref.at[to], mixed, send, recv, (dp, to))

    repeat(1, N_CTX, lambda k: copy(k).start())
    own = pltpu.make_async_copy(mix_ref.at[ctx], mixed, recv)
    own.start()

    padded[pl.ds(0, EDGE), :] = halo_ref[0]
    padded[pl.ds(EDGE, COLUMN), :] = rows_ref[...]
    padded[pl.ds(EDGE + COLUMN, EDGE), :] = halo_ref[1]
    ends = [jnp.int32(0), len_ref[0, 0]]
    for i in range(1, 4):
        ends.append(ends[-1] + len_ref[0, i])
    window = SEG_UNIT + 2 * EDGE

    def channels(group):
        lanes = pl.ds(pl.multiple_of(group * LANES, LANES), LANES)
        scale = scale_ref[:, lanes]
        shift = shift_ref[:, lanes]

        def unit(u):
            place_ = ctx * UNITS + u
            cut_before = jnp.bool_(False)
            cut_after = jnp.bool_(False)
            for end in ends:
                cut_before = cut_before | (place_ == end)
                cut_after = cut_after | (place_ + 1 == end)
            frames = padded[pl.ds(pl.multiple_of(u * SEG_UNIT, SEG_UNIT), window), lanes]
            frames = frames.astype(jnp.float32)
            side = jnp.zeros((EDGE, LANES), jnp.float32)
            frames = jnp.concatenate(
                [
                    jnp.where(cut_before, side, frames[:EDGE]),
                    frames[EDGE : EDGE + SEG_UNIT],
                    jnp.where(cut_after, side, frames[EDGE + SEG_UNIT :]),
                ],
                axis=0,
            )
            total = jnp.zeros((SEG_UNIT, LANES), jnp.float32)
            for turn in range(8):
                turned = pltpu.roll(frames, window - turn, 0) if turn else frames
                for tap in range((turn - 1) % 8, KERNEL, 8):
                    at = tap + 1 - turn
                    total = total + taps_ref[pl.ds(tap, 1), lanes] * turned[at : at + SEG_UNIT]
            value = scale * total + shift
            value = value / (1.0 + jnp.exp(-value))
            conv_out[pl.ds(pl.multiple_of(u * SEG_UNIT, SEG_UNIT), SEG_UNIT), lanes] = value.astype(
                jnp.bfloat16
            )

        repeat(0, UNITS, unit)

    repeat(0, CHANNELS // LANES, channels)
    repeat(1, N_CTX, lambda k: copy(k).wait_send())
    await_all(heads_out, recv)


def last(lengths, mix, rows, halo, taps, scale, shift):
    vmem = pl.BlockSpec(memory_space=pltpu.VMEM)
    anywhere = pl.BlockSpec(memory_space=pl.ANY)
    return pl.pallas_call(
        last_kernel,
        out_shape=(
            jax.ShapeDtypeStruct((COLUMN, N_CTX * LANES), mix.dtype),
            jax.ShapeDtypeStruct((COLUMN, CHANNELS), mix.dtype),
        ),
        in_specs=[pl.BlockSpec(memory_space=pltpu.SMEM), anywhere] + [vmem] * 5,
        out_specs=[anywhere, vmem],
        scratch_shapes=[
            pltpu.VMEM((COLUMN + 2 * EDGE, CHANNELS), mix.dtype),
            pltpu.SemaphoreType.DMA,
            pltpu.SemaphoreType.DMA,
        ],
        compiler_params=pltpu.CompilerParams(
            collective_id=2, has_side_effects=True, vmem_limit_bytes=32 * 2**20
        ),
        name="convolve_and_return",
    )(lengths, mix, rows, halo, taps, scale, shift)


STEP = 2


def attend_kernel(len_ref, q_ref, k_ref, v_ref, out_ref):
    block = pl.program_id(0)
    ends = [len_ref[0, 0]]
    for i in range(1, 4):
        ends.append(ends[-1] + len_ref[0, i])
    first = block * UNITS
    last = first + UNITS - 1
    low = jnp.int32(0)
    high = jnp.int32(FRAMES // SEG_UNIT)
    for end in ends:
        low = jnp.where(end <= first, jnp.maximum(low, end), low)
        high = jnp.where(end > last, jnp.minimum(high, end), high)
    per_key = KBLOCK // SEG_UNIT
    low_block = low // per_key
    steps = ((high + per_key - 1) // per_key - low_block + STEP - 1) // STEP
    low_block = jnp.minimum(low_block, FRAMES // KBLOCK - STEP * steps)

    def segment(unit):
        seg = jnp.zeros(unit.shape, jnp.int32)
        for end in ends[:3]:
            seg = seg + (unit >= end).astype(jnp.int32)
        return seg

    queries = q_ref[...] * 0.125
    lane = lax.broadcasted_iota(jnp.int32, (QBLOCK, LANES), 1)
    zero = jnp.zeros_like(queries)
    both = jnp.concatenate(
        [jnp.where(lane < HEAD_DIM, queries, zero), jnp.where(lane < HEAD_DIM, zero, queries)], axis=0
    )
    row = lax.broadcasted_iota(jnp.int32, (2 * QBLOCK, 1), 0)
    row_seg = segment(first + lax.rem(row, QBLOCK) // SEG_UNIT)
    def step(index, carry):
        top, total, mixed = carry
        at = low_block + index * STEP
        part = pl.ds(pl.multiple_of(at * KBLOCK, KBLOCK), STEP * KBLOCK)
        keys = k_ref[part, :]
        values = v_ref[part, :]
        scores = lax.dot_general(
            both, keys, (((1,), (1,)), ((), ())), preferred_element_type=jnp.float32
        )
        col = lax.broadcasted_iota(jnp.int32, (1, STEP * KBLOCK), 1)
        col_seg = segment(at * per_key + col // SEG_UNIT)
        scores = jnp.where(row_seg == col_seg, scores, -2e30)
        new_top = jnp.maximum(top, jnp.max(scores, axis=1, keepdims=True))
        weights = jnp.exp(scores - new_top)
        scale = jnp.exp(top - new_top)
        total = total * scale + jnp.sum(weights, axis=1, keepdims=True)
        mixed = mixed * scale + jnp.dot(
            weights.astype(jnp.bfloat16), values, preferred_element_type=jnp.float32
        )
        return new_top, total, mixed

    top, total, mixed = lax.fori_loop(
        0,
        steps,
        step,
        (
            jnp.full((2 * QBLOCK, 1), -1e30, jnp.float32),
            jnp.zeros((2 * QBLOCK, 1), jnp.float32),
            jnp.zeros((2 * QBLOCK, LANES), jnp.float32),
        ),
    )
    mixed = mixed / total
    out_ref[0] = jnp.where(lane < HEAD_DIM, mixed[:QBLOCK], mixed[QBLOCK:]).astype(jnp.bfloat16)


def attend(lengths, q, k, v):
    blocks = FRAMES // QBLOCK
    return pl.pallas_call(
        attend_kernel,
        grid_spec=pltpu.PrefetchScalarGridSpec(
            num_scalar_prefetch=1,
            grid=(blocks,),
            in_specs=[
                pl.BlockSpec((QBLOCK, LANES), lambda i, lens: (i, 0)),
                pl.BlockSpec((FRAMES, LANES), lambda i, lens: (0, 0)),
                pl.BlockSpec((FRAMES, LANES), lambda i, lens: (0, 0)),
            ],
            out_specs=pl.BlockSpec((1, QBLOCK, LANES), lambda i, lens: (i, 0, 0)),
        ),
        out_shape=jax.ShapeDtypeStruct((blocks, QBLOCK, LANES), jnp.bfloat16),
        compiler_params=pltpu.CompilerParams(vmem_limit_bytes=48 * 2**20),
        cost_estimate=pl.CostEstimate(
            flops=8 * FRAMES * FRAMES * LANES, bytes_accessed=2**21, transcendentals=2 * FRAMES * FRAMES
        ),
        name="attend",
    )(lengths, q, k, v)


def segment_of(positions, seg_ends):
    unit_index = positions // SEG_UNIT
    return jnp.sum((seg_ends[None, :] <= unit_index[:, None]).astype(jnp.int32), axis=1)


def convolve(signal, halo, lengths, conv_taps, norm_scale, norm_shift):
    seg_ends = jnp.cumsum(lengths[0])
    column = lax.axis_index("ctx")
    half_width = (KERNEL - 1) // 2
    query_seg = segment_of(column * COLUMN + jnp.arange(COLUMN, dtype=jnp.int32), seg_ends)
    before = jnp.where(column > 0, halo[0], 0)
    after = jnp.where(column < N_CTX - 1, halo[1], 0)
    padded = jnp.concatenate([before[1:], signal, after[:half_width]], axis=0).astype(jnp.float32)
    padded_seg = segment_of(
        column * COLUMN - half_width + jnp.arange(COLUMN + 2 * half_width, dtype=jnp.int32), seg_ends
    )
    conv_sum = jnp.zeros(signal.shape, jnp.float32)
    for tap in range(KERNEL):
        same_seg = (padded_seg[tap : tap + COLUMN] == query_seg)[:, None]
        conv_sum = conv_sum + jnp.where(same_seg, conv_taps[tap] * padded[tap : tap + COLUMN], 0.0)
    return jax.nn.silu(norm_scale * conv_sum + norm_shift).astype(jnp.bfloat16)


def share_of(dp, ctx):
    return (dp // 8) * 8 + lax.rem(dp + ctx, 8)


def entry(count, device):
    barrier = pltpu.get_barrier_semaphore()

    def one(k, carry):
        pl.semaphore_signal(barrier, inc=1, device_id=device(k), device_id_type=MESH)
        return carry

    lax.fori_loop(0, count, one, 0)
    pl.semaphore_wait(barrier, count)


def all_arrived(ref, sem):
    pltpu.make_async_copy(ref, ref, sem).wait()


def general_spread_kernel(x_ref, out_ref, send_sem, recv_sem):
    dp, ctx = lax.axis_index("dp"), lax.axis_index("ctx")
    entry(N_DP - 1, lambda k: (lax.rem(dp + 1 + k, N_DP), ctx))

    def copy(k):
        peer = lax.rem(dp + k, N_DP)
        return pltpu.make_async_remote_copy(
            src_ref=x_ref.at[share_of(peer, ctx)],
            dst_ref=out_ref.at[dp],
            send_sem=send_sem,
            recv_sem=recv_sem,
            device_id=(peer, ctx),
            device_id_type=MESH,
        )

    own = pltpu.make_async_copy(x_ref.at[share_of(dp, ctx)], out_ref.at[dp], recv_sem)

    def start(k, carry):
        copy(k).start()
        return carry

    def sent(k, carry):
        copy(k).wait_send()
        return carry

    lax.fori_loop(1, N_DP, start, 0)
    own.start()
    lax.fori_loop(1, N_DP, sent, 0)
    all_arrived(out_ref, recv_sem)


def general_spread(x):
    return pl.pallas_call(
        general_spread_kernel,
        out_shape=jax.ShapeDtypeStruct(x.shape, x.dtype),
        in_specs=[pl.BlockSpec(memory_space=pl.ANY)],
        out_specs=pl.BlockSpec(memory_space=pl.ANY),
        scratch_shapes=[pltpu.SemaphoreType.DMA, pltpu.SemaphoreType.DMA],
        compiler_params=pltpu.CompilerParams(collective_id=3, has_side_effects=True),
        name="general_spread",
    )(x)


def general_heads_kernel(x_ref, out_ref, send_sem, recv_sem):
    dp, ctx = lax.axis_index("dp"), lax.axis_index("ctx")
    share = share_of(dp, ctx)
    group, column = share // 8, lax.rem(share, 8)

    def sender(k):
        other = k // 8
        return (lax.rem(k, 8) * 8 + lax.rem(ctx - other + 8, 8), other)

    barrier = pltpu.get_barrier_semaphore()

    def greet(k, carry):
        peer = sender(k)

        @pl.when(jnp.logical_or(peer[0] != dp, peer[1] != ctx))
        def _():
            pl.semaphore_signal(barrier, inc=1, device_id=peer, device_id_type=MESH)

        return carry

    lax.fori_loop(0, N_DP, greet, 0)
    is_own = column == ctx

    @pl.when(is_own)
    def _():
        pl.semaphore_wait(barrier, N_DP - 1)

    @pl.when(jnp.logical_not(is_own))
    def _():
        pl.semaphore_wait(barrier, N_DP)

    def copy(k):
        peer = lax.rem(dp + k, N_DP)
        return pltpu.make_async_remote_copy(
            src_ref=x_ref.at[peer],
            dst_ref=out_ref.at[pl.ds(ctx * TILES_DEV, TILES_DEV), group],
            send_sem=send_sem,
            recv_sem=recv_sem,
            device_id=(peer, column),
            device_id_type=MESH,
        )

    def start(k, carry):
        copy(k).start()
        return carry

    def sent(k, carry):
        copy(k).wait_send()
        return carry

    lax.fori_loop(1, N_DP, start, 0)

    @pl.when(is_own)
    def _():
        pltpu.make_async_copy(
            x_ref.at[dp], out_ref.at[pl.ds(ctx * TILES_DEV, TILES_DEV), group], recv_sem
        ).start()

    @pl.when(jnp.logical_not(is_own))
    def _():
        copy(0).start()
        copy(0).wait_send()

    lax.fori_loop(1, N_DP, sent, 0)
    all_arrived(out_ref, recv_sem)


def general_heads(x):
    return pl.pallas_call(
        general_heads_kernel,
        out_shape=jax.ShapeDtypeStruct((N_CTX * TILES_DEV, TILE // ROWS, 3, ROWS, LANES), x.dtype),
        in_specs=[pl.BlockSpec(memory_space=pl.ANY)],
        out_specs=pl.BlockSpec(memory_space=pl.ANY),
        scratch_shapes=[pltpu.SemaphoreType.DMA, pltpu.SemaphoreType.DMA],
        compiler_params=pltpu.CompilerParams(collective_id=4, has_side_effects=True),
        name="general_heads",
    )(x)


def general_deliver_kernel(x_ref, mix_ref, out_ref, heads_ref, send_sem, recv_sem, mix_send, mix_recv):
    dp, ctx = lax.axis_index("dp"), lax.axis_index("ctx")
    share = share_of(dp, ctx)
    barrier = pltpu.get_barrier_semaphore()

    def greet_dp(k, carry):
        pl.semaphore_signal(
            barrier, inc=1, device_id=(lax.rem(dp + k, N_DP), ctx), device_id_type=MESH
        )
        return carry

    def greet_ctx(k, carry):
        pl.semaphore_signal(
            barrier, inc=1, device_id=(dp, lax.rem(ctx + k, N_CTX)), device_id_type=MESH
        )
        return carry

    lax.fori_loop(1, N_DP, greet_dp, 0)
    lax.fori_loop(1, N_CTX, greet_ctx, 0)
    pl.semaphore_wait(barrier, N_DP - 1 + N_CTX - 1)

    def mix_copy(k):
        peer = lax.rem(ctx + k, N_CTX)
        return pltpu.make_async_remote_copy(
            src_ref=mix_ref.at[peer],
            dst_ref=heads_ref.at[:, pl.ds(pl.multiple_of(ctx * LANES, LANES), LANES)],
            send_sem=mix_send,
            recv_sem=mix_recv,
            device_id=(dp, peer),
            device_id_type=MESH,
        )

    def copy(k):
        peer = lax.rem(dp + k, N_DP)
        return pltpu.make_async_remote_copy(
            src_ref=x_ref.at[peer],
            dst_ref=out_ref.at[share],
            send_sem=send_sem,
            recv_sem=recv_sem,
            device_id=(peer, ctx),
            device_id_type=MESH,
        )

    def start(k, carry):
        copy(k).start()
        return carry

    def sent(k, carry):
        copy(k).wait_send()
        return carry

    def mix_start(k, carry):
        mix_copy(k).start()
        return carry

    def mix_sent(k, carry):
        mix_copy(k).wait_send()
        return carry

    lax.fori_loop(1, N_DP, start, 0)
    lax.fori_loop(1, N_CTX, mix_start, 0)
    pltpu.make_async_copy(x_ref.at[dp], out_ref.at[share], recv_sem).start()
    pltpu.make_async_copy(
        mix_ref.at[ctx],
        heads_ref.at[:, pl.ds(pl.multiple_of(ctx * LANES, LANES), LANES)],
        mix_recv,
    ).start()
    lax.fori_loop(1, N_DP, sent, 0)
    lax.fori_loop(1, N_CTX, mix_sent, 0)
    all_arrived(out_ref, recv_sem)
    all_arrived(heads_ref, mix_recv)


def general_deliver(x, mix):
    rows = FRAMES // N_CTX
    return pl.pallas_call(
        general_deliver_kernel,
        out_shape=(
            jax.ShapeDtypeStruct(x.shape, x.dtype),
            jax.ShapeDtypeStruct((rows, N_CTX * LANES), x.dtype),
        ),
        in_specs=[pl.BlockSpec(memory_space=pl.ANY)] * 2,
        out_specs=[pl.BlockSpec(memory_space=pl.ANY)] * 2,
        scratch_shapes=[pltpu.SemaphoreType.DMA] * 4,
        compiler_params=pltpu.CompilerParams(collective_id=5, has_side_effects=True),
        name="general_deliver",
    )(x, mix)


def general_path(
    query_loader,
    key_loader,
    value_loader,
    conv_loader,
    slot_tile,
    lengths,
    conv_taps,
    norm_scale,
    norm_shift,
):
    qkv = jnp.stack([query_loader[0], key_loader[0], value_loader[0]])
    qkv = qkv.reshape(3, TILES_DEV, TILE // ROWS, ROWS, N_CTX, LANES)
    qkv = jnp.transpose(qkv, (2, 4, 1, 0, 3, 5)).reshape(N_DP, TILES_DEV * QKV, LANES)
    conv = conv_loader[0].reshape(TILES_DEV, N_DP, CONV_ROWS, LANES)
    conv = jnp.transpose(conv, (1, 0, 2, 3)).reshape(N_DP, TILES_DEV * CONV_ROWS, LANES)
    got = general_spread(jnp.concatenate([qkv, conv], axis=1))
    order = slot_tile[0]
    got_qkv = got[:, : TILES_DEV * QKV].reshape(N_DP * TILES_DEV, 3, ROWS, LANES)
    send_qkv = got_qkv[order].reshape(N_DP, TILES_DEV, 3, ROWS, LANES)
    got_conv = got[:, TILES_DEV * QKV :].reshape(N_DP * TILES_DEV, CONV_ROWS, LANES)
    send_conv = got_conv[order].reshape(N_DP, TILES_DEV * CONV_ROWS, LANES)
    heads = general_heads(send_qkv)
    flat = (FRAMES, LANES)
    mix = attend(lengths, *(heads[:, :, i].reshape(flat) for i in range(3)))
    signal, attention_out = general_deliver(send_conv, mix)
    signal = signal.reshape(N_DP, TILES_DEV, TILE // N_DP, CONV_ROWS // 2 * LANES)
    signal = jnp.transpose(signal, (1, 0, 2, 3)).reshape(TILES_DEV * TILE, CONV_ROWS // 2 * LANES)
    ends = N_CTX - 1
    halo = jnp.stack(
        [
            lax.ppermute(signal[COLUMN - 16 :], "ctx", [(i, i + 1) for i in range(ends)]),
            lax.ppermute(signal[:16], "ctx", [(i + 1, i) for i in range(ends)]),
        ]
    )
    conv_out = convolve(signal, halo, lengths, conv_taps, norm_scale, norm_shift)
    return attention_out[None], conv_out[None]


def on_device(*inputs):
    query, key, value, conv, slot_tile, lengths, conv_taps, norm_scale, norm_shift = inputs
    places = jnp.transpose(slot_tile[0].reshape(N_Z, 8))
    places = jnp.pad(places, ((0, 0), (0, LANES - N_Z)), constant_values=1 << 16)
    shape = (TILES_DEV, PLANE_DP, SEG_UNIT, HEADS * HEAD_DIM)
    held_q, lists = first(query.reshape(shape), places)
    table = route(lists.reshape(HELD, LANES))
    q, k, v, rows, halo = exchange(
        table,
        held_q,
        conv.reshape(TILES_DEV, N_CTX, 16, CHANNELS),
        key.reshape(shape),
        value.reshape(shape),
    )
    heads = (FRAMES, LANES)
    mix = attend(lengths, q.reshape(heads), k.reshape(heads), v.reshape(heads))
    attention_out, conv_out = last(
        lengths,
        mix,
        rows.reshape(COLUMN, CHANNELS),
        halo,
        conv_taps,
        norm_scale.reshape(1, CHANNELS),
        norm_shift.reshape(1, CHANNELS),
    )
    return lax.cond(
        table[AT_BAD] == 0,
        lambda: (attention_out[None], conv_out[None]),
        lambda: general_path(*inputs),
    )


def solution(mesh):
    return jax.shard_map(
        on_device,
        mesh=mesh,
        in_specs=(
            P("dp", "ctx", None),
            P("dp", "ctx", None),
            P("dp", "ctx", None),
            P("dp", "ctx", None),
            P("ctx", None),
            P("dp", None),
            P(),
            P(),
            P(),
        ),
        out_specs=(P("dp", "ctx", None), P("dp", "ctx", None)),
        check_vma=False,
    )
```

```python
import jax
import jax.numpy as jnp
from jax import lax
from jax.experimental import pallas as pl
from jax.experimental.pallas import tpu as pltpu
from jax.sharding import PartitionSpec as P

MESH = pl.DeviceIdType.MESH
HEADS = 16
HEAD_DIM = 64
CHANNELS = 1536
KERNEL = 31
TILE = 128
TILES_DEV = 2
SEG_UNIT = 32
FRAMES = 2048
COLUMN = 256
LANES = 128
N_DP = 64
N_CTX = 8
ROWS = 16
QKV = 3 * ROWS
CONV_ROWS = 24
KEYS = 512
QBLOCK = 256
KBLOCK = 256
UNITS = QBLOCK // SEG_UNIT

N_Z = 16
PLANE_DP = 4
PLANE = PLANE_DP * N_CTX
HELD = PLANE * TILES_DEV
SHIFTS = N_Z - 1
NEAR, NEAR_SLOTS, FAR_SLOTS = 6, 5, 4
RELAYS, RELAY_SLOTS = 10, 2
MAIN = NEAR * NEAR_SLOTS + (SHIFTS - NEAR) * FAR_SLOTS
EXTRA = RELAYS * RELAY_SLOTS
TABLE = 256
AT_MAIN, AT_EXTRA, AT_FINAL, AT_BAD = 0, 72, 96, 160
RANKS = 16
PAIRS = N_Z * N_Z
LIST = 2304
FIELDS = 0x55555555


def shift_of(j):
    half = j // 2
    return jnp.where(j % 2 == 0, half + 1, N_Z - 1 - half)


def order_of(shift):
    return jnp.where(shift <= N_Z // 2, 2 * (shift - 1), 2 * (N_Z - shift) - 1)


def main_slots(shift):
    return jnp.where(order_of(shift) < NEAR, NEAR_SLOTS, FAR_SLOTS)


def main_offset(shift):
    j = order_of(shift)
    return jnp.where(j < NEAR, NEAR_SLOTS * j, NEAR * NEAR_SLOTS + FAR_SLOTS * (j - NEAR))


def relay_offset(shift):
    return RELAY_SLOTS * order_of(shift)


def place():
    dp, ctx = lax.axis_index("dp"), lax.axis_index("ctx")
    return dp // PLANE_DP, dp % PLANE_DP, ctx


def plane_peer(z, row, ctx, k):
    index = (row * N_CTX + ctx + k) % PLANE
    return index // N_CTX, index % N_CTX, (z * PLANE_DP + index // N_CTX, index % N_CTX)


def z_peer(z, row, ctx, j):
    return ((z + shift_of(j)) % N_Z * PLANE_DP + row, ctx)


def repeat(first, last, body):
    def one(k, carry):
        body(k)
        return carry

    lax.fori_loop(first, last, one, 0)


def remote(src, dst, send, recv, device):
    return pltpu.make_async_remote_copy(
        src_ref=src, dst_ref=dst, send_sem=send, recv_sem=recv, device_id=device, device_id_type=MESH
    )


def await_all(ref, sem):
    pltpu.make_async_copy(ref, ref, sem).wait()


def signal(device):
    pl.semaphore_signal(pltpu.get_barrier_semaphore(), inc=1, device_id=device, device_id_type=MESH)


class Spread:
    def __init__(self, piece, held, send, recv):
        z, row, ctx = place()
        mine = pl.ds((ctx * PLANE_DP + row) * TILES_DEV, TILES_DEV)

        def copy(k):
            to_row, to_ctx, device = plane_peer(z, row, ctx, k)
            return remote(piece(to_row, to_ctx), held.at[mine], send, recv, device)

        self.copy, self.held, self.recv = copy, held, recv
        self.own = pltpu.make_async_copy(piece(row, ctx), held.at[mine], recv)

    def start(self):
        repeat(1, PLANE, lambda k: self.copy(k).start())
        self.own.start()

    def arrived(self):
        await_all(self.held, self.recv)

    def sent(self):
        repeat(1, PLANE, lambda k: self.copy(k).wait_send())


class Along:
    def __init__(self, groups, staged, got, send, recv):
        z, row, ctx = place()
        self.staged, self.got, self.send, self.recv = staged, got, send, recv

        def copy(j, offset, slots):
            part = pl.ds(offset, slots)
            return remote(staged.at[part], got.at[part], send, recv, z_peer(z, row, ctx, j))

        self.copy, self.groups = copy, groups

    def start(self):
        for first, last, base, slots in self.groups:
            repeat(
                first,
                last,
                lambda j: self.copy(j, base + (j - first) * slots, slots).start(),
            )

    def arrived(self):
        await_all(self.got, self.recv)

    def sent(self):
        await_all(self.staged, self.send)


MAIN_GROUPS = ((0, NEAR, 0, NEAR_SLOTS), (NEAR, SHIFTS, NEAR * NEAR_SLOTS, FAR_SLOTS))
EXTRA_GROUPS = ((0, RELAYS, 0, RELAY_SLOTS),)


def stage_main(table, held, staged):
    def one(i):
        staged[i] = held[table[AT_MAIN + i]]

    repeat(0, MAIN, one)


def stage_extra(table, held, got, staged):
    def one(i):
        code = table[AT_EXTRA + i]
        staged[i] = jnp.where(
            code < HELD, held[jnp.minimum(code, HELD - 1)], got[jnp.clip(code - HELD, 0, MAIN - 1)]
        )

    repeat(0, EXTRA, one)


def stage_final(table, held, got, more, staged):
    def one(i):
        code = table[AT_FINAL + i]
        first = held[jnp.minimum(code, HELD - 1)]
        second = got[jnp.clip(code - HELD, 0, MAIN - 1)]
        third = more[jnp.clip(code - HELD - MAIN, 0, EXTRA - 1)]
        staged[i] = jnp.where(code < HELD, first, jnp.where(code < HELD + MAIN, second, third))

    repeat(0, HELD, one)


def head_piece(ref):
    return lambda row, ctx: ref.at[:, row, :, pl.ds(pl.multiple_of(ctx * LANES, LANES), LANES)]


WIDE = CHANNELS // PLANE_DP


def first_kernel(q_ref, list_ref, held_ref, lists_ref, send, recv, list_send, list_recv):
    z, row, ctx = place()
    repeat(1, PLANE, lambda k: signal(plane_peer(z, row, ctx, k)[2]))
    pl.semaphore_wait(pltpu.get_barrier_semaphore(), PLANE - 1)

    def tell(k):
        device = (z * PLANE_DP + row, (ctx + k) % N_CTX)
        return remote(list_ref, lists_ref.at[ctx], list_send, list_recv, device)

    repeat(1, N_CTX, lambda k: tell(k).start())
    pltpu.make_async_copy(list_ref, lists_ref.at[ctx], list_recv).start()
    spread = Spread(head_piece(q_ref), held_ref, send, recv)
    spread.start()
    repeat(1, N_CTX, lambda k: tell(k).wait_send())
    await_all(lists_ref, list_recv)
    spread.arrived()
    spread.sent()


def first(q, own_list):
    return pl.pallas_call(
        first_kernel,
        out_shape=(
            jax.ShapeDtypeStruct((HELD, SEG_UNIT, LANES), q.dtype),
            jax.ShapeDtypeStruct((N_CTX,) + own_list.shape, own_list.dtype),
        ),
        in_specs=[pl.BlockSpec(memory_space=pl.ANY)] * 2,
        out_specs=[pl.BlockSpec(memory_space=pl.ANY)] * 2,
        scratch_shapes=[pltpu.SemaphoreType.DMA] * 4,
        compiler_params=pltpu.CompilerParams(collective_id=0, has_side_effects=True),
        name="spread_queries",
    )(q, own_list)


def filled(fields):
    return (fields | (fields >> 1)) & FIELDS


def field_index(bit):
    def step(mask, worth):
        return jnp.where((bit & mask) != 0, worth, 0)

    high = jnp.where(bit >= (1 << 16), 8, 0)
    return high + step(0x7F00FF00, 4) + step(0x70F0F0F0, 2) + step(0x4CCCCCCC & FIELDS, 1)


def field_value(fields, bit):
    return jnp.where((fields & bit) != 0, 1, 0) + jnp.where((fields & (bit << 1)) != 0, 2, 0)


def relay_fields(y):
    fields = 0
    for m in range(N_Z):
        shift = (y - m) % N_Z
        order = 2 * (shift - 1) if shift <= N_Z // 2 else 2 * (N_Z - shift) - 1
        if shift and order < RELAYS:
            fields |= RELAY_SLOTS << (2 * m)
    return fields - (1 << 32) if fields >= 1 << 31 else fields


LOW, HIGH, OVER = N_Z, N_Z + 1, N_Z + 2


def route_kernel(
    lists_ref,
    table,
    count_v,
    excess_v,
    tile_v,
    slot_v,
    count,
    excess,
    tile,
    slot,
    direct,
    relay_free,
    sems,
):
    me = lax.axis_index("dp") // PLANE_DP
    tiles = lists_ref[...]
    source = tiles >> 3
    rows = lax.broadcasted_iota(jnp.int32, (HELD, LANES), 0)
    lanes = lax.broadcasted_iota(jnp.int32, (HELD, LANES), 1)
    local = (rows & ~7) + (tiles & 7)
    position = ((rows & 7) >> 1) * 16 + (rows >> 3) * 2 + (rows & 1)

    def total(values):
        return jnp.sum(values, axis=0, keepdims=True, dtype=jnp.int32)

    for i in range(N_Z):
        count_v[pl.ds(i, 1), :] = total(jnp.where(source == i, 1, 0))
    held = count_v[...]
    z = lax.broadcasted_iota(jnp.int32, held.shape, 0)
    y = lax.broadcasted_iota(jnp.int32, held.shape, 1)
    shift = (y - z) & 15
    stays = shift == 0
    most = jnp.where(stays, RANKS, main_slots(shift))
    real = y < N_Z
    left = jnp.where(stays, 3, jnp.clip(most - held, 0, 3)) << (2 * (y & 7))
    low = jnp.sum(jnp.where(y < 8, left, 0), axis=1, keepdims=True)
    high = jnp.sum(jnp.where((y >= 8) & real, left, 0), axis=1, keepdims=True)
    over = jnp.max(jnp.where(real & (held > RANKS), 1, 0), axis=1, keepdims=True)
    extra = jnp.where(real, jnp.maximum(jnp.minimum(held, RANKS) - most, 0), 0)
    extra = jnp.where(y == LOW, low, jnp.where(y == HIGH, high, jnp.where(y == OVER, over, extra)))
    excess_v[...] = extra
    copies = [
        pltpu.make_async_copy(a, b, sems.at[i])
        for i, (a, b) in enumerate(
            ((count_v, count), (excess_v, excess), (tile_v, tile), (slot_v, slot))
        )
    ]
    copies[0].start()
    copies[1].start()

    def add_rank(i, rank):
        other = lists_ref[pl.ds(i, 1), :] >> 3
        return rank + jnp.where((other == source) & (rows > i), 1, 0)

    rank = lax.fori_loop(0, HELD, add_rank, jnp.zeros((HELD, LANES), jnp.int32), unroll=8)
    here = lanes == me
    column_source = jnp.sum(jnp.where(here, source, 0), axis=1, keepdims=True)
    column_rank = jnp.sum(jnp.where(here, rank, 0), axis=1, keepdims=True)
    mine = jnp.where(source == me, rank, -1)
    taken = jnp.where(column_source == lanes, column_rank, -1)
    for i in range(RANKS):
        tile_v[pl.ds(i, 1), :] = total(jnp.where(mine == i, local, 0))
        slot_v[pl.ds(i, 1), :] = total(jnp.where(taken == i, position, 0))
    copies[2].start()
    copies[3].start()
    for i in range(AT_BAD):
        table[i] = 0
    for i in range(N_Z):
        relay_free[i] = jnp.int32(relay_fields(i))
    for copy in copies:
        copy.wait()

    def open_row(z):
        def open_pair(y):
            shift = (y - z) & 15
            most = jnp.where(shift == 0, RANKS, main_slots(shift))
            direct[z * N_Z + y] = jnp.minimum(count[z, y], most)

        for y in range(N_Z):
            open_pair(y)

    repeat(0, N_Z, open_row)
    my_bit = jnp.int32(1) << (2 * me)

    def record(z, y, bit, rank, free, relay, main):
        @pl.when((z == me) | (bit == my_bit) | (y == me))
        def _():
            m = field_index(bit)
            own = jnp.where(main >= 0, main, count[z, m] + field_value(free, bit) - 1)
            main_at = main_offset((m - z) & 15) + own
            extra_at = relay_offset((y - m) & 15) + field_value(relay, bit) - 1

            @pl.when((z == me) & (m != z))
            def _():
                table[AT_MAIN + main_at] = tile[rank, y]

            @pl.when(m == me)
            def _():
                table[AT_EXTRA + extra_at] = jnp.where(m == z, tile[rank, y], HELD + main_at)

            @pl.when(y == me)
            def _():
                table[AT_FINAL + slot[rank, z]] = HELD + MAIN + extra_at

    def place_row(z, bad):
        own = jnp.int32(1) << (2 * z)

        def take(free, bit):
            return free - jnp.where(bit == own, 0, bit)

        def place_pair(i, carry):
            y = (i + z) & 15
            most = main_slots(i)

            def place_one(e, carry):
                free, bad = carry
                relay = relay_free[y]
                open_ = filled(free) & filled(relay)

                def simple():
                    late = open_ & (jnp.int32(-1) << (2 * ((y + 8) & 15)))
                    chosen = jnp.where(late != 0, late, open_)
                    bit = chosen & -chosen
                    record(z, y, bit, most + e, free, relay, jnp.int32(-1))
                    relay_free[y] = relay - bit
                    return take(free, bit), bad

                def swap():
                    def look(m, carry):
                        free, done = carry
                        bit = jnp.int32(1) << (2 * m)
                        relay_m = relay_free[m]
                        other = filled(free) & filled(relay_m)
                        straight = direct[z * N_Z + m]
                        fits = (
                            (done == 0)
                            & (m != z)
                            & (m != y)
                            & ((filled(relay) & bit) != 0)
                            & (straight > 0)
                            & (other != 0)
                        )

                        def do():
                            instead = other & -other
                            direct[z * N_Z + m] = straight - 1
                            record(z, m, instead, straight - 1, free, relay_m, jnp.int32(-1))
                            record(z, y, bit, most + e, free, relay, straight - 1)
                            relay_free[m] = relay_m - instead
                            relay_free[y] = relay - bit
                            return take(free, instead), jnp.int32(1)

                        return lax.cond(fits, do, lambda: (free, done))

                    free_, done = lax.fori_loop(0, N_Z, look, (free, jnp.int32(0)))
                    return free_, bad | (1 - done)

                return lax.cond(open_ != 0, simple, swap)

            return lax.fori_loop(0, excess[z, y], place_one, carry)

        free = excess[z, LOW] | (excess[z, HIGH] << 16)
        free, bad = lax.fori_loop(1, N_Z, place_pair, (free, bad | excess[z, OVER]))
        return bad

    table[AT_BAD] = lax.fori_loop(0, N_Z, place_row, jnp.int32(0))

    def straight(other):
        shift_out = (other - me) & 15
        shift_in = (me - other) & 15

        @pl.when(shift_out != 0)
        def _():
            first_out = AT_MAIN + main_offset(shift_out)
            first_in = HELD + main_offset(shift_in)

            def out(r):
                table[first_out + r] = tile[r, other]

            def arrive(r):
                table[AT_FINAL + slot[r, other]] = first_in + r

            repeat(0, direct[me * N_Z + other], out)
            repeat(0, direct[other * N_Z + me], arrive)

        @pl.when(shift_out == 0)
        def _():
            def keep(r):
                table[AT_FINAL + slot[r, me]] = tile[r, me]

            repeat(0, direct[me * N_Z + me], keep)

    repeat(0, N_Z, straight)


def route(lists):
    smem = pltpu.SMEM
    square = smem((N_Z, LANES), jnp.int32)
    square_v = pltpu.VMEM((N_Z, LANES), jnp.int32)
    return pl.pallas_call(
        route_kernel,
        out_shape=jax.ShapeDtypeStruct((TABLE,), jnp.int32),
        in_specs=[pl.BlockSpec(memory_space=pltpu.VMEM)],
        out_specs=pl.BlockSpec(memory_space=smem),
        scratch_shapes=[square_v] * 4
        + [square] * 4
        + [smem((PAIRS,), jnp.int32), smem((N_Z,), jnp.int32), pltpu.SemaphoreType.DMA((4,))],
        name="route",
    )(lists)


PARTS = ((0, 128), (128, 128), (256, 128))
ARRAYS = 3 + len(PARTS)


def conv_lanes(row, part):
    first, width = PARTS[part]
    return pl.ds(pl.multiple_of(row * WIDE + first, LANES), width)


def conv_piece(ref, part):
    return lambda row, ctx: ref.at[:, ctx, :, conv_lanes(row, part)]


def exchange_kernel(
    table, lengths, held_q, k_ref, v_ref, conv_ref, heads_out, rows_out, halo_out, *scratch
):
    z, row, ctx = place()
    dp = z * PLANE_DP + row
    repeat(1, PLANE, lambda k: signal(plane_peer(z, row, ctx, k)[2]))
    repeat(0, SHIFTS, lambda j: signal(z_peer(z, row, ctx, j)))
    pl.semaphore_wait(pltpu.get_barrier_semaphore(), PLANE - 1 + SHIFTS)
    held = (held_q,) + scratch[: ARRAYS - 1]
    main_staged, main_got, extra_staged, extra_got, staged = (
        scratch[ARRAYS * (i + 1) - 1 : ARRAYS * (i + 2) - 1] for i in range(5)
    )
    group = scratch[6 * ARRAYS - 1 : 6 * ARRAYS + 2]
    mixture, sems, halo_sems, mix_sems = scratch[6 * ARRAYS + 2 :]
    pieces = [None, head_piece(k_ref), head_piece(v_ref)] + [conv_piece(conv_ref, i) for i in range(len(PARTS))]
    spread = [None] + [
        Spread(pieces[i], held[i], sems.at[0, i], sems.at[1, i]) for i in range(1, ARRAYS)
    ]
    main = [
        Along(MAIN_GROUPS, main_staged[i], main_got[i], sems.at[2, i], sems.at[3, i])
        for i in range(ARRAYS)
    ]
    extra = [
        Along(EXTRA_GROUPS, extra_staged[i], extra_got[i], sems.at[4, i], sems.at[5, i])
        for i in range(ARRAYS)
    ]

    def start_main(i):
        if i:
            spread[i].arrived()
        stage_main(table, held[i], main_staged[i])
        main[i].start()

    def start_extra(i):
        main[i].arrived()
        stage_extra(table, held[i], main_got[i], extra_staged[i])
        extra[i].start()

    def head_copy(i, k):
        to = (row + k) % PLANE_DP
        return remote(
            staged[i].at[pl.ds(to * 16, 16)],
            group[i].at[:, row],
            sems.at[6, i],
            sems.at[7, i],
            (z * PLANE_DP + to, ctx),
        )

    def part(i, to_row, to_ctx):
        return staged[i].at[pl.ds(to_row * 16 + to_ctx * TILES_DEV, TILES_DEV)]

    def rows_part(i):
        return rows_out.at[:, ctx, :, conv_lanes(row, i - 3)]

    def conv_copy(i, k):
        to_row, to_ctx, device = plane_peer(z, row, ctx, k)
        return remote(part(i, to_row, to_ctx), rows_part(i), sems.at[6, i], sems.at[7, 3], device)

    def halo(i, side, act):
        step, tile = (1, 1) if side == 0 else (-1, 0)

        def one(k):
            to_row = k // (N_CTX - 1)
            column = k % (N_CTX - 1) + (0 if side == 0 else 1)
            target = column + step
            src = staged[i].at[to_row * 16 + column * TILES_DEV + tile]
            dst = halo_out.at[side, :, conv_lanes(row, i - 3)]
            is_own = (to_row == row) & (target == ctx)

            @pl.when(is_own)
            def _():
                if act == "start":
                    pltpu.make_async_copy(src, dst, halo_sems.at[side]).start()

            @pl.when(jnp.logical_not(is_own))
            def _():
                far = remote(
                    src, dst, halo_sems.at[2], halo_sems.at[side], (z * PLANE_DP + to_row, target)
                )
                if act == "start":
                    far.start()
                else:
                    far.wait_send()

        @pl.when(ctx == (N_CTX - 1 if side == 0 else 0))
        def _():
            repeat(0, PLANE_DP * (N_CTX - 1), one)

    def start_final(i):
        extra[i].arrived()
        stage_final(table, held[i], main_got[i], extra_got[i], staged[i])
        if i >= 3:
            repeat(1, PLANE, lambda k: conv_copy(i, k).start())
            pltpu.make_async_copy(part(i, row, ctx), rows_part(i), sems.at[7, 3]).start()
            halo(i, 0, "start")
            halo(i, 1, "start")
        else:
            repeat(1, PLANE_DP, lambda k: head_copy(i, k).start())
            pltpu.make_async_copy(
                staged[i].at[pl.ds(row * 16, 16)], group[i].at[:, row], sems.at[7, i]
            ).start()

    ends = [lengths[0, 0]]
    for i in range(1, 3):
        ends.append(ends[-1] + lengths[0, i])

    def segment(unit):
        seg = jnp.zeros(unit.shape, jnp.int32)
        for end in ends:
            seg = seg + (unit >= end).astype(jnp.int32)
        return seg

    mixed_at = heads_out.at[:, pl.ds(pl.multiple_of(ctx * LANES, LANES), LANES)]

    def mix_copy(block):
        return remote(mixture.at[block], mixed_at, mix_sems.at[0], mix_sems.at[1], (dp, block))

    lane = lax.broadcasted_iota(jnp.int32, (QBLOCK, LANES), 1)
    query = lax.broadcasted_iota(jnp.int32, (2 * QBLOCK, 1), 0) % QBLOCK
    key = lax.broadcasted_iota(jnp.int32, (1, KEYS), 1)

    def attend_block(block, first_key, steps):
        queries = group[0][pl.ds(block * TILES_DEV, TILES_DEV)].reshape(QBLOCK, LANES) * 0.125
        zero = jnp.zeros_like(queries)
        both = jnp.concatenate(
            [jnp.where(lane < HEAD_DIM, queries, zero), jnp.where(lane < HEAD_DIM, zero, queries)],
            axis=0,
        )
        query_seg = segment(block * UNITS + query // SEG_UNIT)

        def step(index, carry):
            top, total, mixed = carry
            at = first_key + index * KEYS
            tiles = pl.ds(first_key // TILE + index * (KEYS // TILE), KEYS // TILE)
            keys = group[1][tiles].reshape(KEYS, LANES)
            values = group[2][tiles].reshape(KEYS, LANES)
            scores = lax.dot_general(
                both, keys, (((1,), (1,)), ((), ())), preferred_element_type=jnp.float32
            )
            key_seg = segment((at + key) // SEG_UNIT)
            scores = jnp.where(query_seg == key_seg, scores, -2e30)
            new_top = jnp.maximum(top, jnp.max(scores, axis=1, keepdims=True))
            weights = jnp.exp(scores - new_top)
            scale = jnp.exp(top - new_top)
            total = total * scale + jnp.sum(weights, axis=1, keepdims=True)
            mixed = mixed * scale + jnp.dot(
                weights.astype(jnp.bfloat16), values, preferred_element_type=jnp.float32
            )
            return new_top, total, mixed

        _, total, mixed = lax.fori_loop(
            0,
            steps,
            step,
            (
                jnp.full((2 * QBLOCK, 1), -1e30, jnp.float32),
                jnp.zeros((2 * QBLOCK, 1), jnp.float32),
                jnp.zeros((2 * QBLOCK, LANES), jnp.float32),
            ),
        )
        mixed = mixed / total
        mixture[block] = jnp.where(lane < HEAD_DIM, mixed[:QBLOCK], mixed[QBLOCK:]).astype(jnp.bfloat16)

        @pl.when(block == ctx)
        def _():
            pltpu.make_async_copy(mixture.at[block], mixed_at, mix_sems.at[1]).start()

        @pl.when(block != ctx)
        def _():
            mix_copy(block).start()

    def attend_blocks(first, last, first_key, steps):
        repeat(first, last, lambda block: attend_block(block, first_key, steps))

    spread[1].start()
    start_main(0)
    spread[2].start()
    start_main(1)
    spread[3].start()
    spread[4].start()
    spread[5].start()
    start_extra(0)
    start_main(2)
    start_extra(1)
    start_final(0)
    start_main(3)
    start_extra(2)
    start_main(4)
    start_main(5)
    start_final(1)
    start_final(2)
    for i in range(3):
        await_all(group[i], sems.at[7, i])
    attend_blocks(0, 2, 0, 3)
    start_extra(3)
    attend_blocks(2, 4, 0, 4)
    start_final(3)
    start_extra(4)
    attend_blocks(4, 6, 0, 4)
    start_final(4)
    start_extra(5)
    attend_blocks(6, 8, FRAMES - 3 * KEYS, 3)
    start_final(5)
    for i in range(ARRAYS):
        if i:
            spread[i].sent()
        main[i].sent()
        extra[i].sent()
        if i < 3:
            repeat(1, PLANE_DP, lambda k: head_copy(i, k).wait_send())
        else:
            repeat(1, PLANE, lambda k: conv_copy(i, k).wait_send())
            halo(i, 0, "sent")
            halo(i, 1, "sent")

    def mix_sent(block):
        @pl.when(block != ctx)
        def _():
            mix_copy(block).wait_send()

    repeat(0, N_CTX, mix_sent)
    await_all(heads_out, mix_sems.at[1])
    await_all(rows_out, sems.at[7, 3])

    @pl.when(ctx > 0)
    def _():
        await_all(halo_out.at[0], halo_sems.at[0])

    @pl.when(ctx < N_CTX - 1)
    def _():
        await_all(halo_out.at[1], halo_sems.at[1])


def exchange(table, lengths, held_q, k, v, conv):
    unit = (SEG_UNIT, LANES)
    kind = held_q.dtype

    def buffers(count):
        return [pltpu.VMEM((count,) + (unit if i < 3 else (16, PARTS[i - 3][1])), kind) for i in range(ARRAYS)]

    smem = pl.BlockSpec(memory_space=pltpu.SMEM)
    return pl.pallas_call(
        exchange_kernel,
        out_shape=(
            jax.ShapeDtypeStruct((COLUMN, N_CTX * LANES), kind),
            jax.ShapeDtypeStruct((TILES_DEV, N_CTX, 16, CHANNELS), kind),
            jax.ShapeDtypeStruct((2, 16, CHANNELS), kind),
        ),
        in_specs=[smem, smem, pl.BlockSpec(memory_space=pltpu.VMEM)]
        + [pl.BlockSpec(memory_space=pl.ANY)] * 3,
        out_specs=[pl.BlockSpec(memory_space=pl.ANY)] * 3,
        scratch_shapes=buffers(HELD)[1:]
        + buffers(MAIN)
        + buffers(MAIN)
        + buffers(EXTRA)
        + buffers(EXTRA)
        + buffers(HELD)
        + [pltpu.VMEM((N_CTX * TILES_DEV, PLANE_DP) + unit, kind)] * 3
        + [
            pltpu.VMEM((N_CTX, COLUMN, LANES), kind),
            pltpu.SemaphoreType.DMA((8, ARRAYS)),
            pltpu.SemaphoreType.DMA((3,)),
            pltpu.SemaphoreType.DMA((2,)),
        ],
        compiler_params=pltpu.CompilerParams(
            collective_id=1, has_side_effects=True, vmem_limit_bytes=48 * 2**20
        ),
        name="exchange",
    )(table, lengths, held_q, k, v, conv)


EDGE = 16


def convolve_kernel(
    len_ref,
    rows_ref,
    halo_ref,
    taps_ref,
    scale_ref,
    shift_ref,
    conv_out,
    padded,
):
    ctx = lax.axis_index("ctx")
    padded[pl.ds(0, EDGE), :] = halo_ref[0]
    padded[pl.ds(EDGE, COLUMN), :] = rows_ref[...]
    padded[pl.ds(EDGE + COLUMN, EDGE), :] = halo_ref[1]
    ends = [jnp.int32(0), len_ref[0, 0]]
    for i in range(1, 4):
        ends.append(ends[-1] + len_ref[0, i])
    window = SEG_UNIT + 2 * EDGE

    def channels(group):
        lanes = pl.ds(pl.multiple_of(group * LANES, LANES), LANES)
        scale = scale_ref[:, lanes]
        shift = shift_ref[:, lanes]

        def unit(u):
            place_ = ctx * UNITS + u
            cut_before = jnp.bool_(False)
            cut_after = jnp.bool_(False)
            for end in ends:
                cut_before = cut_before | (place_ == end)
                cut_after = cut_after | (place_ + 1 == end)
            frames = padded[pl.ds(pl.multiple_of(u * SEG_UNIT, SEG_UNIT), window), lanes]
            frames = frames.astype(jnp.float32)
            side = jnp.zeros((EDGE, LANES), jnp.float32)
            frames = jnp.concatenate(
                [
                    jnp.where(cut_before, side, frames[:EDGE]),
                    frames[EDGE : EDGE + SEG_UNIT],
                    jnp.where(cut_after, side, frames[EDGE + SEG_UNIT :]),
                ],
                axis=0,
            )
            total = jnp.zeros((SEG_UNIT, LANES), jnp.float32)
            for turn in range(8):
                turned = pltpu.roll(frames, window - turn, 0) if turn else frames
                for tap in range((turn - 1) % 8, KERNEL, 8):
                    at = tap + 1 - turn
                    total = total + taps_ref[pl.ds(tap, 1), lanes] * turned[at : at + SEG_UNIT]
            value = scale * total + shift
            value = value / (1.0 + jnp.exp(-value))
            conv_out[pl.ds(pl.multiple_of(u * SEG_UNIT, SEG_UNIT), SEG_UNIT), lanes] = value.astype(
                jnp.bfloat16
            )

        repeat(0, UNITS, unit)

    repeat(0, CHANNELS // LANES, channels)


def convolve_column(lengths, rows, halo, taps, scale, shift):
    vmem = pl.BlockSpec(memory_space=pltpu.VMEM)
    return pl.pallas_call(
        convolve_kernel,
        out_shape=jax.ShapeDtypeStruct((COLUMN, CHANNELS), rows.dtype),
        in_specs=[pl.BlockSpec(memory_space=pltpu.SMEM)] + [vmem] * 5,
        out_specs=vmem,
        scratch_shapes=[pltpu.VMEM((COLUMN + 2 * EDGE, CHANNELS), rows.dtype)],
        compiler_params=pltpu.CompilerParams(vmem_limit_bytes=32 * 2**20),
        name="convolve",
    )(lengths, rows, halo, taps, scale, shift)


STEP = 2


def attend_kernel(len_ref, q_ref, k_ref, v_ref, out_ref):
    block = pl.program_id(0)
    ends = [len_ref[0, 0]]
    for i in range(1, 4):
        ends.append(ends[-1] + len_ref[0, i])
    first = block * UNITS
    last = first + UNITS - 1
    low = jnp.int32(0)
    high = jnp.int32(FRAMES // SEG_UNIT)
    for end in ends:
        low = jnp.where(end <= first, jnp.maximum(low, end), low)
        high = jnp.where(end > last, jnp.minimum(high, end), high)
    per_key = KBLOCK // SEG_UNIT
    low_block = low // per_key
    steps = ((high + per_key - 1) // per_key - low_block + STEP - 1) // STEP
    low_block = jnp.minimum(low_block, FRAMES // KBLOCK - STEP * steps)

    def segment(unit):
        seg = jnp.zeros(unit.shape, jnp.int32)
        for end in ends[:3]:
            seg = seg + (unit >= end).astype(jnp.int32)
        return seg

    queries = q_ref[...] * 0.125
    lane = lax.broadcasted_iota(jnp.int32, (QBLOCK, LANES), 1)
    zero = jnp.zeros_like(queries)
    both = jnp.concatenate(
        [jnp.where(lane < HEAD_DIM, queries, zero), jnp.where(lane < HEAD_DIM, zero, queries)], axis=0
    )
    row = lax.broadcasted_iota(jnp.int32, (2 * QBLOCK, 1), 0)
    row_seg = segment(first + lax.rem(row, QBLOCK) // SEG_UNIT)
    def step(index, carry):
        top, total, mixed = carry
        at = low_block + index * STEP
        part = pl.ds(pl.multiple_of(at * KBLOCK, KBLOCK), STEP * KBLOCK)
        keys = k_ref[part, :]
        values = v_ref[part, :]
        scores = lax.dot_general(
            both, keys, (((1,), (1,)), ((), ())), preferred_element_type=jnp.float32
        )
        col = lax.broadcasted_iota(jnp.int32, (1, STEP * KBLOCK), 1)
        col_seg = segment(at * per_key + col // SEG_UNIT)
        scores = jnp.where(row_seg == col_seg, scores, -2e30)
        new_top = jnp.maximum(top, jnp.max(scores, axis=1, keepdims=True))
        weights = jnp.exp(scores - new_top)
        scale = jnp.exp(top - new_top)
        total = total * scale + jnp.sum(weights, axis=1, keepdims=True)
        mixed = mixed * scale + jnp.dot(
            weights.astype(jnp.bfloat16), values, preferred_element_type=jnp.float32
        )
        return new_top, total, mixed

    top, total, mixed = lax.fori_loop(
        0,
        steps,
        step,
        (
            jnp.full((2 * QBLOCK, 1), -1e30, jnp.float32),
            jnp.zeros((2 * QBLOCK, 1), jnp.float32),
            jnp.zeros((2 * QBLOCK, LANES), jnp.float32),
        ),
    )
    mixed = mixed / total
    out_ref[0] = jnp.where(lane < HEAD_DIM, mixed[:QBLOCK], mixed[QBLOCK:]).astype(jnp.bfloat16)


def attend(lengths, q, k, v):
    blocks = FRAMES // QBLOCK
    return pl.pallas_call(
        attend_kernel,
        grid_spec=pltpu.PrefetchScalarGridSpec(
            num_scalar_prefetch=1,
            grid=(blocks,),
            in_specs=[
                pl.BlockSpec((QBLOCK, LANES), lambda i, lens: (i, 0)),
                pl.BlockSpec((FRAMES, LANES), lambda i, lens: (0, 0)),
                pl.BlockSpec((FRAMES, LANES), lambda i, lens: (0, 0)),
            ],
            out_specs=pl.BlockSpec((1, QBLOCK, LANES), lambda i, lens: (i, 0, 0)),
        ),
        out_shape=jax.ShapeDtypeStruct((blocks, QBLOCK, LANES), jnp.bfloat16),
        compiler_params=pltpu.CompilerParams(vmem_limit_bytes=48 * 2**20),
        cost_estimate=pl.CostEstimate(
            flops=8 * FRAMES * FRAMES * LANES, bytes_accessed=2**21, transcendentals=2 * FRAMES * FRAMES
        ),
        name="attend",
    )(lengths, q, k, v)


def segment_of(positions, seg_ends):
    unit_index = positions // SEG_UNIT
    return jnp.sum((seg_ends[None, :] <= unit_index[:, None]).astype(jnp.int32), axis=1)


def convolve(signal, halo, lengths, conv_taps, norm_scale, norm_shift):
    seg_ends = jnp.cumsum(lengths[0])
    column = lax.axis_index("ctx")
    half_width = (KERNEL - 1) // 2
    query_seg = segment_of(column * COLUMN + jnp.arange(COLUMN, dtype=jnp.int32), seg_ends)
    before = jnp.where(column > 0, halo[0], 0)
    after = jnp.where(column < N_CTX - 1, halo[1], 0)
    padded = jnp.concatenate([before[1:], signal, after[:half_width]], axis=0).astype(jnp.float32)
    padded_seg = segment_of(
        column * COLUMN - half_width + jnp.arange(COLUMN + 2 * half_width, dtype=jnp.int32), seg_ends
    )
    conv_sum = jnp.zeros(signal.shape, jnp.float32)
    for tap in range(KERNEL):
        same_seg = (padded_seg[tap : tap + COLUMN] == query_seg)[:, None]
        conv_sum = conv_sum + jnp.where(same_seg, conv_taps[tap] * padded[tap : tap + COLUMN], 0.0)
    return jax.nn.silu(norm_scale * conv_sum + norm_shift).astype(jnp.bfloat16)


def share_of(dp, ctx):
    return (dp // 8) * 8 + lax.rem(dp + ctx, 8)


def entry(count, device):
    barrier = pltpu.get_barrier_semaphore()

    def one(k, carry):
        pl.semaphore_signal(barrier, inc=1, device_id=device(k), device_id_type=MESH)
        return carry

    lax.fori_loop(0, count, one, 0)
    pl.semaphore_wait(barrier, count)


def all_arrived(ref, sem):
    pltpu.make_async_copy(ref, ref, sem).wait()


def general_spread_kernel(x_ref, out_ref, send_sem, recv_sem):
    dp, ctx = lax.axis_index("dp"), lax.axis_index("ctx")
    entry(N_DP - 1, lambda k: (lax.rem(dp + 1 + k, N_DP), ctx))

    def copy(k):
        peer = lax.rem(dp + k, N_DP)
        return pltpu.make_async_remote_copy(
            src_ref=x_ref.at[share_of(peer, ctx)],
            dst_ref=out_ref.at[dp],
            send_sem=send_sem,
            recv_sem=recv_sem,
            device_id=(peer, ctx),
            device_id_type=MESH,
        )

    own = pltpu.make_async_copy(x_ref.at[share_of(dp, ctx)], out_ref.at[dp], recv_sem)

    def start(k, carry):
        copy(k).start()
        return carry

    def sent(k, carry):
        copy(k).wait_send()
        return carry

    lax.fori_loop(1, N_DP, start, 0)
    own.start()
    lax.fori_loop(1, N_DP, sent, 0)
    all_arrived(out_ref, recv_sem)


def general_spread(x):
    return pl.pallas_call(
        general_spread_kernel,
        out_shape=jax.ShapeDtypeStruct(x.shape, x.dtype),
        in_specs=[pl.BlockSpec(memory_space=pl.ANY)],
        out_specs=pl.BlockSpec(memory_space=pl.ANY),
        scratch_shapes=[pltpu.SemaphoreType.DMA, pltpu.SemaphoreType.DMA],
        compiler_params=pltpu.CompilerParams(collective_id=3, has_side_effects=True),
        name="general_spread",
    )(x)


def general_heads_kernel(x_ref, out_ref, send_sem, recv_sem):
    dp, ctx = lax.axis_index("dp"), lax.axis_index("ctx")
    share = share_of(dp, ctx)
    group, column = share // 8, lax.rem(share, 8)

    def sender(k):
        other = k // 8
        return (lax.rem(k, 8) * 8 + lax.rem(ctx - other + 8, 8), other)

    barrier = pltpu.get_barrier_semaphore()

    def greet(k, carry):
        peer = sender(k)

        @pl.when(jnp.logical_or(peer[0] != dp, peer[1] != ctx))
        def _():
            pl.semaphore_signal(barrier, inc=1, device_id=peer, device_id_type=MESH)

        return carry

    lax.fori_loop(0, N_DP, greet, 0)
    is_own = column == ctx

    @pl.when(is_own)
    def _():
        pl.semaphore_wait(barrier, N_DP - 1)

    @pl.when(jnp.logical_not(is_own))
    def _():
        pl.semaphore_wait(barrier, N_DP)

    def copy(k):
        peer = lax.rem(dp + k, N_DP)
        return pltpu.make_async_remote_copy(
            src_ref=x_ref.at[peer],
            dst_ref=out_ref.at[pl.ds(ctx * TILES_DEV, TILES_DEV), group],
            send_sem=send_sem,
            recv_sem=recv_sem,
            device_id=(peer, column),
            device_id_type=MESH,
        )

    def start(k, carry):
        copy(k).start()
        return carry

    def sent(k, carry):
        copy(k).wait_send()
        return carry

    lax.fori_loop(1, N_DP, start, 0)

    @pl.when(is_own)
    def _():
        pltpu.make_async_copy(
            x_ref.at[dp], out_ref.at[pl.ds(ctx * TILES_DEV, TILES_DEV), group], recv_sem
        ).start()

    @pl.when(jnp.logical_not(is_own))
    def _():
        copy(0).start()
        copy(0).wait_send()

    lax.fori_loop(1, N_DP, sent, 0)
    all_arrived(out_ref, recv_sem)


def general_heads(x):
    return pl.pallas_call(
        general_heads_kernel,
        out_shape=jax.ShapeDtypeStruct((N_CTX * TILES_DEV, TILE // ROWS, 3, ROWS, LANES), x.dtype),
        in_specs=[pl.BlockSpec(memory_space=pl.ANY)],
        out_specs=pl.BlockSpec(memory_space=pl.ANY),
        scratch_shapes=[pltpu.SemaphoreType.DMA, pltpu.SemaphoreType.DMA],
        compiler_params=pltpu.CompilerParams(collective_id=4, has_side_effects=True),
        name="general_heads",
    )(x)


def general_deliver_kernel(x_ref, mix_ref, out_ref, heads_ref, send_sem, recv_sem, mix_send, mix_recv):
    dp, ctx = lax.axis_index("dp"), lax.axis_index("ctx")
    share = share_of(dp, ctx)
    barrier = pltpu.get_barrier_semaphore()

    def greet_dp(k, carry):
        pl.semaphore_signal(
            barrier, inc=1, device_id=(lax.rem(dp + k, N_DP), ctx), device_id_type=MESH
        )
        return carry

    def greet_ctx(k, carry):
        pl.semaphore_signal(
            barrier, inc=1, device_id=(dp, lax.rem(ctx + k, N_CTX)), device_id_type=MESH
        )
        return carry

    lax.fori_loop(1, N_DP, greet_dp, 0)
    lax.fori_loop(1, N_CTX, greet_ctx, 0)
    pl.semaphore_wait(barrier, N_DP - 1 + N_CTX - 1)

    def mix_copy(k):
        peer = lax.rem(ctx + k, N_CTX)
        return pltpu.make_async_remote_copy(
            src_ref=mix_ref.at[peer],
            dst_ref=heads_ref.at[:, pl.ds(pl.multiple_of(ctx * LANES, LANES), LANES)],
            send_sem=mix_send,
            recv_sem=mix_recv,
            device_id=(dp, peer),
            device_id_type=MESH,
        )

    def copy(k):
        peer = lax.rem(dp + k, N_DP)
        return pltpu.make_async_remote_copy(
            src_ref=x_ref.at[peer],
            dst_ref=out_ref.at[share],
            send_sem=send_sem,
            recv_sem=recv_sem,
            device_id=(peer, ctx),
            device_id_type=MESH,
        )

    def start(k, carry):
        copy(k).start()
        return carry

    def sent(k, carry):
        copy(k).wait_send()
        return carry

    def mix_start(k, carry):
        mix_copy(k).start()
        return carry

    def mix_sent(k, carry):
        mix_copy(k).wait_send()
        return carry

    lax.fori_loop(1, N_DP, start, 0)
    lax.fori_loop(1, N_CTX, mix_start, 0)
    pltpu.make_async_copy(x_ref.at[dp], out_ref.at[share], recv_sem).start()
    pltpu.make_async_copy(
        mix_ref.at[ctx],
        heads_ref.at[:, pl.ds(pl.multiple_of(ctx * LANES, LANES), LANES)],
        mix_recv,
    ).start()
    lax.fori_loop(1, N_DP, sent, 0)
    lax.fori_loop(1, N_CTX, mix_sent, 0)
    all_arrived(out_ref, recv_sem)
    all_arrived(heads_ref, mix_recv)


def general_deliver(x, mix):
    rows = FRAMES // N_CTX
    return pl.pallas_call(
        general_deliver_kernel,
        out_shape=(
            jax.ShapeDtypeStruct(x.shape, x.dtype),
            jax.ShapeDtypeStruct((rows, N_CTX * LANES), x.dtype),
        ),
        in_specs=[pl.BlockSpec(memory_space=pl.ANY)] * 2,
        out_specs=[pl.BlockSpec(memory_space=pl.ANY)] * 2,
        scratch_shapes=[pltpu.SemaphoreType.DMA] * 4,
        compiler_params=pltpu.CompilerParams(collective_id=5, has_side_effects=True),
        name="general_deliver",
    )(x, mix)


def general_path(
    query_loader,
    key_loader,
    value_loader,
    conv_loader,
    slot_tile,
    lengths,
    conv_taps,
    norm_scale,
    norm_shift,
):
    qkv = jnp.stack([query_loader[0], key_loader[0], value_loader[0]])
    qkv = qkv.reshape(3, TILES_DEV, TILE // ROWS, ROWS, N_CTX, LANES)
    qkv = jnp.transpose(qkv, (2, 4, 1, 0, 3, 5)).reshape(N_DP, TILES_DEV * QKV, LANES)
    conv = conv_loader[0].reshape(TILES_DEV, N_DP, CONV_ROWS, LANES)
    conv = jnp.transpose(conv, (1, 0, 2, 3)).reshape(N_DP, TILES_DEV * CONV_ROWS, LANES)
    got = general_spread(jnp.concatenate([qkv, conv], axis=1))
    order = slot_tile[0]
    got_qkv = got[:, : TILES_DEV * QKV].reshape(N_DP * TILES_DEV, 3, ROWS, LANES)
    send_qkv = got_qkv[order].reshape(N_DP, TILES_DEV, 3, ROWS, LANES)
    got_conv = got[:, TILES_DEV * QKV :].reshape(N_DP * TILES_DEV, CONV_ROWS, LANES)
    send_conv = got_conv[order].reshape(N_DP, TILES_DEV * CONV_ROWS, LANES)
    heads = general_heads(send_qkv)
    flat = (FRAMES, LANES)
    mix = attend(lengths, *(heads[:, :, i].reshape(flat) for i in range(3)))
    signal, attention_out = general_deliver(send_conv, mix)
    signal = signal.reshape(N_DP, TILES_DEV, TILE // N_DP, CONV_ROWS // 2 * LANES)
    signal = jnp.transpose(signal, (1, 0, 2, 3)).reshape(TILES_DEV * TILE, CONV_ROWS // 2 * LANES)
    ends = N_CTX - 1
    halo = jnp.stack(
        [
            lax.ppermute(signal[COLUMN - 16 :], "ctx", [(i, i + 1) for i in range(ends)]),
            lax.ppermute(signal[:16], "ctx", [(i + 1, i) for i in range(ends)]),
        ]
    )
    conv_out = convolve(signal, halo, lengths, conv_taps, norm_scale, norm_shift)
    return attention_out[None], conv_out[None]


def on_device(*inputs):
    query, key, value, conv, slot_tile, lengths, conv_taps, norm_scale, norm_shift = inputs
    places = jnp.transpose(slot_tile[0].reshape(N_Z, 8))
    places = jnp.pad(places, ((0, 0), (0, LANES - N_Z)), constant_values=1 << 16)
    shape = (TILES_DEV, PLANE_DP, SEG_UNIT, HEADS * HEAD_DIM)
    held_q, lists = first(query.reshape(shape), places)
    table = route(lists.reshape(HELD, LANES))
    attention_out, rows, halo = exchange(
        table,
        lengths,
        held_q,
        key.reshape(shape),
        value.reshape(shape),
        conv.reshape(TILES_DEV, N_CTX, 16, CHANNELS),
    )
    conv_out = convolve_column(
        lengths,
        rows.reshape(COLUMN, CHANNELS),
        halo,
        conv_taps,
        norm_scale.reshape(1, CHANNELS),
        norm_shift.reshape(1, CHANNELS),
    )
    return lax.cond(
        table[AT_BAD] == 0,
        lambda: (attention_out[None], conv_out[None]),
        lambda: general_path(*inputs),
    )


def solution(mesh):
    return jax.shard_map(
        on_device,
        mesh=mesh,
        in_specs=(
            P("dp", "ctx", None),
            P("dp", "ctx", None),
            P("dp", "ctx", None),
            P("dp", "ctx", None),
            P("ctx", None),
            P("dp", None),
            P(),
            P(),
            P(),
        ),
        out_specs=(P("dp", "ctx", None), P("dp", "ctx", None)),
        check_vma=False,
    )
```

```python
import jax
import jax.numpy as jnp
from jax import lax
from jax.experimental import pallas as pl
from jax.experimental.pallas import tpu as pltpu
from jax.sharding import PartitionSpec as P

MESH = pl.DeviceIdType.MESH
HEADS = 16
HEAD_DIM = 64
CHANNELS = 1536
KERNEL = 31
TILE = 128
TILES_DEV = 2
SEG_UNIT = 32
FRAMES = 2048
COLUMN = 256
LANES = 128
N_DP = 64
N_CTX = 8
ROWS = 16
QKV = 3 * ROWS
CONV_ROWS = 24
KEYS = 512
QBLOCK = 256
KBLOCK = 256
UNITS = QBLOCK // SEG_UNIT

N_Z = 16
PLANE_DP = 4
PLANE = PLANE_DP * N_CTX
HELD = PLANE * TILES_DEV
SHIFTS = N_Z - 1
NEAR, NEAR_SLOTS, FAR_SLOTS = 6, 5, 4
RELAYS, RELAY_SLOTS = 10, 2
MAIN = NEAR * NEAR_SLOTS + (SHIFTS - NEAR) * FAR_SLOTS
EXTRA = RELAYS * RELAY_SLOTS
TABLE = 256
AT_MAIN, AT_EXTRA, AT_FINAL, AT_BAD = 0, 72, 96, 160
RANKS = 16
PAIRS = N_Z * N_Z
LIST = 2304
FIELDS = 0x55555555


def shift_of(j):
    half = j // 2
    return jnp.where(j % 2 == 0, half + 1, N_Z - 1 - half)


def order_of(shift):
    return jnp.where(shift <= N_Z // 2, 2 * (shift - 1), 2 * (N_Z - shift) - 1)


def main_slots(shift):
    return jnp.where(order_of(shift) < NEAR, NEAR_SLOTS, FAR_SLOTS)


def main_offset(shift):
    j = order_of(shift)
    return jnp.where(j < NEAR, NEAR_SLOTS * j, NEAR * NEAR_SLOTS + FAR_SLOTS * (j - NEAR))


def relay_offset(shift):
    return RELAY_SLOTS * order_of(shift)


def place():
    dp, ctx = lax.axis_index("dp"), lax.axis_index("ctx")
    return dp // PLANE_DP, dp % PLANE_DP, ctx


def plane_peer(z, row, ctx, k):
    index = (row * N_CTX + ctx + k) % PLANE
    return index // N_CTX, index % N_CTX, (z * PLANE_DP + index // N_CTX, index % N_CTX)


def z_peer(z, row, ctx, j):
    return ((z + shift_of(j)) % N_Z * PLANE_DP + row, ctx)


def repeat(first, last, body):
    def one(k, carry):
        body(k)
        return carry

    lax.fori_loop(first, last, one, 0)


def remote(src, dst, send, recv, device):
    return pltpu.make_async_remote_copy(
        src_ref=src, dst_ref=dst, send_sem=send, recv_sem=recv, device_id=device, device_id_type=MESH
    )


def await_all(ref, sem):
    pltpu.make_async_copy(ref, ref, sem).wait()


def signal(device):
    pl.semaphore_signal(pltpu.get_barrier_semaphore(), inc=1, device_id=device, device_id_type=MESH)


class Spread:
    def __init__(self, piece, held, send, recv):
        z, row, ctx = place()
        mine = pl.ds((ctx * PLANE_DP + row) * TILES_DEV, TILES_DEV)

        def copy(k):
            to_row, to_ctx, device = plane_peer(z, row, ctx, k)
            return remote(piece(to_row, to_ctx), held.at[mine], send, recv, device)

        self.copy, self.held, self.recv = copy, held, recv
        self.own = pltpu.make_async_copy(piece(row, ctx), held.at[mine], recv)

    def start(self):
        repeat(1, PLANE, lambda k: self.copy(k).start())
        self.own.start()

    def arrived(self):
        await_all(self.held, self.recv)

    def sent(self):
        repeat(1, PLANE, lambda k: self.copy(k).wait_send())


class Along:
    def __init__(self, groups, staged, got, send, recv):
        z, row, ctx = place()
        self.staged, self.got, self.send, self.recv = staged, got, send, recv

        def copy(j, offset, slots):
            part = pl.ds(offset, slots)
            return remote(staged.at[part], got.at[part], send, recv, z_peer(z, row, ctx, j))

        self.copy, self.groups = copy, groups

    def start(self):
        for first, last, base, slots in self.groups:
            repeat(
                first,
                last,
                lambda j: self.copy(j, base + (j - first) * slots, slots).start(),
            )

    def arrived(self):
        await_all(self.got, self.recv)

    def sent(self):
        await_all(self.staged, self.send)


MAIN_GROUPS = ((0, NEAR, 0, NEAR_SLOTS), (NEAR, SHIFTS, NEAR * NEAR_SLOTS, FAR_SLOTS))
EXTRA_GROUPS = ((0, RELAYS, 0, RELAY_SLOTS),)


def stage_main(table, held, staged):
    def one(i):
        staged[i] = held[table[AT_MAIN + i]]

    repeat(0, MAIN, one)


def stage_extra(table, held, got, staged):
    def one(i):
        code = table[AT_EXTRA + i]
        staged[i] = jnp.where(
            code < HELD, held[jnp.minimum(code, HELD - 1)], got[jnp.clip(code - HELD, 0, MAIN - 1)]
        )

    repeat(0, EXTRA, one)


def stage_final(table, held, got, more, staged):
    def one(i):
        code = table[AT_FINAL + i]
        first = held[jnp.minimum(code, HELD - 1)]
        second = got[jnp.clip(code - HELD, 0, MAIN - 1)]
        third = more[jnp.clip(code - HELD - MAIN, 0, EXTRA - 1)]
        staged[i] = jnp.where(code < HELD, first, jnp.where(code < HELD + MAIN, second, third))

    repeat(0, HELD, one)


def head_piece(ref):
    return lambda row, ctx: ref.at[:, row, :, pl.ds(pl.multiple_of(ctx * LANES, LANES), LANES)]


WIDE = CHANNELS // PLANE_DP


def first_kernel(q_ref, list_ref, held_ref, lists_ref, send, recv, list_send, list_recv):
    z, row, ctx = place()
    repeat(1, PLANE, lambda k: signal(plane_peer(z, row, ctx, k)[2]))
    pl.semaphore_wait(pltpu.get_barrier_semaphore(), PLANE - 1)

    def tell(k):
        device = (z * PLANE_DP + row, (ctx + k) % N_CTX)
        return remote(list_ref, lists_ref.at[ctx], list_send, list_recv, device)

    repeat(1, N_CTX, lambda k: tell(k).start())
    pltpu.make_async_copy(list_ref, lists_ref.at[ctx], list_recv).start()
    spread = Spread(head_piece(q_ref), held_ref, send, recv)
    spread.start()
    repeat(1, N_CTX, lambda k: tell(k).wait_send())
    await_all(lists_ref, list_recv)
    spread.arrived()
    spread.sent()


def first(q, own_list):
    return pl.pallas_call(
        first_kernel,
        out_shape=(
            jax.ShapeDtypeStruct((HELD, SEG_UNIT, LANES), q.dtype),
            jax.ShapeDtypeStruct((N_CTX,) + own_list.shape, own_list.dtype),
        ),
        in_specs=[pl.BlockSpec(memory_space=pl.ANY)] * 2,
        out_specs=[pl.BlockSpec(memory_space=pl.ANY)] * 2,
        scratch_shapes=[pltpu.SemaphoreType.DMA] * 4,
        compiler_params=pltpu.CompilerParams(collective_id=0, has_side_effects=True),
        name="spread_queries",
    )(q, own_list)


def filled(fields):
    return (fields | (fields >> 1)) & FIELDS


def field_index(bit):
    def step(mask, worth):
        return jnp.where((bit & mask) != 0, worth, 0)

    high = jnp.where(bit >= (1 << 16), 8, 0)
    return high + step(0x7F00FF00, 4) + step(0x70F0F0F0, 2) + step(0x4CCCCCCC & FIELDS, 1)


def field_value(fields, bit):
    return jnp.where((fields & bit) != 0, 1, 0) + jnp.where((fields & (bit << 1)) != 0, 2, 0)


STEPS = 12
MOST_LANE, OVER_LANE = N_Z, N_Z + 1
A_ROW, B_ROW, MISSED_ROW = 0, 1, 2


def route_kernel(
    lists_ref,
    table,
    count_v,
    extra_v,
    excess_v,
    tile_v,
    slot_v,
    code_v,
    state_v,
    relay_v,
    count,
    excess,
    tile,
    slot,
    code,
    state,
    relay,
    direct,
    free_s,
    relay_free,
    sems,
):
    me = lax.axis_index("dp") // PLANE_DP
    tiles = lists_ref[...]
    source = tiles >> 3
    rows = lax.broadcasted_iota(jnp.int32, (HELD, LANES), 0)
    lanes = lax.broadcasted_iota(jnp.int32, (HELD, LANES), 1)
    local = (rows & ~7) + (tiles & 7)
    position = ((rows & 7) >> 1) * 16 + (rows >> 3) * 2 + (rows & 1)

    def total(values):
        return jnp.sum(values, axis=0, keepdims=True, dtype=jnp.int32)

    for i in range(N_Z):
        count_v[pl.ds(i, 1), :] = total(jnp.where(source == ((lanes - i) & 15), 1, 0))
    held = count_v[...]
    shift = lax.broadcasted_iota(jnp.int32, held.shape, 0)
    lane = lax.broadcasted_iota(jnp.int32, held.shape, 1)
    stays = shift == 0
    most = jnp.where(stays, RANKS, main_slots(shift))
    left = jnp.where(stays, 3, jnp.clip(most - held, 0, 3)) << (2 * (lane & 15))
    extra = jnp.maximum(jnp.minimum(held, RANKS) - most, 0)
    extra_v[...] = extra
    largest = jnp.minimum(jnp.max(extra, axis=1, keepdims=True), STEPS)
    over = jnp.max(jnp.where((held > RANKS) | (extra > STEPS), 1, 0), axis=1, keepdims=True)
    kept = jnp.minimum(extra, STEPS)
    excess_v[...] = jnp.where(lane == MOST_LANE, largest, jnp.where(lane == OVER_LANE, over, kept))
    ahead = pltpu.make_async_copy(excess_v, excess, sems.at[0])
    ahead.start()
    count_copy = pltpu.make_async_copy(count_v, count, sems.at[1])
    count_copy.start()

    def add_rank(i, rank):
        other = lists_ref[pl.ds(i, 1), :] >> 3
        return rank + jnp.where((other == source) & (rows > i), 1, 0)

    rank = lax.fori_loop(0, HELD, add_rank, jnp.zeros((HELD, LANES), jnp.int32), unroll=8)
    here = lanes == me
    column_source = jnp.sum(jnp.where(here, source, 0), axis=1, keepdims=True)
    column_rank = jnp.sum(jnp.where(here, rank, 0), axis=1, keepdims=True)
    mine = jnp.where(source == me, rank, -1)
    taken = jnp.where(column_source == lanes, column_rank, -1)
    for i in range(RANKS):
        tile_v[pl.ds(i, 1), :] = total(jnp.where(mine == i, local, 0))
        slot_v[pl.ds(i, 1), :] = total(jnp.where(taken == i, position, 0))
    copies = [
        pltpu.make_async_copy(tile_v, tile, sems.at[2]),
        pltpu.make_async_copy(slot_v, slot, sems.at[3]),
    ]
    for copy in copies:
        copy.start()

    y = lax.broadcasted_iota(jnp.int32, (1, LANES), 1) & 15
    free = jnp.zeros((1, LANES), jnp.int32)
    relays = jnp.zeros((1, LANES), jnp.int32)
    for i in range(N_Z):
        row = left[i : i + 1, :]
        free = free | (pltpu.roll(row, LANES - i, 1) if i else row)
        away = (y - i) & 15
        opened = (away != 0) & (order_of(away) < RELAYS)
        relays = relays | (jnp.where(opened, RELAY_SLOTS, 0) << (2 * i))
    code_v[...] = jnp.zeros(code_v.shape, jnp.int32)
    ahead.wait()

    def displacement(i, carry):
        free, relays, missed = carry
        free = pltpu.roll(free, 1, 1)
        z = (y - i) & 15
        own = 1 << (2 * z)
        from_z = jnp.int32(-1) << (2 * z)
        wanted = extra_v[pl.ds(i, 1), :]

        def one(e, carry):
            free, relays, missed = carry
            active = wanted > e
            open_ = filled(free) & filled(relays)
            late = open_ & from_z
            chosen = jnp.where(late != 0, late, open_)
            bit = jnp.where(active, chosen & -chosen, 0)
            entry_ = (
                (1 << 12)
                | field_index(bit)
                | (field_value(free, bit) << 4)
                | (field_value(relays, bit) << 8)
            )
            code_v[pl.ds(i * STEPS + e, 1), :] = jnp.where(bit != 0, entry_, 0)
            missed = missed | jnp.where(active & (open_ == 0), 1 << i, 0)
            return free - jnp.where(bit == own, 0, bit), relays - bit, missed

        return lax.fori_loop(0, excess[i, MOST_LANE], one, (free, relays, missed))

    free, relays, missed = lax.fori_loop(
        1, N_Z, displacement, (free, relays, jnp.zeros((1, LANES), jnp.int32))
    )
    state_v[pl.ds(A_ROW, 1), :] = pltpu.roll(free, 1, 1)
    state_v[pl.ds(B_ROW, 1), :] = relays
    state_v[pl.ds(MISSED_ROW, 1), :] = missed
    last_copies = [
        pltpu.make_async_copy(code_v, code, sems.at[4]),
        pltpu.make_async_copy(state_v, state, sems.at[5]),
    ]
    for copy in last_copies:
        copy.start()
    codes = code_v[...]
    places = lax.broadcasted_iota(jnp.int32, codes.shape, 0)
    from_shift = (places * 171) >> 11
    places = (from_shift << 4) | (places - STEPS * from_shift)
    through_me = jnp.where((codes != 0) & ((codes & 15) == me), codes >> 8 & 3, 0)
    for i in range(RELAY_SLOTS):
        relay_v[pl.ds(i, 1), :] = total(
            jnp.where(through_me == i + 1, (1 << 12) | (places << 4) | ((codes >> 4) & 3), 0)
        )
    relay_copy = pltpu.make_async_copy(relay_v, relay, sems.at[6])
    relay_copy.start()
    for i in range(AT_BAD):
        table[i] = 0
    count_copy.wait()
    for copy in copies + last_copies:
        copy.wait()
    relay_copy.wait()

    def slots_of(shift):
        return jnp.where(shift == 0, RANKS, main_slots(shift))

    def open_row(shift):
        for y in range(N_Z):
            direct[shift * N_Z + y] = jnp.minimum(count[shift, y], slots_of(shift))

    repeat(0, N_Z, open_row)

    def open_plane(i):
        free_s[i] = state[A_ROW, i]
        relay_free[i] = state[B_ROW, i]

    for i in range(N_Z):
        open_plane(i)

    def own_main(z, m, field):
        return main_offset((m - z) & 15) + count[(m - z) & 15, m] + field - 1

    def leave(shift):
        y = (me + shift) & 15

        def one(e):
            entry_ = code[shift * STEPS + e, y]
            m = entry_ & 15

            @pl.when((entry_ != 0) & (m != me))
            def _():
                table[AT_MAIN + own_main(me, m, (entry_ >> 4) & 3)] = tile[main_slots(shift) + e, y]

        repeat(0, excess[shift, y], one)

    def reach(shift):
        z = (me - shift) & 15

        def one(e):
            entry_ = code[shift * STEPS + e, me]

            @pl.when(entry_ != 0)
            def _():
                extra_at = relay_offset((me - (entry_ & 15)) & 15) + ((entry_ >> 8) & 3) - 1
                table[AT_FINAL + slot[main_slots(shift) + e, z]] = HELD + MAIN + extra_at

        repeat(0, excess[shift, me], one)

    repeat(1, N_Z, leave)
    repeat(1, N_Z, reach)

    def pass_on(y):
        for i in range(RELAY_SLOTS):
            entry_ = relay[i, y]

            @pl.when(entry_ != 0)
            def _():
                shift = (entry_ >> 8) & 15
                z = (y - shift) & 15
                rank = main_slots(shift) + ((entry_ >> 4) & 15)
                table[AT_EXTRA + relay_offset((y - me) & 15) + i] = jnp.where(
                    z == me, tile[rank, y], HELD + own_main(z, me, entry_ & 3)
                )

    repeat(0, N_Z, pass_on)
    my_bit = jnp.int32(1) << (2 * me)

    def record(z, y, bit, rank, free, relay_, main):
        @pl.when((z == me) | (bit == my_bit) | (y == me))
        def _():
            m = field_index(bit)
            main_at = jnp.where(
                main >= 0, main_offset((m - z) & 15) + main, own_main(z, m, field_value(free, bit))
            )
            extra_at = relay_offset((y - m) & 15) + field_value(relay_, bit) - 1

            @pl.when((z == me) & (m != z))
            def _():
                table[AT_MAIN + main_at] = tile[rank, y]

            @pl.when(m == me)
            def _():
                table[AT_EXTRA + extra_at] = jnp.where(m == z, tile[rank, y], HELD + main_at)

            @pl.when(y == me)
            def _():
                table[AT_FINAL + slot[rank, z]] = HELD + MAIN + extra_at

    def mend(shift, e, y):
        z = (y - shift) & 15
        own = jnp.int32(1) << (2 * z)
        rank = main_slots(shift) + e
        mine_free, mine_relay = free_s[z], relay_free[y]
        open_ = filled(mine_free) & filled(mine_relay)

        def take(bit):
            free_s[z] = free_s[z] - jnp.where(bit == own, 0, bit)

        def simple():
            bit = open_ & -open_
            record(z, y, bit, rank, mine_free, mine_relay, jnp.int32(-1))
            take(bit)
            relay_free[y] = mine_relay - bit
            return jnp.int32(0)

        def swap():
            def look(m, done):
                bit = jnp.int32(1) << (2 * m)
                relay_m = relay_free[m]
                other = filled(mine_free) & filled(relay_m)
                at = ((m - z) & 15) * N_Z + m
                straight = direct[at]
                fits = (
                    (done == 0)
                    & (m != z)
                    & (m != y)
                    & ((filled(mine_relay) & bit) != 0)
                    & (straight > 0)
                    & (other != 0)
                )

                def do():
                    instead = other & -other
                    direct[at] = straight - 1
                    record(z, m, instead, straight - 1, mine_free, relay_m, jnp.int32(-1))
                    record(z, y, bit, rank, mine_free, mine_relay, straight - 1)
                    relay_free[m] = relay_m - instead
                    relay_free[y] = mine_relay - bit
                    take(instead)
                    return jnp.int32(1)

                return lax.cond(fits, do, lambda: done)

            return 1 - lax.fori_loop(0, N_Z, look, jnp.int32(0))

        return lax.cond(open_ != 0, simple, swap)

    def mend_target(y, bad):
        gaps = state[MISSED_ROW, y]

        def mend_pair(shift, bad):
            def mend_one(e, bad):
                return lax.cond(
                    code[shift * STEPS + e, y] == 0, lambda: bad | mend(shift, e, y), lambda: bad
                )

            count_ = jnp.where(((gaps >> shift) & 1) != 0, excess[shift, y], 0)
            return lax.fori_loop(0, count_, mend_one, bad)

        return lax.fori_loop(1, jnp.where(gaps != 0, N_Z, 1), mend_pair, bad)

    bad = lax.fori_loop(0, N_Z, mend_target, jnp.int32(0))
    for i in range(N_Z):
        bad = bad | excess[i, OVER_LANE]
    table[AT_BAD] = bad

    def straight(other):
        shift_out = (other - me) & 15
        shift_in = (me - other) & 15

        @pl.when(shift_out != 0)
        def _():
            first_out = AT_MAIN + main_offset(shift_out)
            first_in = HELD + main_offset(shift_in)

            def out(r):
                table[first_out + r] = tile[r, other]

            def arrive(r):
                table[AT_FINAL + slot[r, other]] = first_in + r

            repeat(0, direct[shift_out * N_Z + other], out)
            repeat(0, direct[shift_in * N_Z + me], arrive)

        @pl.when(shift_out == 0)
        def _():
            def keep(r):
                table[AT_FINAL + slot[r, me]] = tile[r, me]

            repeat(0, direct[me], keep)

    repeat(0, N_Z, straight)


def route(lists):
    vmem, smem = pltpu.VMEM, pltpu.SMEM
    square = (N_Z, LANES)
    steps = (N_Z * STEPS, LANES)
    small = (8, LANES)
    kind = jnp.int32
    return pl.pallas_call(
        route_kernel,
        out_shape=jax.ShapeDtypeStruct((TABLE,), kind),
        in_specs=[pl.BlockSpec(memory_space=vmem)],
        out_specs=pl.BlockSpec(memory_space=smem),
        scratch_shapes=[vmem(square, kind)] * 5
        + [vmem(steps, kind), vmem(small, kind), vmem(small, kind)]
        + [smem(square, kind)] * 4
        + [smem(steps, kind), smem(small, kind), smem(small, kind)]
        + [smem((PAIRS,), kind), smem((N_Z,), kind), smem((N_Z,), kind), pltpu.SemaphoreType.DMA((7,))],
        name="route",
    )(lists)


PARTS = ((0, 128), (128, 128), (256, 128))
ARRAYS = 3 + len(PARTS)


def conv_lanes(row, part):
    first, width = PARTS[part]
    return pl.ds(pl.multiple_of(row * WIDE + first, LANES), width)


def conv_piece(ref, part):
    return lambda row, ctx: ref.at[:, ctx, :, conv_lanes(row, part)]


def exchange_kernel(
    table, lengths, held_q, k_ref, v_ref, conv_ref, heads_out, rows_out, halo_out, *scratch
):
    z, row, ctx = place()
    dp = z * PLANE_DP + row
    repeat(1, PLANE, lambda k: signal(plane_peer(z, row, ctx, k)[2]))
    repeat(0, SHIFTS, lambda j: signal(z_peer(z, row, ctx, j)))
    pl.semaphore_wait(pltpu.get_barrier_semaphore(), PLANE - 1 + SHIFTS)
    held = (held_q,) + scratch[: ARRAYS - 1]
    main_staged, main_got, extra_staged, extra_got, staged = (
        scratch[ARRAYS * (i + 1) - 1 : ARRAYS * (i + 2) - 1] for i in range(5)
    )
    group = scratch[6 * ARRAYS - 1 : 6 * ARRAYS + 2]
    mixture, sems, halo_sems, mix_sems = scratch[6 * ARRAYS + 2 :]
    pieces = [None, head_piece(k_ref), head_piece(v_ref)] + [conv_piece(conv_ref, i) for i in range(len(PARTS))]
    spread = [None] + [
        Spread(pieces[i], held[i], sems.at[0, i], sems.at[1, i]) for i in range(1, ARRAYS)
    ]
    main = [
        Along(MAIN_GROUPS, main_staged[i], main_got[i], sems.at[2, i], sems.at[3, i])
        for i in range(ARRAYS)
    ]
    extra = [
        Along(EXTRA_GROUPS, extra_staged[i], extra_got[i], sems.at[4, i], sems.at[5, i])
        for i in range(ARRAYS)
    ]

    def start_main(i):
        if i:
            spread[i].arrived()
        stage_main(table, held[i], main_staged[i])
        main[i].start()

    def start_extra(i):
        main[i].arrived()
        stage_extra(table, held[i], main_got[i], extra_staged[i])
        extra[i].start()

    def head_copy(i, k):
        to = (row + k) % PLANE_DP
        return remote(
            staged[i].at[pl.ds(to * 16, 16)],
            group[i].at[:, row],
            sems.at[6, i],
            sems.at[7, i],
            (z * PLANE_DP + to, ctx),
        )

    def part(i, to_row, to_ctx):
        return staged[i].at[pl.ds(to_row * 16 + to_ctx * TILES_DEV, TILES_DEV)]

    def rows_part(i):
        return rows_out.at[:, ctx, :, conv_lanes(row, i - 3)]

    def conv_copy(i, k):
        to_row, to_ctx, device = plane_peer(z, row, ctx, k)
        return remote(part(i, to_row, to_ctx), rows_part(i), sems.at[6, i], sems.at[7, 3], device)

    def halo(i, side, act):
        step, tile = (1, 1) if side == 0 else (-1, 0)

        def one(k):
            to_row = k // (N_CTX - 1)
            column = k % (N_CTX - 1) + (0 if side == 0 else 1)
            target = column + step
            src = staged[i].at[to_row * 16 + column * TILES_DEV + tile]
            dst = halo_out.at[side, :, conv_lanes(row, i - 3)]
            is_own = (to_row == row) & (target == ctx)

            @pl.when(is_own)
            def _():
                if act == "start":
                    pltpu.make_async_copy(src, dst, halo_sems.at[side]).start()

            @pl.when(jnp.logical_not(is_own))
            def _():
                far = remote(
                    src, dst, halo_sems.at[2], halo_sems.at[side], (z * PLANE_DP + to_row, target)
                )
                if act == "start":
                    far.start()
                else:
                    far.wait_send()

        @pl.when(ctx == (N_CTX - 1 if side == 0 else 0))
        def _():
            repeat(0, PLANE_DP * (N_CTX - 1), one)

    def start_final(i):
        extra[i].arrived()
        stage_final(table, held[i], main_got[i], extra_got[i], staged[i])
        if i >= 3:
            repeat(1, PLANE, lambda k: conv_copy(i, k).start())
            pltpu.make_async_copy(part(i, row, ctx), rows_part(i), sems.at[7, 3]).start()
            halo(i, 0, "start")
            halo(i, 1, "start")
        else:
            repeat(1, PLANE_DP, lambda k: head_copy(i, k).start())
            pltpu.make_async_copy(
                staged[i].at[pl.ds(row * 16, 16)], group[i].at[:, row], sems.at[7, i]
            ).start()

    ends = [lengths[0, 0]]
    for i in range(1, 3):
        ends.append(ends[-1] + lengths[0, i])

    def segment(unit):
        seg = jnp.zeros(unit.shape, jnp.int32)
        for end in ends:
            seg = seg + (unit >= end).astype(jnp.int32)
        return seg

    mixed_at = heads_out.at[:, pl.ds(pl.multiple_of(ctx * LANES, LANES), LANES)]

    def mix_copy(block):
        return remote(mixture.at[block], mixed_at, mix_sems.at[0], mix_sems.at[1], (dp, block))

    lane = lax.broadcasted_iota(jnp.int32, (QBLOCK, LANES), 1)
    query = lax.broadcasted_iota(jnp.int32, (2 * QBLOCK, 1), 0) % QBLOCK
    key = lax.broadcasted_iota(jnp.int32, (1, KEYS), 1)

    def attend_block(block, first_key, steps):
        queries = group[0][pl.ds(block * TILES_DEV, TILES_DEV)].reshape(QBLOCK, LANES) * 0.125
        zero = jnp.zeros_like(queries)
        both = jnp.concatenate(
            [jnp.where(lane < HEAD_DIM, queries, zero), jnp.where(lane < HEAD_DIM, zero, queries)],
            axis=0,
        )
        query_seg = segment(block * UNITS + query // SEG_UNIT)

        def step(index, carry):
            top, total, mixed = carry
            at = first_key + index * KEYS
            tiles = pl.ds(first_key // TILE + index * (KEYS // TILE), KEYS // TILE)
            keys = group[1][tiles].reshape(KEYS, LANES)
            values = group[2][tiles].reshape(KEYS, LANES)
            scores = lax.dot_general(
                both, keys, (((1,), (1,)), ((), ())), preferred_element_type=jnp.float32
            )
            key_seg = segment((at + key) // SEG_UNIT)
            scores = jnp.where(query_seg == key_seg, scores, -2e30)
            new_top = jnp.maximum(top, jnp.max(scores, axis=1, keepdims=True))
            weights = jnp.exp(scores - new_top)
            scale = jnp.exp(top - new_top)
            total = total * scale + jnp.sum(weights, axis=1, keepdims=True)
            mixed = mixed * scale + jnp.dot(
                weights.astype(jnp.bfloat16), values, preferred_element_type=jnp.float32
            )
            return new_top, total, mixed

        _, total, mixed = lax.fori_loop(
            0,
            steps,
            step,
            (
                jnp.full((2 * QBLOCK, 1), -1e30, jnp.float32),
                jnp.zeros((2 * QBLOCK, 1), jnp.float32),
                jnp.zeros((2 * QBLOCK, LANES), jnp.float32),
            ),
        )
        mixed = mixed / total
        mixture[block] = jnp.where(lane < HEAD_DIM, mixed[:QBLOCK], mixed[QBLOCK:]).astype(jnp.bfloat16)

        @pl.when(block == ctx)
        def _():
            pltpu.make_async_copy(mixture.at[block], mixed_at, mix_sems.at[1]).start()

        @pl.when(block != ctx)
        def _():
            mix_copy(block).start()

    def attend_blocks(first, last, first_key, steps):
        repeat(first, last, lambda block: attend_block(block, first_key, steps))

    spread[1].start()
    start_main(0)
    spread[2].start()
    start_main(1)
    spread[3].start()
    spread[4].start()
    spread[5].start()
    start_extra(0)
    start_main(2)
    start_extra(1)
    start_final(0)
    start_main(3)
    start_extra(2)
    start_main(4)
    start_main(5)
    start_final(1)
    start_final(2)
    for i in range(3):
        await_all(group[i], sems.at[7, i])
    attend_blocks(0, 2, 0, 3)
    start_extra(3)
    attend_blocks(2, 4, 0, 4)
    start_final(3)
    start_extra(4)
    attend_blocks(4, 6, 0, 4)
    start_final(4)
    start_extra(5)
    attend_blocks(6, 8, FRAMES - 3 * KEYS, 3)
    start_final(5)
    for i in range(ARRAYS):
        if i:
            spread[i].sent()
        main[i].sent()
        extra[i].sent()
        if i < 3:
            repeat(1, PLANE_DP, lambda k: head_copy(i, k).wait_send())
        else:
            repeat(1, PLANE, lambda k: conv_copy(i, k).wait_send())
            halo(i, 0, "sent")
            halo(i, 1, "sent")

    def mix_sent(block):
        @pl.when(block != ctx)
        def _():
            mix_copy(block).wait_send()

    repeat(0, N_CTX, mix_sent)
    await_all(heads_out, mix_sems.at[1])
    await_all(rows_out, sems.at[7, 3])

    @pl.when(ctx > 0)
    def _():
        await_all(halo_out.at[0], halo_sems.at[0])

    @pl.when(ctx < N_CTX - 1)
    def _():
        await_all(halo_out.at[1], halo_sems.at[1])


def exchange(table, lengths, held_q, k, v, conv):
    unit = (SEG_UNIT, LANES)
    kind = held_q.dtype

    def buffers(count):
        return [pltpu.VMEM((count,) + (unit if i < 3 else (16, PARTS[i - 3][1])), kind) for i in range(ARRAYS)]

    smem = pl.BlockSpec(memory_space=pltpu.SMEM)
    return pl.pallas_call(
        exchange_kernel,
        out_shape=(
            jax.ShapeDtypeStruct((COLUMN, N_CTX * LANES), kind),
            jax.ShapeDtypeStruct((TILES_DEV, N_CTX, 16, CHANNELS), kind),
            jax.ShapeDtypeStruct((2, 16, CHANNELS), kind),
        ),
        in_specs=[smem, smem, pl.BlockSpec(memory_space=pltpu.VMEM)]
        + [pl.BlockSpec(memory_space=pl.ANY)] * 3,
        out_specs=[pl.BlockSpec(memory_space=pl.ANY)] * 3,
        scratch_shapes=buffers(HELD)[1:]
        + buffers(MAIN)
        + buffers(MAIN)
        + buffers(EXTRA)
        + buffers(EXTRA)
        + buffers(HELD)
        + [pltpu.VMEM((N_CTX * TILES_DEV, PLANE_DP) + unit, kind)] * 3
        + [
            pltpu.VMEM((N_CTX, COLUMN, LANES), kind),
            pltpu.SemaphoreType.DMA((8, ARRAYS)),
            pltpu.SemaphoreType.DMA((3,)),
            pltpu.SemaphoreType.DMA((2,)),
        ],
        compiler_params=pltpu.CompilerParams(
            collective_id=1, has_side_effects=True, vmem_limit_bytes=48 * 2**20
        ),
        name="exchange",
    )(table, lengths, held_q, k, v, conv)


EDGE = 16


def convolve_kernel(
    len_ref,
    rows_ref,
    halo_ref,
    taps_ref,
    scale_ref,
    shift_ref,
    conv_out,
    padded,
):
    ctx = lax.axis_index("ctx")
    padded[pl.ds(0, EDGE), :] = halo_ref[0]
    padded[pl.ds(EDGE, COLUMN), :] = rows_ref[...]
    padded[pl.ds(EDGE + COLUMN, EDGE), :] = halo_ref[1]
    ends = [jnp.int32(0), len_ref[0, 0]]
    for i in range(1, 4):
        ends.append(ends[-1] + len_ref[0, i])
    window = SEG_UNIT + 2 * EDGE

    def channels(group):
        lanes = pl.ds(pl.multiple_of(group * LANES, LANES), LANES)
        scale = scale_ref[:, lanes]
        shift = shift_ref[:, lanes]

        def unit(u):
            place_ = ctx * UNITS + u
            cut_before = jnp.bool_(False)
            cut_after = jnp.bool_(False)
            for end in ends:
                cut_before = cut_before | (place_ == end)
                cut_after = cut_after | (place_ + 1 == end)
            frames = padded[pl.ds(pl.multiple_of(u * SEG_UNIT, SEG_UNIT), window), lanes]
            frames = frames.astype(jnp.float32)
            side = jnp.zeros((EDGE, LANES), jnp.float32)
            frames = jnp.concatenate(
                [
                    jnp.where(cut_before, side, frames[:EDGE]),
                    frames[EDGE : EDGE + SEG_UNIT],
                    jnp.where(cut_after, side, frames[EDGE + SEG_UNIT :]),
                ],
                axis=0,
            )
            total = jnp.zeros((SEG_UNIT, LANES), jnp.float32)
            for turn in range(8):
                turned = pltpu.roll(frames, window - turn, 0) if turn else frames
                for tap in range((turn - 1) % 8, KERNEL, 8):
                    at = tap + 1 - turn
                    total = total + taps_ref[pl.ds(tap, 1), lanes] * turned[at : at + SEG_UNIT]
            value = scale * total + shift
            value = value / (1.0 + jnp.exp(-value))
            conv_out[pl.ds(pl.multiple_of(u * SEG_UNIT, SEG_UNIT), SEG_UNIT), lanes] = value.astype(
                jnp.bfloat16
            )

        repeat(0, UNITS, unit)

    repeat(0, CHANNELS // LANES, channels)


def convolve_column(lengths, rows, halo, taps, scale, shift):
    vmem = pl.BlockSpec(memory_space=pltpu.VMEM)
    return pl.pallas_call(
        convolve_kernel,
        out_shape=jax.ShapeDtypeStruct((COLUMN, CHANNELS), rows.dtype),
        in_specs=[pl.BlockSpec(memory_space=pltpu.SMEM)] + [vmem] * 5,
        out_specs=vmem,
        scratch_shapes=[pltpu.VMEM((COLUMN + 2 * EDGE, CHANNELS), rows.dtype)],
        compiler_params=pltpu.CompilerParams(vmem_limit_bytes=32 * 2**20),
        name="convolve",
    )(lengths, rows, halo, taps, scale, shift)


STEP = 2


def attend_kernel(len_ref, q_ref, k_ref, v_ref, out_ref):
    block = pl.program_id(0)
    ends = [len_ref[0, 0]]
    for i in range(1, 4):
        ends.append(ends[-1] + len_ref[0, i])
    first = block * UNITS
    last = first + UNITS - 1
    low = jnp.int32(0)
    high = jnp.int32(FRAMES // SEG_UNIT)
    for end in ends:
        low = jnp.where(end <= first, jnp.maximum(low, end), low)
        high = jnp.where(end > last, jnp.minimum(high, end), high)
    per_key = KBLOCK // SEG_UNIT
    low_block = low // per_key
    steps = ((high + per_key - 1) // per_key - low_block + STEP - 1) // STEP
    low_block = jnp.minimum(low_block, FRAMES // KBLOCK - STEP * steps)

    def segment(unit):
        seg = jnp.zeros(unit.shape, jnp.int32)
        for end in ends[:3]:
            seg = seg + (unit >= end).astype(jnp.int32)
        return seg

    queries = q_ref[...] * 0.125
    lane = lax.broadcasted_iota(jnp.int32, (QBLOCK, LANES), 1)
    zero = jnp.zeros_like(queries)
    both = jnp.concatenate(
        [jnp.where(lane < HEAD_DIM, queries, zero), jnp.where(lane < HEAD_DIM, zero, queries)], axis=0
    )
    row = lax.broadcasted_iota(jnp.int32, (2 * QBLOCK, 1), 0)
    row_seg = segment(first + lax.rem(row, QBLOCK) // SEG_UNIT)
    def step(index, carry):
        top, total, mixed = carry
        at = low_block + index * STEP
        part = pl.ds(pl.multiple_of(at * KBLOCK, KBLOCK), STEP * KBLOCK)
        keys = k_ref[part, :]
        values = v_ref[part, :]
        scores = lax.dot_general(
            both, keys, (((1,), (1,)), ((), ())), preferred_element_type=jnp.float32
        )
        col = lax.broadcasted_iota(jnp.int32, (1, STEP * KBLOCK), 1)
        col_seg = segment(at * per_key + col // SEG_UNIT)
        scores = jnp.where(row_seg == col_seg, scores, -2e30)
        new_top = jnp.maximum(top, jnp.max(scores, axis=1, keepdims=True))
        weights = jnp.exp(scores - new_top)
        scale = jnp.exp(top - new_top)
        total = total * scale + jnp.sum(weights, axis=1, keepdims=True)
        mixed = mixed * scale + jnp.dot(
            weights.astype(jnp.bfloat16), values, preferred_element_type=jnp.float32
        )
        return new_top, total, mixed

    top, total, mixed = lax.fori_loop(
        0,
        steps,
        step,
        (
            jnp.full((2 * QBLOCK, 1), -1e30, jnp.float32),
            jnp.zeros((2 * QBLOCK, 1), jnp.float32),
            jnp.zeros((2 * QBLOCK, LANES), jnp.float32),
        ),
    )
    mixed = mixed / total
    out_ref[0] = jnp.where(lane < HEAD_DIM, mixed[:QBLOCK], mixed[QBLOCK:]).astype(jnp.bfloat16)


def attend(lengths, q, k, v):
    blocks = FRAMES // QBLOCK
    return pl.pallas_call(
        attend_kernel,
        grid_spec=pltpu.PrefetchScalarGridSpec(
            num_scalar_prefetch=1,
            grid=(blocks,),
            in_specs=[
                pl.BlockSpec((QBLOCK, LANES), lambda i, lens: (i, 0)),
                pl.BlockSpec((FRAMES, LANES), lambda i, lens: (0, 0)),
                pl.BlockSpec((FRAMES, LANES), lambda i, lens: (0, 0)),
            ],
            out_specs=pl.BlockSpec((1, QBLOCK, LANES), lambda i, lens: (i, 0, 0)),
        ),
        out_shape=jax.ShapeDtypeStruct((blocks, QBLOCK, LANES), jnp.bfloat16),
        compiler_params=pltpu.CompilerParams(vmem_limit_bytes=48 * 2**20),
        cost_estimate=pl.CostEstimate(
            flops=8 * FRAMES * FRAMES * LANES, bytes_accessed=2**21, transcendentals=2 * FRAMES * FRAMES
        ),
        name="attend",
    )(lengths, q, k, v)


def segment_of(positions, seg_ends):
    unit_index = positions // SEG_UNIT
    return jnp.sum((seg_ends[None, :] <= unit_index[:, None]).astype(jnp.int32), axis=1)


def convolve(signal, halo, lengths, conv_taps, norm_scale, norm_shift):
    seg_ends = jnp.cumsum(lengths[0])
    column = lax.axis_index("ctx")
    half_width = (KERNEL - 1) // 2
    query_seg = segment_of(column * COLUMN + jnp.arange(COLUMN, dtype=jnp.int32), seg_ends)
    before = jnp.where(column > 0, halo[0], 0)
    after = jnp.where(column < N_CTX - 1, halo[1], 0)
    padded = jnp.concatenate([before[1:], signal, after[:half_width]], axis=0).astype(jnp.float32)
    padded_seg = segment_of(
        column * COLUMN - half_width + jnp.arange(COLUMN + 2 * half_width, dtype=jnp.int32), seg_ends
    )
    conv_sum = jnp.zeros(signal.shape, jnp.float32)
    for tap in range(KERNEL):
        same_seg = (padded_seg[tap : tap + COLUMN] == query_seg)[:, None]
        conv_sum = conv_sum + jnp.where(same_seg, conv_taps[tap] * padded[tap : tap + COLUMN], 0.0)
    return jax.nn.silu(norm_scale * conv_sum + norm_shift).astype(jnp.bfloat16)


def share_of(dp, ctx):
    return (dp // 8) * 8 + lax.rem(dp + ctx, 8)


def entry(count, device):
    barrier = pltpu.get_barrier_semaphore()

    def one(k, carry):
        pl.semaphore_signal(barrier, inc=1, device_id=device(k), device_id_type=MESH)
        return carry

    lax.fori_loop(0, count, one, 0)
    pl.semaphore_wait(barrier, count)


def all_arrived(ref, sem):
    pltpu.make_async_copy(ref, ref, sem).wait()


def general_spread_kernel(x_ref, out_ref, send_sem, recv_sem):
    dp, ctx = lax.axis_index("dp"), lax.axis_index("ctx")
    entry(N_DP - 1, lambda k: (lax.rem(dp + 1 + k, N_DP), ctx))

    def copy(k):
        peer = lax.rem(dp + k, N_DP)
        return pltpu.make_async_remote_copy(
            src_ref=x_ref.at[share_of(peer, ctx)],
            dst_ref=out_ref.at[dp],
            send_sem=send_sem,
            recv_sem=recv_sem,
            device_id=(peer, ctx),
            device_id_type=MESH,
        )

    own = pltpu.make_async_copy(x_ref.at[share_of(dp, ctx)], out_ref.at[dp], recv_sem)

    def start(k, carry):
        copy(k).start()
        return carry

    def sent(k, carry):
        copy(k).wait_send()
        return carry

    lax.fori_loop(1, N_DP, start, 0)
    own.start()
    lax.fori_loop(1, N_DP, sent, 0)
    all_arrived(out_ref, recv_sem)


def general_spread(x):
    return pl.pallas_call(
        general_spread_kernel,
        out_shape=jax.ShapeDtypeStruct(x.shape, x.dtype),
        in_specs=[pl.BlockSpec(memory_space=pl.ANY)],
        out_specs=pl.BlockSpec(memory_space=pl.ANY),
        scratch_shapes=[pltpu.SemaphoreType.DMA, pltpu.SemaphoreType.DMA],
        compiler_params=pltpu.CompilerParams(collective_id=3, has_side_effects=True),
        name="general_spread",
    )(x)


def general_heads_kernel(x_ref, out_ref, send_sem, recv_sem):
    dp, ctx = lax.axis_index("dp"), lax.axis_index("ctx")
    share = share_of(dp, ctx)
    group, column = share // 8, lax.rem(share, 8)

    def sender(k):
        other = k // 8
        return (lax.rem(k, 8) * 8 + lax.rem(ctx - other + 8, 8), other)

    barrier = pltpu.get_barrier_semaphore()

    def greet(k, carry):
        peer = sender(k)

        @pl.when(jnp.logical_or(peer[0] != dp, peer[1] != ctx))
        def _():
            pl.semaphore_signal(barrier, inc=1, device_id=peer, device_id_type=MESH)

        return carry

    lax.fori_loop(0, N_DP, greet, 0)
    is_own = column == ctx

    @pl.when(is_own)
    def _():
        pl.semaphore_wait(barrier, N_DP - 1)

    @pl.when(jnp.logical_not(is_own))
    def _():
        pl.semaphore_wait(barrier, N_DP)

    def copy(k):
        peer = lax.rem(dp + k, N_DP)
        return pltpu.make_async_remote_copy(
            src_ref=x_ref.at[peer],
            dst_ref=out_ref.at[pl.ds(ctx * TILES_DEV, TILES_DEV), group],
            send_sem=send_sem,
            recv_sem=recv_sem,
            device_id=(peer, column),
            device_id_type=MESH,
        )

    def start(k, carry):
        copy(k).start()
        return carry

    def sent(k, carry):
        copy(k).wait_send()
        return carry

    lax.fori_loop(1, N_DP, start, 0)

    @pl.when(is_own)
    def _():
        pltpu.make_async_copy(
            x_ref.at[dp], out_ref.at[pl.ds(ctx * TILES_DEV, TILES_DEV), group], recv_sem
        ).start()

    @pl.when(jnp.logical_not(is_own))
    def _():
        copy(0).start()
        copy(0).wait_send()

    lax.fori_loop(1, N_DP, sent, 0)
    all_arrived(out_ref, recv_sem)


def general_heads(x):
    return pl.pallas_call(
        general_heads_kernel,
        out_shape=jax.ShapeDtypeStruct((N_CTX * TILES_DEV, TILE // ROWS, 3, ROWS, LANES), x.dtype),
        in_specs=[pl.BlockSpec(memory_space=pl.ANY)],
        out_specs=pl.BlockSpec(memory_space=pl.ANY),
        scratch_shapes=[pltpu.SemaphoreType.DMA, pltpu.SemaphoreType.DMA],
        compiler_params=pltpu.CompilerParams(collective_id=4, has_side_effects=True),
        name="general_heads",
    )(x)


def general_deliver_kernel(x_ref, mix_ref, out_ref, heads_ref, send_sem, recv_sem, mix_send, mix_recv):
    dp, ctx = lax.axis_index("dp"), lax.axis_index("ctx")
    share = share_of(dp, ctx)
    barrier = pltpu.get_barrier_semaphore()

    def greet_dp(k, carry):
        pl.semaphore_signal(
            barrier, inc=1, device_id=(lax.rem(dp + k, N_DP), ctx), device_id_type=MESH
        )
        return carry

    def greet_ctx(k, carry):
        pl.semaphore_signal(
            barrier, inc=1, device_id=(dp, lax.rem(ctx + k, N_CTX)), device_id_type=MESH
        )
        return carry

    lax.fori_loop(1, N_DP, greet_dp, 0)
    lax.fori_loop(1, N_CTX, greet_ctx, 0)
    pl.semaphore_wait(barrier, N_DP - 1 + N_CTX - 1)

    def mix_copy(k):
        peer = lax.rem(ctx + k, N_CTX)
        return pltpu.make_async_remote_copy(
            src_ref=mix_ref.at[peer],
            dst_ref=heads_ref.at[:, pl.ds(pl.multiple_of(ctx * LANES, LANES), LANES)],
            send_sem=mix_send,
            recv_sem=mix_recv,
            device_id=(dp, peer),
            device_id_type=MESH,
        )

    def copy(k):
        peer = lax.rem(dp + k, N_DP)
        return pltpu.make_async_remote_copy(
            src_ref=x_ref.at[peer],
            dst_ref=out_ref.at[share],
            send_sem=send_sem,
            recv_sem=recv_sem,
            device_id=(peer, ctx),
            device_id_type=MESH,
        )

    def start(k, carry):
        copy(k).start()
        return carry

    def sent(k, carry):
        copy(k).wait_send()
        return carry

    def mix_start(k, carry):
        mix_copy(k).start()
        return carry

    def mix_sent(k, carry):
        mix_copy(k).wait_send()
        return carry

    lax.fori_loop(1, N_DP, start, 0)
    lax.fori_loop(1, N_CTX, mix_start, 0)
    pltpu.make_async_copy(x_ref.at[dp], out_ref.at[share], recv_sem).start()
    pltpu.make_async_copy(
        mix_ref.at[ctx],
        heads_ref.at[:, pl.ds(pl.multiple_of(ctx * LANES, LANES), LANES)],
        mix_recv,
    ).start()
    lax.fori_loop(1, N_DP, sent, 0)
    lax.fori_loop(1, N_CTX, mix_sent, 0)
    all_arrived(out_ref, recv_sem)
    all_arrived(heads_ref, mix_recv)


def general_deliver(x, mix):
    rows = FRAMES // N_CTX
    return pl.pallas_call(
        general_deliver_kernel,
        out_shape=(
            jax.ShapeDtypeStruct(x.shape, x.dtype),
            jax.ShapeDtypeStruct((rows, N_CTX * LANES), x.dtype),
        ),
        in_specs=[pl.BlockSpec(memory_space=pl.ANY)] * 2,
        out_specs=[pl.BlockSpec(memory_space=pl.ANY)] * 2,
        scratch_shapes=[pltpu.SemaphoreType.DMA] * 4,
        compiler_params=pltpu.CompilerParams(collective_id=5, has_side_effects=True),
        name="general_deliver",
    )(x, mix)


def general_path(
    query_loader,
    key_loader,
    value_loader,
    conv_loader,
    slot_tile,
    lengths,
    conv_taps,
    norm_scale,
    norm_shift,
):
    qkv = jnp.stack([query_loader[0], key_loader[0], value_loader[0]])
    qkv = qkv.reshape(3, TILES_DEV, TILE // ROWS, ROWS, N_CTX, LANES)
    qkv = jnp.transpose(qkv, (2, 4, 1, 0, 3, 5)).reshape(N_DP, TILES_DEV * QKV, LANES)
    conv = conv_loader[0].reshape(TILES_DEV, N_DP, CONV_ROWS, LANES)
    conv = jnp.transpose(conv, (1, 0, 2, 3)).reshape(N_DP, TILES_DEV * CONV_ROWS, LANES)
    got = general_spread(jnp.concatenate([qkv, conv], axis=1))
    order = slot_tile[0]
    got_qkv = got[:, : TILES_DEV * QKV].reshape(N_DP * TILES_DEV, 3, ROWS, LANES)
    send_qkv = got_qkv[order].reshape(N_DP, TILES_DEV, 3, ROWS, LANES)
    got_conv = got[:, TILES_DEV * QKV :].reshape(N_DP * TILES_DEV, CONV_ROWS, LANES)
    send_conv = got_conv[order].reshape(N_DP, TILES_DEV * CONV_ROWS, LANES)
    heads = general_heads(send_qkv)
    flat = (FRAMES, LANES)
    mix = attend(lengths, *(heads[:, :, i].reshape(flat) for i in range(3)))
    signal, attention_out = general_deliver(send_conv, mix)
    signal = signal.reshape(N_DP, TILES_DEV, TILE // N_DP, CONV_ROWS // 2 * LANES)
    signal = jnp.transpose(signal, (1, 0, 2, 3)).reshape(TILES_DEV * TILE, CONV_ROWS // 2 * LANES)
    ends = N_CTX - 1
    halo = jnp.stack(
        [
            lax.ppermute(signal[COLUMN - 16 :], "ctx", [(i, i + 1) for i in range(ends)]),
            lax.ppermute(signal[:16], "ctx", [(i + 1, i) for i in range(ends)]),
        ]
    )
    conv_out = convolve(signal, halo, lengths, conv_taps, norm_scale, norm_shift)
    return attention_out[None], conv_out[None]


def on_device(*inputs):
    query, key, value, conv, slot_tile, lengths, conv_taps, norm_scale, norm_shift = inputs
    places = jnp.transpose(slot_tile[0].reshape(N_Z, 8))
    places = jnp.tile(places, (1, LANES // N_Z))
    shape = (TILES_DEV, PLANE_DP, SEG_UNIT, HEADS * HEAD_DIM)
    held_q, lists = first(query.reshape(shape), places)
    table = route(lists.reshape(HELD, LANES))
    attention_out, rows, halo = exchange(
        table,
        lengths,
        held_q,
        key.reshape(shape),
        value.reshape(shape),
        conv.reshape(TILES_DEV, N_CTX, 16, CHANNELS),
    )
    conv_out = convolve_column(
        lengths,
        rows.reshape(COLUMN, CHANNELS),
        halo,
        conv_taps,
        norm_scale.reshape(1, CHANNELS),
        norm_shift.reshape(1, CHANNELS),
    )
    return lax.cond(
        table[AT_BAD] == 0,
        lambda: (attention_out[None], conv_out[None]),
        lambda: general_path(*inputs),
    )


def solution(mesh):
    return jax.shard_map(
        on_device,
        mesh=mesh,
        in_specs=(
            P("dp", "ctx", None),
            P("dp", "ctx", None),
            P("dp", "ctx", None),
            P("dp", "ctx", None),
            P("ctx", None),
            P("dp", None),
            P(),
            P(),
            P(),
        ),
        out_specs=(P("dp", "ctx", None), P("dp", "ctx", None)),
        check_vma=False,
    )
```
